32 devices in a mesh: dp: 2 (over y), seq: 16 (over z, x, core).
Axes of the slice: x: 2, y: 2, z: 4, core: 2. Of those that a mesh axis runs over, the one named last changes fastest.
Arguments:
- hidden_in: bfloat16 [8, 4096, 768], P('dp', 'seq'), may hold values from -6 to 6
- positions: int32 [8, 4096], P('dp', 'seq'), may hold values from 0 to 4095
- ln1_gain: float32 [768], replicated, may hold values from 0.5 to 1.5
- ln1_bias: float32 [768], replicated, may hold values from -4 to 4
- ln2_gain: float32 [768], replicated, may hold values from 0.5 to 1.5
- ln2_bias: float32 [768], replicated, may hold values from -4 to 4
- query_projection: bfloat16 [768, 768], replicated, may hold values from -0.3125 to 0.3125
- query_bias: float32 [768], replicated, may hold values from -4 to 4
- shared_key_weight: bfloat16 [768, 64], replicated, may hold values from -0.21875 to 0.21875
- shared_key_bias: float32 [64], replicated, may hold values from -4 to 4
- shared_value_weight: bfloat16 [768, 64], replicated, may hold values from -0.21875 to 0.21875
- shared_value_bias: float32 [64], replicated, may hold values from -4 to 4
- output_weight: bfloat16 [768, 768], replicated, may hold values from -0.625 to 0.625
- output_bias: float32 [768], replicated, may hold values from -4 to 4
- up_weight: bfloat16 [768, 3072], replicated, may hold values from -0.21875 to 0.21875
- up_bias: float32 [3072], replicated, may hold values from -4 to 4
- down_weight: bfloat16 [3072, 768], replicated, may hold values from -0.109375 to 0.109375
- down_bias: float32 [768], replicated, may hold values from -4 to 4
- cotangent: bfloat16 [8, 4096, 768], P('dp', 'seq'), may hold values from -6 to 6
Outputs:
- layer_out: float32 [8, 4096, 768], P('dp', 'seq')
- input_grad: float32 [8, 4096, 768], P('dp', 'seq')
- grad_ln1_gain: float32 [768], replicated
- grad_ln1_bias: float32 [768], replicated
- grad_ln2_gain: float32 [768], replicated
- grad_ln2_bias: float32 [768], replicated
- grad_w_query: float32 [768, 768], replicated
- grad_b_query: float32 [768], replicated
- grad_w_key: float32 [768, 64], replicated
- grad_b_key: float32 [64], replicated
- grad_w_value: float32 [768, 64], replicated
- grad_b_value: float32 [64], replicated
- grad_w_out: float32 [768, 768], replicated
- grad_b_out: float32 [768], replicated
- up_weight_gradient: float32 [768, 3072], replicated
- grad_b_up: float32 [3072], replicated
- grad_w_down: float32 [3072, 768], replicated
- grad_b_down: float32 [768], replicated
The draws below stay inside these ranges and needn't reach their ends.
All inputs are finite; a program needn't handle non-finite values.
Results may differ from the reference program's by a relative error of at most 0.033.
Values may be sent and summed in bfloat16 or wider, within the bound.
A program may use at most 192 MiB of HBM per device.

```python
import math
import jax
import jax.numpy as jnp
from jax import lax

D = 768
HEADS = 12
HEAD_DIM = 64
ROT_DIMS = 16
FF = 3072
SEQ_LEN = 4096
SEQS_ALL = 8


def place_ends(entries, rng, least, high):
    longest = entries.shape.index(max(entries.shape))
    spots = []
    for shift in (0, 1):
        where = [jax.random.randint(jax.random.fold_in(rng, axis), (), 0, length) for axis, length in enumerate(entries.shape)]
        where[longest] = (where[longest] + shift) % entries.shape[longest]
        spots.append(tuple(where))
    return entries.at[spots[0]].set(least).at[spots[1]].set(high)


def steps_of(own_key, dims, cuts, least, top_value):
    def one(dim, shards_of):
        steps = jax.random.uniform(jax.random.fold_in(jax.random.fold_in(own_key, 6), dim), (shards_of,), jnp.float32, least / len(cuts), top_value / len(cuts))
        return jnp.repeat(jnp.exp(steps), dims[dim] // shards_of).reshape((-1,) + (1,) * (len(dims) - dim - 1))

    loudness = one(*cuts[0])
    for cut in cuts[1:]:
        loudness = loudness * one(*cut)
    return loudness


def normal_values(own_key, extent, scale, reach, shards=(), kind=jnp.bfloat16):
    factor_of = steps_of(own_key, extent, shards, -0.22, 0.18) if shards else 1.0
    values = jax.random.normal(own_key, extent, jnp.float32) * scale * factor_of
    return jnp.minimum(jnp.maximum(values, -reach), reach).astype(kind)


def setup_inputs(seed: int = 0) -> dict:
    keys = jax.random.split(jax.random.key(seed), 20)
    return {
        "hidden_in": normal_values(keys[0], (SEQS_ALL, SEQ_LEN, D), 1.0, 6.0, ((0, 2), (1, 16))),
        "positions": place_ends(jax.random.randint(keys[1], (SEQS_ALL, SEQ_LEN), 0, SEQ_LEN), jax.random.fold_in(keys[1], 1), 0, SEQ_LEN - 1).astype(jnp.int32),
        "ln1_gain": jnp.clip(1.0 + 0.1 * jax.random.normal(keys[2], (D,), jnp.float32), 0.5, 1.5),
        "ln1_bias": normal_values(keys[3], (D,), 0.3, 4.0, (), jnp.float32),
        "ln2_gain": jnp.clip(1.0 + 0.1 * jax.random.normal(keys[4], (D,), jnp.float32), 0.5, 1.5),
        "ln2_bias": normal_values(keys[5], (D,), 0.3, 4.0, (), jnp.float32),
        "query_projection": normal_values(keys[6], (D, D), (D // 2) ** -0.5, 0.3125),
        "query_bias": normal_values(keys[7], (D,), 0.3, 4.0, (), jnp.float32),
        "shared_key_weight": normal_values(keys[8], (D, HEAD_DIM), D ** -0.5, 0.21875),
        "shared_key_bias": normal_values(keys[9], (HEAD_DIM,), 0.3, 4.0, (), jnp.float32),
        "shared_value_weight": normal_values(keys[10], (D, HEAD_DIM), D ** -0.5, 0.21875),
        "shared_value_bias": normal_values(keys[11], (HEAD_DIM,), 0.3, 4.0, (), jnp.float32),
        "output_weight": normal_values(keys[12], (D, D), (D // 8) ** -0.5, 0.625),
        "output_bias": normal_values(keys[13], (D,), 0.3, 4.0, (), jnp.float32),
        "up_weight": normal_values(keys[14], (D, FF), D ** -0.5, 0.21875),
        "up_bias": normal_values(keys[15], (FF,), 0.3, 4.0, (), jnp.float32),
        "down_weight": normal_values(keys[16], (FF, D), FF ** -0.5, 0.109375),
        "down_bias": normal_values(keys[17], (D,), 0.3, 4.0, (), jnp.float32),
        "cotangent": normal_values(keys[18], (SEQS_ALL, SEQ_LEN, D), 1.0, 6.0, ((0, 2), (1, 16))),
    }


FULL_PRECISION = lax.Precision.HIGHEST

@jax.custom_vjp
def low(v):
    return lax.optimization_barrier(v.astype(jnp.bfloat16)).astype(jnp.float32)

@jax.custom_vjp
def low_back(v):
    return v

def low_keep(v):
    return (low(v), None)

def low_pass(kept, grad):
    return (grad,)

def back_keep(v):
    return (v, None)

def back_low(kept, grad):
    return (low(grad),)
low.defvjp(low_keep, low_pass)
low_back.defvjp(back_keep, back_low)

def forward_and_backward(values):
    return low(low_back(values))

def layer_norm(values, gain, bias):
    center = values - lax.optimization_barrier(jnp.mean(values, axis=-1, keepdims=True))
    spread = lax.optimization_barrier(jnp.mean(center * center, axis=-1, keepdims=True))
    return center * lax.rsqrt(spread + 1e-05) * gain + bias

def gelu_exact(values):
    return 0.5 * values * (1.0 + jax.scipy.special.erf(values * (1.0 / math.sqrt(2.0))))

def rotary(values, cosine, sine_part):
    halfway = cosine.shape[-1]
    first_half = values[..., :halfway]
    second_half = values[..., halfway:2 * halfway]
    return jnp.concatenate([first_half * cosine - second_half * sine_part, second_half * cosine + first_half * sine_part, values[..., 2 * halfway:]], axis=-1)

def angles_of(positions):
    halfway = ROT_DIMS // 2
    frequency = jnp.exp(jnp.arange(halfway).astype(jnp.float32) * (-2.0 * math.log(10000.0) / ROT_DIMS))
    angle_all = positions.astype(jnp.float32)[..., None] * frequency
    return (jnp.cos(angle_all), jnp.sin(angle_all))

def attend_sequence(operands):
    queries, key_all, value_every_token = operands
    block_len = min(512, SEQ_LEN)
    block_count = SEQ_LEN // block_len
    score_scale = HEAD_DIM ** (-0.5)
    columns = jnp.arange(SEQ_LEN, dtype=jnp.int32)

    def one_block(pieces):
        query_rows, row_start = pieces
        scores = low_back(jnp.einsum('hqd,kd->hqk', query_rows, key_all, precision=FULL_PRECISION) * score_scale)
        query_pos = row_start + jnp.arange(block_len, dtype=jnp.int32)
        scores = jnp.where(columns[None, None, :] <= query_pos[None, :, None], scores, -1e+30)
        row_top = lax.optimization_barrier(jnp.max(scores, axis=-1, keepdims=True))
        log_total = row_top + jnp.log(lax.optimization_barrier(jnp.sum(jnp.exp(scores - row_top), axis=-1, keepdims=True)))
        return jnp.einsum('hqk,kd->hqd', low(jnp.exp(scores - log_total)), value_every_token, precision=FULL_PRECISION)
    split_rows = queries.reshape(HEADS, block_count, block_len, HEAD_DIM).transpose(1, 0, 2, 3)
    starts = jnp.arange(block_count, dtype=jnp.int32) * block_len
    blocks = lax.map(jax.checkpoint(one_block), (split_rows, starts))
    return blocks.transpose(1, 0, 2, 3).reshape(HEADS, SEQ_LEN, HEAD_DIM)

def forward(hidden, cosine, sine_all, ln1_gain, ln1_bias, ln2_gain, ln2_bias, query_projection, query_bias, shared_key_weight, shared_key_bias, shared_value_weight, shared_value_bias, output_weight, output_bias, up_weight, up_bias, down_weight, down_bias):
    seq_count = hidden.shape[0]
    attention_normed_input = low(layer_norm(hidden, ln1_gain, ln1_bias))
    feedforward_normed_input = low(layer_norm(hidden, ln2_gain, ln2_bias))
    query_before_rotary = low_back(jnp.einsum('mhu,up->mhp', attention_normed_input, query_projection, precision=FULL_PRECISION) + query_bias)
    query_all = query_before_rotary.reshape(seq_count, SEQ_LEN, HEADS, HEAD_DIM)
    query_all = forward_and_backward(rotary(query_all, cosine[:, :, None, :], sine_all[:, :, None, :]))
    key_before_rotary = low_back(jnp.einsum('mhu,up->mhp', attention_normed_input, shared_key_weight, precision=FULL_PRECISION) + shared_key_bias)
    key_all = forward_and_backward(rotary(key_before_rotary, cosine, sine_all))
    value_every_token = forward_and_backward(jnp.einsum('mhu,up->mhp', attention_normed_input, shared_value_weight, precision=FULL_PRECISION) + shared_value_bias)
    attended_values = lax.map(attend_sequence, (query_all.transpose(0, 2, 1, 3), key_all, value_every_token))
    attended_values = forward_and_backward(attended_values.transpose(0, 2, 1, 3).reshape(seq_count, SEQ_LEN, D))
    attention_output = jnp.einsum('mhu,up->mhp', attended_values, output_weight, precision=FULL_PRECISION) + output_bias
    up_before_activation = low_back(jnp.einsum('aet,tn->aen', feedforward_normed_input, up_weight, precision=FULL_PRECISION) + up_bias)
    activated_hidden = low(gelu_exact(up_before_activation))
    feedforward_output = jnp.einsum('tpx,xe->tpe', activated_hidden, down_weight, precision=FULL_PRECISION) + down_bias
    return hidden + attention_output + feedforward_output

def reference(hidden_in, positions, ln1_gain, ln1_bias, ln2_gain, ln2_bias, query_projection, query_bias, shared_key_weight, shared_key_bias, shared_value_weight, shared_value_bias, output_weight, output_bias, up_weight, up_bias, down_weight, down_bias, cotangent):
    cosine, sine_all = angles_of(positions)

    def apply_layer(hidden, *parameters):
        return forward(hidden, cosine, sine_all, *parameters)
    parameters = [parameter.astype(jnp.float32) for parameter in (ln1_gain, ln1_bias, ln2_gain, ln2_bias, query_projection, query_bias, shared_key_weight, shared_key_bias, shared_value_weight, shared_value_bias, output_weight, output_bias, up_weight, up_bias, down_weight, down_bias)]
    output, pull_back = jax.vjp(apply_layer, hidden_in.astype(jnp.float32), *parameters)
    gradients = pull_back(cotangent.astype(jnp.float32))
    return (output, gradients[0], gradients[1], gradients[2], gradients[3], gradients[4], gradients[5], gradients[6], gradients[7], gradients[8], gradients[9], gradients[10], gradients[11], gradients[12], gradients[13], gradients[14], gradients[15], gradients[16])
```

```python
import math

import jax
import jax.numpy as jnp
from jax import lax
from jax.experimental import pallas as pl
from jax.experimental.pallas import tpu as pltpu
from jax.sharding import PartitionSpec as P

D = 768
HEADS = 12
HEAD_DIM = 64
ROT_DIMS = 16
BF = jnp.bfloat16
F32 = jnp.float32
LOG2E = math.log2(math.e)
TILE = 256


def layer_norm(values, gain, bias):
    center = values - jnp.mean(values, axis=-1, keepdims=True)
    spread = jnp.mean(center * center, axis=-1, keepdims=True)
    return center * lax.rsqrt(spread + 1e-05) * gain + bias


def gelu_exact(values):
    return 0.5 * values * (1.0 + jax.scipy.special.erf(values * (1.0 / math.sqrt(2.0))))


def rotary_rows(values, cosine, sine):
    half = cosine.shape[-2]
    first, second = values[..., :half, :], values[..., half : 2 * half, :]
    return jnp.concatenate(
        [first * cosine - second * sine, second * cosine + first * sine, values[..., 2 * half :, :]],
        axis=-2,
    )


def angles_of(positions):
    half = ROT_DIMS // 2
    frequency = jnp.exp(
        jnp.arange(half).astype(F32) * (-2.0 * math.log(10000.0) / ROT_DIMS)
    )
    angle = positions.astype(F32)[:, None, :] * frequency[None, :, None]
    return jnp.cos(angle), jnp.sin(angle)


def dot(a, b, ca, cb):
    return lax.dot_general(a, b, (((ca,), (cb,)), ((), ())), preferred_element_type=F32)


def attention_kernel(
    q_ref, g_ref, k_ref, v_ref, kt_ref, vt_ref, o_ref, dq_ref, dk_ref, dv_ref, s_ref, p_ref
):
    tiles, width, rows = q_ref.shape
    heads = width // HEAD_DIM
    lanes = heads * rows
    block = rows
    dk_ref[...] = jnp.zeros_like(dk_ref)
    dv_ref[...] = jnp.zeros_like(dv_ref)
    keep = lax.broadcasted_iota(jnp.int32, (block, rows), 0) <= lax.broadcasted_iota(
        jnp.int32, (block, rows), 1
    )
    keep = jnp.concatenate([keep] * heads, axis=1)

    def side(ref, j):
        return jnp.concatenate(
            [ref[j, HEAD_DIM * h : HEAD_DIM * (h + 1), :] for h in range(heads)], axis=1
        )

    def at(kb):
        return pl.ds(pl.multiple_of(kb * block, block), block)

    def tile(step, carry):
        j = tiles - 1 - step
        q = side(q_ref, j)
        g = side(g_ref, j)

        def scores(kb, top):
            s = dot(k_ref[at(kb), :], q, 1, 0)
            s_ref[at(kb), :] = s
            return jnp.maximum(top, jnp.max(s, axis=0, keepdims=True))

        s = jnp.where(keep, dot(k_ref[at(j), :], q, 1, 0), -1e30)
        s_ref[at(j), :] = s
        top = lax.fori_loop(0, j, scores, jnp.max(s, axis=0, keepdims=True))

        def forward(kb, state):
            total, out = state
            p = jnp.exp2(s_ref[at(kb), :] - top)
            low = p.astype(BF)
            p_ref[at(kb), :] = low
            return (
                total + jnp.sum(p, axis=0, keepdims=True),
                out + dot(vt_ref[:, at(kb)], low, 1, 0),
            )

        total, out = lax.fori_loop(
            0,
            j + 1,
            forward,
            (jnp.zeros((1, lanes), F32), jnp.zeros((HEAD_DIM, lanes), F32)),
        )
        inverse = 1.0 / total
        out = out * inverse
        scaled = (g.astype(F32) * inverse).astype(BF)
        delta = jnp.sum(scaled.astype(F32) * out, axis=0, keepdims=True)
        high = delta.astype(BF)
        rest = delta - high.astype(F32)
        middle = rest.astype(BF)
        last = (rest - middle.astype(F32)).astype(BF)
        stacked = jnp.concatenate(
            [scaled, high, middle, last, jnp.zeros((13, lanes), BF)], axis=0
        )
        for h in range(heads):
            o_ref[j, HEAD_DIM * h : HEAD_DIM * (h + 1), :] = out[
                :, h * rows : (h + 1) * rows
            ].astype(BF)

        def backward(kb, dq):
            p = p_ref[at(kb), :]
            dp = dot(v_ref[at(kb), :], stacked, 1, 0)
            ds = (p.astype(F32) * dp).astype(BF)
            dv_ref[at(kb), :] += dot(p, scaled, 1, 1)
            dk_ref[at(kb), :] += dot(ds, q, 1, 1)
            return dq + dot(kt_ref[:, at(kb)], ds, 1, 0)

        dq = lax.fori_loop(0, j + 1, backward, jnp.zeros((HEAD_DIM, lanes), F32))
        dq = dq * (HEAD_DIM**-0.5)
        for h in range(heads):
            dq_ref[j, HEAD_DIM * h : HEAD_DIM * (h + 1), :] = dq[
                :, h * rows : (h + 1) * rows
            ].astype(BF)
        return carry

    lax.fori_loop(0, tiles, tile, 0)


def attention(q, g, key, value):
    tiles, width, rows = q.shape
    length = tiles * rows
    lanes = width // HEAD_DIM * rows
    ones = jnp.concatenate([jnp.full((length, 3), -1, BF), jnp.zeros((length, 13), BF)], axis=1)
    whole = pl.BlockSpec(memory_space=pltpu.VMEM)
    flops = 12 * length * length // 2 * width
    return pl.pallas_call(
        attention_kernel,
        out_shape=[jax.ShapeDtypeStruct(q.shape, BF)] * 2
        + [jax.ShapeDtypeStruct((length, HEAD_DIM), F32)] * 2,
        in_specs=[whole] * 6,
        out_specs=[whole] * 4,
        scratch_shapes=[pltpu.VMEM((length, lanes), F32), pltpu.VMEM((length, lanes), BF)],
        compiler_params=pltpu.CompilerParams(vmem_limit_bytes=56 * 2**20),
        cost_estimate=pl.CostEstimate(
            flops=6 * flops, bytes_accessed=4 * q.size, transcendentals=length * length // 2 * 3
        ),
        name="attention",
    )(q, g, key, jnp.concatenate([value, ones], axis=1), key.T, value.T)


def local(
    hidden_in,
    positions,
    ln1_gain,
    ln1_bias,
    ln2_gain,
    ln2_bias,
    query_projection,
    query_bias,
    shared_key_weight,
    shared_key_bias,
    shared_value_weight,
    shared_value_bias,
    output_weight,
    output_bias,
    up_weight,
    up_bias,
    down_weight,
    down_bias,
    cotangent,
):
    seq_count, local_len = hidden_in.shape[0], hidden_in.shape[1]
    ring = lax.axis_size("seq")
    groups = ring // seq_count
    per_group = HEADS // groups
    width = per_group * HEAD_DIM
    length = ring * local_len
    hidden = hidden_in.astype(F32)
    cosine, sine = angles_of(positions)
    normed_a, pull_a = jax.vjp(layer_norm, hidden, ln1_gain, ln1_bias)
    normed_m, pull_m = jax.vjp(layer_norm, hidden, ln2_gain, ln2_bias)
    normed_a = normed_a.astype(BF)
    normed_m = normed_m.astype(BF)

    def swap(x):
        return lax.all_to_all(x, "seq", split_axis=0, concat_axis=0, tiled=True)

    kv_weight = jnp.concatenate([shared_key_weight, shared_value_weight], axis=1)
    kv_bias = jnp.concatenate([shared_key_bias, shared_value_bias])
    kv_pre = jnp.einsum("stc,cw->swt", normed_a, kv_weight, preferred_element_type=F32)
    kv_pre = kv_pre + kv_bias[:, None]
    kv_low = jnp.concatenate(
        [rotary_rows(kv_pre[:, :HEAD_DIM], cosine, sine), kv_pre[:, HEAD_DIM:]], axis=1
    ).astype(BF)
    kv_send = jnp.broadcast_to(
        kv_low[:, None], (seq_count, groups, 2 * HEAD_DIM, local_len)
    ).reshape(ring, 2 * HEAD_DIM, local_len)
    query_pre = jnp.einsum("stc,cw->swt", normed_a, query_projection, preferred_element_type=F32)
    query_pre = (query_pre + query_bias[:, None]).reshape(seq_count, HEADS, HEAD_DIM, local_len)
    query_low = (rotary_rows(query_pre, cosine[:, None], sine[:, None]) * (LOG2E / 8.0)).astype(BF)
    query_send = query_low.reshape(ring, width, local_len)
    grad_attended = jnp.einsum(
        "stc,wc->swt", cotangent, output_weight, preferred_element_type=F32
    ).astype(BF)
    grad_send = grad_attended.reshape(ring, width, local_len)
    query_send, kv_send, grad_send = lax.optimization_barrier((query_send, kv_send, grad_send))
    kv_here = swap(kv_send)
    query_here = swap(query_send)
    grad_here = swap(grad_send)

    up_pre = jnp.einsum("stc,cf->stf", normed_m, up_weight, preferred_element_type=F32) + up_bias
    activation, pull_gelu = jax.vjp(gelu_exact, up_pre)
    activation = activation.astype(BF)
    feedforward = jnp.einsum(
        "stf,fc->stc", activation, down_weight, preferred_element_type=F32
    )
    activation_gradient = jnp.einsum(
        "stc,fc->stf", cotangent, down_weight, preferred_element_type=F32
    )
    grad_up = pull_gelu(activation_gradient)[0].astype(BF)
    grad_w_down = jnp.einsum(
        "stf,stc->fc", activation, cotangent, preferred_element_type=F32
    ).astype(BF)
    grad_w_up = jnp.einsum("stc,stf->cf", normed_m, grad_up, preferred_element_type=F32).astype(BF)
    grad_normed_m = jnp.einsum("stf,cf->stc", grad_up, up_weight, preferred_element_type=F32)
    grad_w_up, grad_w_down = lax.psum((grad_w_up, grad_w_down), ("dp", "seq"))
    grad_b_up = jnp.sum(grad_up.astype(F32), axis=(0, 1))
    grad_b_down = jnp.sum(cotangent.astype(F32), axis=(0, 1))

    def to_tiles(x):
        tile_len = max(TILE, local_len)
        x = x.reshape(length // tile_len, tile_len // local_len, width, local_len)
        return x.transpose(0, 2, 1, 3).reshape(length // tile_len, width, tile_len)

    def from_tiles(x):
        tile_len = max(TILE, local_len)
        x = x.reshape(length // tile_len, width, tile_len // local_len, local_len)
        return x.transpose(0, 2, 1, 3).reshape(ring, width, local_len)

    kv_rows = kv_here.transpose(0, 2, 1).reshape(length, 2 * HEAD_DIM)
    out, dq, dk, dv = attention(
        to_tiles(query_here), to_tiles(grad_here), kv_rows[:, :HEAD_DIM], kv_rows[:, HEAD_DIM:]
    )
    attended = swap(from_tiles(out)).reshape(seq_count, D, local_len)
    query_back = swap(from_tiles(dq)).reshape(seq_count, HEADS, HEAD_DIM, local_len)
    kv_part = jnp.concatenate([dk * (1.0 / LOG2E), dv], axis=1).astype(BF)
    kv_back = swap(kv_part.reshape(ring, local_len, 2 * HEAD_DIM)).astype(F32)
    kv_grad = jnp.sum(kv_back.reshape(seq_count, groups, local_len, 2 * HEAD_DIM), axis=1)
    kv_grad = kv_grad.astype(BF).astype(F32).transpose(0, 2, 1)

    attention_out = jnp.einsum(
        "swt,wc->stc", attended, output_weight, preferred_element_type=F32
    )
    layer_out = hidden + attention_out + feedforward + (output_bias + down_bias)
    grad_w_out = jnp.einsum("swt,stc->wc", attended, cotangent, preferred_element_type=F32)

    kv_raw = jnp.concatenate(
        [rotary_rows(kv_grad[:, :HEAD_DIM], cosine, -sine), kv_grad[:, HEAD_DIM:]], axis=1
    ).astype(BF)
    query_raw = (
        rotary_rows(query_back.astype(F32), cosine[:, None], -sine[:, None])
        .astype(BF)
        .reshape(seq_count, D, local_len)
    )
    raw = jnp.concatenate([query_raw, kv_raw], axis=1)
    weight = jnp.concatenate([query_projection, kv_weight], axis=1)
    grad_w_qkv = jnp.einsum("stc,swt->cw", normed_a, raw, preferred_element_type=F32)
    grad_b_qkv = jnp.sum(raw.astype(F32), axis=(0, 2))
    grad_normed_a = jnp.einsum("swt,cw->stc", raw, weight, preferred_element_type=F32)
    grad_hidden_a, grad_ln1_gain, grad_ln1_bias = pull_a(grad_normed_a)
    grad_hidden_m, grad_ln2_gain, grad_ln2_bias = pull_m(grad_normed_m)
    input_grad = cotangent.astype(F32) + grad_hidden_a + grad_hidden_m

    vectors = jnp.concatenate(
        [
            grad_ln1_gain,
            grad_ln1_bias,
            grad_ln2_gain,
            grad_ln2_bias,
            grad_b_qkv,
            grad_b_up,
            grad_b_down,
        ]
    )
    rest = jnp.concatenate(
        [grad_w_qkv, grad_w_out],
        axis=1,
    ).astype(BF)
    rest, grad_w_up, grad_w_down = lax.optimization_barrier((rest, grad_w_up, grad_w_down))
    rest, vectors = lax.psum((rest, vectors), ("dp", "seq"))
    rest = rest.astype(F32)
    qkv = D + 2 * HEAD_DIM
    ff = up_weight.shape[1]
    b_qkv = vectors[4 * D : 4 * D + qkv]
    b_up = vectors[4 * D + qkv : 4 * D + qkv + ff]
    b_down = vectors[4 * D + qkv + ff :]
    return (
        layer_out,
        input_grad,
        vectors[:D],
        vectors[D : 2 * D],
        vectors[2 * D : 3 * D],
        vectors[3 * D : 4 * D],
        rest[:, :D],
        b_qkv[:D],
        rest[:, D : D + HEAD_DIM],
        b_qkv[D : D + HEAD_DIM],
        rest[:, D + HEAD_DIM : qkv],
        b_qkv[D + HEAD_DIM :],
        rest[:, qkv:],
        b_down,
        grad_w_up.astype(F32),
        b_up,
        grad_w_down.astype(F32),
        b_down,
    )


def solution(mesh):
    rows = P("dp", "seq", None)
    placed = (rows, P("dp", "seq")) + (P(),) * 16 + (rows,)
    return jax.shard_map(
        local,
        mesh=mesh,
        in_specs=placed,
        out_specs=(rows, rows) + (P(),) * 16,
        check_vma=False,
    )
```

```python
import functools
import math

import jax
import jax.numpy as jnp
from jax import lax
from jax.experimental import pallas as pl
from jax.experimental.pallas import tpu as pltpu
from jax.sharding import PartitionSpec as P

D = 768
HEADS = 12
HEAD_DIM = 64
ROT_DIMS = 16
BF = jnp.bfloat16
F32 = jnp.float32
LOG2E = math.log2(math.e)
TILE = 256


def layer_norm(values, gain, bias):
    center = values - jnp.mean(values, axis=-1, keepdims=True)
    spread = jnp.mean(center * center, axis=-1, keepdims=True)
    return center * lax.rsqrt(spread + 1e-05) * gain + bias


def gelu_exact(values):
    return 0.5 * values * (1.0 + jax.scipy.special.erf(values * (1.0 / math.sqrt(2.0))))


def rotary_rows(values, cosine, sine):
    half = cosine.shape[-2]
    first, second = values[..., :half, :], values[..., half : 2 * half, :]
    return jnp.concatenate(
        [first * cosine - second * sine, second * cosine + first * sine, values[..., 2 * half :, :]],
        axis=-2,
    )


def angles_of(positions):
    half = ROT_DIMS // 2
    frequency = jnp.exp(
        jnp.arange(half).astype(F32) * (-2.0 * math.log(10000.0) / ROT_DIMS)
    )
    angle = positions.astype(F32)[:, None, :] * frequency[None, :, None]
    return jnp.cos(angle), jnp.sin(angle)


def dot(a, b, ca, cb):
    return lax.dot_general(a, b, (((ca,), (cb,)), ((), ())), preferred_element_type=F32)


def attention_kernel(
    q_ref, g_ref, k_ref, v_ref, kt_ref, vt_ref, o_ref, dq_ref, dk_ref, dv_ref, s_ref, p_ref
):
    tiles, width, rows = q_ref.shape
    heads = width // HEAD_DIM
    lanes = heads * rows
    block = rows
    dk_ref[...] = jnp.zeros_like(dk_ref)
    dv_ref[...] = jnp.zeros_like(dv_ref)
    keep = lax.broadcasted_iota(jnp.int32, (block, rows), 0) <= lax.broadcasted_iota(
        jnp.int32, (block, rows), 1
    )
    keep = jnp.concatenate([keep] * heads, axis=1)

    def side(ref, j):
        return jnp.concatenate(
            [ref[j, HEAD_DIM * h : HEAD_DIM * (h + 1), :] for h in range(heads)], axis=1
        )

    def at(kb):
        return pl.ds(pl.multiple_of(kb * block, block), block)

    def tile(step, carry):
        j = tiles - 1 - step
        q = side(q_ref, j)
        g = side(g_ref, j)

        def scores(kb, top):
            s = dot(k_ref[at(kb), :], q, 1, 0)
            s_ref[at(kb), :] = s
            return jnp.maximum(top, jnp.max(s, axis=0, keepdims=True))

        s = jnp.where(keep, dot(k_ref[at(j), :], q, 1, 0), -1e30)
        s_ref[at(j), :] = s
        top = lax.fori_loop(0, j, scores, jnp.max(s, axis=0, keepdims=True))

        def forward(kb, state):
            total, out = state
            p = jnp.exp2(s_ref[at(kb), :] - top)
            low = p.astype(BF)
            p_ref[at(kb), :] = low
            return (
                total + jnp.sum(p, axis=0, keepdims=True),
                out + dot(vt_ref[:, at(kb)], low, 1, 0),
            )

        total, out = lax.fori_loop(
            0,
            j + 1,
            forward,
            (jnp.zeros((1, lanes), F32), jnp.zeros((HEAD_DIM, lanes), F32)),
        )
        inverse = 1.0 / total
        out = out * inverse
        scaled = (g.astype(F32) * inverse).astype(BF)
        delta = jnp.sum(scaled.astype(F32) * out, axis=0, keepdims=True)
        high = delta.astype(BF)
        rest = delta - high.astype(F32)
        middle = rest.astype(BF)
        last = (rest - middle.astype(F32)).astype(BF)
        stacked = jnp.concatenate(
            [scaled, high, middle, last, jnp.zeros((13, lanes), BF)], axis=0
        )
        for h in range(heads):
            o_ref[j, HEAD_DIM * h : HEAD_DIM * (h + 1), :] = out[
                :, h * rows : (h + 1) * rows
            ].astype(BF)

        def backward(kb, dq):
            p = p_ref[at(kb), :]
            dp = dot(v_ref[at(kb), :], stacked, 1, 0)
            ds = (p.astype(F32) * dp).astype(BF)
            dv_ref[at(kb), :] += dot(p, scaled, 1, 1)
            dk_ref[at(kb), :] += dot(ds, q, 1, 1)
            return dq + dot(kt_ref[:, at(kb)], ds, 1, 0)

        dq = lax.fori_loop(0, j + 1, backward, jnp.zeros((HEAD_DIM, lanes), F32))
        dq = dq * (HEAD_DIM**-0.5)
        for h in range(heads):
            dq_ref[j, HEAD_DIM * h : HEAD_DIM * (h + 1), :] = dq[
                :, h * rows : (h + 1) * rows
            ].astype(BF)
        return carry

    lax.fori_loop(0, tiles, tile, 0)


def attention(q, g, key, value):
    tiles, width, rows = q.shape
    length = tiles * rows
    lanes = width // HEAD_DIM * rows
    ones = jnp.concatenate([jnp.full((length, 3), -1, BF), jnp.zeros((length, 13), BF)], axis=1)
    whole = pl.BlockSpec(memory_space=pltpu.VMEM)
    flops = 12 * length * length // 2 * width
    return pl.pallas_call(
        attention_kernel,
        out_shape=[jax.ShapeDtypeStruct(q.shape, BF)] * 2
        + [jax.ShapeDtypeStruct((length, HEAD_DIM), F32)] * 2,
        in_specs=[whole] * 6,
        out_specs=[whole] * 4,
        scratch_shapes=[pltpu.VMEM((length, lanes), F32), pltpu.VMEM((length, lanes), BF)],
        compiler_params=pltpu.CompilerParams(vmem_limit_bytes=56 * 2**20),
        cost_estimate=pl.CostEstimate(
            flops=flops, bytes_accessed=4 * q.size, transcendentals=length * length // 2 * 3
        ),
        name="attention",
    )(q, g, key, jnp.concatenate([value, ones], axis=1), key.T, value.T)


MESH=pl.DeviceIdType.MESH

def bit_orders(dp, ring):
    seq_bits = [("seq", 1 << b) for b in range(ring.bit_length() - 1)]
    dp_bits = [("dp", 1 << b) for b in range(dp.bit_length() - 1)]
    far = seq_bits[2:]
    return (seq_bits[:2] + dp_bits + far, seq_bits[:1] + dp_bits + seq_bits[1:2] + far)

def side_of(bit):
    axis, weight = bit
    return lax.rem(lax.axis_index(axis) // weight, 2)

def partner_of(bit):
    axis, weight = bit
    me = lax.axis_index(axis)
    return {axis: me + weight - 2 * weight * side_of(bit)}

def add_rows(dst, a, b, dst_at, a_at, rows, step):
    def body(i, carry):
        r = pl.multiple_of(i * step, step)
        dst[pl.ds(dst_at + r, step), :] = a[pl.ds(a_at + r, step), :] + b[pl.ds(r, step), :]
        return carry
    lax.fori_loop(0, rows // step, body, 0)

def sum_kernel(orders, x_ref, out_ref, *scratch):
    parts = len(orders)
    stages = len(orders[0])
    rows, cols = x_ref.shape
    wide = cols // parts
    acc, recv, sems = scratch[:parts], scratch[parts:2*parts], scratch[2*parts:]
    send_sem, recv_sem = sems
    barrier = pltpu.get_barrier_semaphore()
    for bit in orders[0]:
        pl.semaphore_signal(barrier, inc=1, device_id=partner_of(bit), device_id_type=MESH)
    pl.semaphore_wait(barrier, stages)
    def copy(p, s, src, dst, bit):
        return pltpu.make_async_remote_copy(src_ref=src, dst_ref=dst, send_sem=send_sem.at[p, s], recv_sem=recv_sem.at[p, s],
            device_id=partner_of(bit), device_id_type=MESH)
    columns = [pl.ds(p * wide, wide) for p in range(parts)]
    start = [0] * parts
    whole = [0] * parts
    live = {}
    base = [0]
    for s in range(stages): base.append(base[-1] + rows // 2 ** min(s + 1, stages - 1))
    def launch(p, s):
        bit = orders[p][s]
        if s < stages - 1:
            half = rows // 2 ** (s + 1)
            other = pl.multiple_of(start[p] + (1 - side_of(bit)) * half, half)
            src = x_ref.at[pl.ds(other, half), columns[p]] if s == 0 else acc[p].at[pl.ds(other, half), :]
        else:
            half = rows // 2 ** s
            src = acc[p].at[pl.ds(pl.multiple_of(start[p], half), half), :]
        live[p] = copy(p, s, src, recv[p].at[pl.ds(base[s], half), :], bit)
        live[p].start()
    for p in range(parts): launch(p, 0)
    for s in range(stages):
        for p in range(parts):
            bit = orders[p][s]
            live[p].wait()
            half = rows // 2 ** min(s + 1, stages - 1)
            step = 16 if half % 64 else 64
            got = recv[p].at[pl.ds(base[s], half), :]
            if s == 0:
                mine = side_of(bit) * half
                whole[p] = mine
                add_rows(acc[p], x_ref.at[:, columns[p]], got, 0, pl.multiple_of(mine, half), half, step)
                start[p] = 0
            elif s < stages - 1:
                mine = pl.multiple_of(start[p] + side_of(bit) * half, half)
                add_rows(acc[p], acc[p], got, mine, mine, half, step)
                whole[p] = whole[p] + side_of(bit) * half
                start[p] = start[p] + side_of(bit) * half
            else:
                at = pl.multiple_of(start[p], half)
                add_rows(out_ref.at[:, columns[p]], acc[p], got, pl.multiple_of(whole[p], half), at, half, step)
            if s < stages - 1: launch(p, s + 1)
    def spread(p, s):
        bit = orders[p][s]
        half = rows // 2 ** (s + 1)
        src = out_ref.at[pl.ds(pl.multiple_of(whole[p], half), half), columns[p]]
        live[p] = copy(p, 2 * stages - 2 - s, src, src, bit)
        live[p].start()
    for p in range(parts): spread(p, stages - 2)
    for s in range(stages - 2, -1, -1):
        for p in range(parts):
            live[p].wait()
            whole[p] = whole[p] - side_of(orders[p][s]) * (rows // 2 ** (s + 1))
            if s: spread(p, s - 1)

def total_of(x, dp, ring, collective_id):
    orders = bit_orders(dp, ring)
    rows, cols = x.shape
    parts, stages = len(orders), len(orders[0])
    wide = cols // parts
    got = sum(rows // 2 ** min(s + 1, stages - 1) for s in range(stages))
    whole = pl.BlockSpec(memory_space=pltpu.VMEM)
    return pl.pallas_call(functools.partial(sum_kernel, orders),
        out_shape=jax.ShapeDtypeStruct(x.shape, BF), in_specs=[whole], out_specs=whole,
        scratch_shapes=[pltpu.VMEM((rows // 2, wide), BF)] * parts + [pltpu.VMEM((got, wide), BF)] * parts
        + [pltpu.SemaphoreType.DMA((parts, 2 * stages - 1))] * 2,
        compiler_params=pltpu.CompilerParams(collective_id=collective_id, has_side_effects=True, vmem_limit_bytes=56*2**20),
        name="total")(x)


def local(
    hidden_in,
    positions,
    ln1_gain,
    ln1_bias,
    ln2_gain,
    ln2_bias,
    query_projection,
    query_bias,
    shared_key_weight,
    shared_key_bias,
    shared_value_weight,
    shared_value_bias,
    output_weight,
    output_bias,
    up_weight,
    up_bias,
    down_weight,
    down_bias,
    cotangent,
):
    seq_count, local_len = hidden_in.shape[0], hidden_in.shape[1]
    ring = lax.axis_size("seq")
    groups = ring // seq_count
    per_group = HEADS // groups
    width = per_group * HEAD_DIM
    length = ring * local_len
    hidden = hidden_in.astype(F32)
    cosine, sine = angles_of(positions)
    normed_a, pull_a = jax.vjp(layer_norm, hidden, ln1_gain, ln1_bias)
    normed_m, pull_m = jax.vjp(layer_norm, hidden, ln2_gain, ln2_bias)
    normed_a = normed_a.astype(BF)
    normed_m = normed_m.astype(BF)

    def swap(x):
        return lax.all_to_all(x, "seq", split_axis=0, concat_axis=0, tiled=True)

    kv_weight = jnp.concatenate([shared_key_weight, shared_value_weight], axis=1)
    kv_bias = jnp.concatenate([shared_key_bias, shared_value_bias])
    kv_pre = jnp.einsum("stc,cw->swt", normed_a, kv_weight, preferred_element_type=F32)
    kv_pre = kv_pre + kv_bias[:, None]
    kv_low = jnp.concatenate(
        [rotary_rows(kv_pre[:, :HEAD_DIM], cosine, sine), kv_pre[:, HEAD_DIM:]], axis=1
    ).astype(BF)
    kv_send = jnp.broadcast_to(
        kv_low[:, None], (seq_count, groups, 2 * HEAD_DIM, local_len)
    ).reshape(ring, 2 * HEAD_DIM, local_len)
    query_pre = jnp.einsum("stc,cw->swt", normed_a, query_projection, preferred_element_type=F32)
    query_pre = (query_pre + query_bias[:, None]).reshape(seq_count, HEADS, HEAD_DIM, local_len)
    query_low = (rotary_rows(query_pre, cosine[:, None], sine[:, None]) * (LOG2E / 8.0)).astype(BF)
    query_send = query_low.reshape(ring, width, local_len)
    grad_attended = jnp.einsum(
        "stc,wc->swt", cotangent, output_weight, preferred_element_type=F32
    ).astype(BF)
    grad_send = grad_attended.reshape(ring, width, local_len)
    query_send, kv_send, grad_send = lax.optimization_barrier((query_send, kv_send, grad_send))
    kv_here = swap(kv_send)
    query_here = swap(query_send)
    grad_here = swap(grad_send)

    up_pre = jnp.einsum("stc,cf->stf", normed_m, up_weight, preferred_element_type=F32) + up_bias
    activation, pull_gelu = jax.vjp(gelu_exact, up_pre)
    activation = activation.astype(BF)
    feedforward = jnp.einsum(
        "stf,fc->stc", activation, down_weight, preferred_element_type=F32
    )
    activation_gradient = jnp.einsum(
        "stc,fc->stf", cotangent, down_weight, preferred_element_type=F32
    )
    grad_up = pull_gelu(activation_gradient)[0].astype(BF)
    grad_w_down = jnp.einsum(
        "stf,stc->fc", activation, cotangent, preferred_element_type=F32
    ).astype(BF)
    grad_w_up = jnp.einsum("stc,stf->cf", normed_m, grad_up, preferred_element_type=F32).astype(BF)
    grad_normed_m = jnp.einsum("stf,cf->stc", grad_up, up_weight, preferred_element_type=F32)
    kv_here, query_here, grad_here, grad_w_up, grad_w_down, feedforward, grad_normed_m = lax.optimization_barrier(
        (kv_here, query_here, grad_here, grad_w_up, grad_w_down, feedforward, grad_normed_m)
    )
    grad_w_down = lax.psum(grad_w_down, ("dp", "seq"))
    grad_b_up = jnp.sum(grad_up.astype(F32), axis=(0, 1))
    grad_b_down = jnp.sum(cotangent.astype(F32), axis=(0, 1))

    def to_tiles(x):
        tile_len = max(TILE, local_len)
        x = x.reshape(length // tile_len, tile_len // local_len, width, local_len)
        return x.transpose(0, 2, 1, 3).reshape(length // tile_len, width, tile_len)

    def from_tiles(x):
        tile_len = max(TILE, local_len)
        x = x.reshape(length // tile_len, width, tile_len // local_len, local_len)
        return x.transpose(0, 2, 1, 3).reshape(ring, width, local_len)

    kv_rows = kv_here.transpose(0, 2, 1).reshape(length, 2 * HEAD_DIM)
    out, dq, dk, dv = attention(
        to_tiles(query_here), to_tiles(grad_here), kv_rows[:, :HEAD_DIM], kv_rows[:, HEAD_DIM:]
    )
    out, dq, dk, dv, grad_w_up, grad_w_down = lax.optimization_barrier(
        (out, dq, dk, dv, grad_w_up, grad_w_down)
    )
    grad_w_up = lax.psum(grad_w_up, ("dp", "seq"))
    attended = swap(from_tiles(out)).reshape(seq_count, D, local_len)
    query_back = swap(from_tiles(dq)).reshape(seq_count, HEADS, HEAD_DIM, local_len)
    kv_part = jnp.concatenate([dk * (1.0 / LOG2E), dv], axis=1).astype(BF)
    kv_back = swap(kv_part.reshape(ring, local_len, 2 * HEAD_DIM)).astype(F32)
    kv_grad = jnp.sum(kv_back.reshape(seq_count, groups, local_len, 2 * HEAD_DIM), axis=1)
    kv_grad = kv_grad.astype(BF).astype(F32).transpose(0, 2, 1)

    attention_out = jnp.einsum(
        "swt,wc->stc", attended, output_weight, preferred_element_type=F32
    )
    layer_out = hidden + attention_out + feedforward + (output_bias + down_bias)
    grad_w_out = jnp.einsum("swt,stc->wc", attended, cotangent, preferred_element_type=F32)

    kv_raw = jnp.concatenate(
        [rotary_rows(kv_grad[:, :HEAD_DIM], cosine, -sine), kv_grad[:, HEAD_DIM:]], axis=1
    ).astype(BF)
    query_raw = (
        rotary_rows(query_back.astype(F32), cosine[:, None], -sine[:, None])
        .astype(BF)
        .reshape(seq_count, D, local_len)
    )
    raw = jnp.concatenate([query_raw, kv_raw], axis=1)
    weight = jnp.concatenate([query_projection, kv_weight], axis=1)
    grad_w_qkv = jnp.einsum("stc,swt->cw", normed_a, raw, preferred_element_type=F32)
    grad_b_qkv = jnp.sum(raw.astype(F32), axis=(0, 2))
    grad_normed_a = jnp.einsum("swt,cw->stc", raw, weight, preferred_element_type=F32)
    grad_hidden_a, grad_ln1_gain, grad_ln1_bias = pull_a(grad_normed_a)
    grad_hidden_m, grad_ln2_gain, grad_ln2_bias = pull_m(grad_normed_m)
    input_grad = cotangent.astype(F32) + grad_hidden_a + grad_hidden_m

    vectors = jnp.concatenate(
        [
            grad_ln1_gain,
            grad_ln1_bias,
            grad_ln2_gain,
            grad_ln2_bias,
            grad_b_qkv,
            grad_b_up,
            grad_b_down,
        ]
    )
    dp = lax.axis_size("dp")
    unit = 16 * dp * ring // 2
    square = D * (2 * D + 2 * HEAD_DIM)
    filled = square // D + -(-vectors.size // D)
    padded = -(-filled // unit) * unit
    rest = jnp.concatenate(
        [
            grad_w_qkv[:, :D],
            grad_w_out,
            grad_w_qkv[:, D:].T,
            jnp.pad(vectors, (0, (padded * D - square) - vectors.size)).reshape(-1, D),
        ],
        axis=0,
    ).astype(BF)
    rest = total_of(rest, dp, ring, 3)
    rest, grad_w_up = lax.optimization_barrier((rest, grad_w_up))
    rest = rest.astype(F32)
    vectors = rest[square // D :].reshape(-1)
    rest_kv = rest[2 * D : 2 * D + 2 * HEAD_DIM]
    qkv = D + 2 * HEAD_DIM
    ff = up_weight.shape[1]
    b_qkv = vectors[4 * D : 4 * D + qkv]
    b_up = vectors[4 * D + qkv : 4 * D + qkv + ff]
    b_down = vectors[4 * D + qkv + ff : 4 * D + qkv + ff + D]
    return (
        layer_out,
        input_grad,
        vectors[:D],
        vectors[D : 2 * D],
        vectors[2 * D : 3 * D],
        vectors[3 * D : 4 * D],
        rest[:D],
        b_qkv[:D],
        rest_kv[:HEAD_DIM].T,
        b_qkv[D : D + HEAD_DIM],
        rest_kv[HEAD_DIM:].T,
        b_qkv[D + HEAD_DIM :],
        rest[D : 2 * D],
        b_down,
        grad_w_up.astype(F32),
        b_up,
        grad_w_down.astype(F32),
        b_down,
    )


def solution(mesh):
    rows = P("dp", "seq", None)
    placed = (rows, P("dp", "seq")) + (P(),) * 16 + (rows,)
    return jax.shard_map(
        local,
        mesh=mesh,
        in_specs=placed,
        out_specs=(rows, rows) + (P(),) * 16,
        check_vma=False,
    )
```

```python
import functools
import math

import jax
import jax.numpy as jnp
from jax import lax
from jax.experimental import pallas as pl
from jax.experimental.pallas import tpu as pltpu
from jax.sharding import PartitionSpec as P

D = 768
HEADS = 12
HEAD_DIM = 64
ROT_DIMS = 16
BF = jnp.bfloat16
F32 = jnp.float32
LOG2E = math.log2(math.e)


def layer_norm(values, gain, bias):
    center = values - jnp.mean(values, axis=-1, keepdims=True)
    spread = jnp.mean(center * center, axis=-1, keepdims=True)
    return center * lax.rsqrt(spread + 1e-05) * gain + bias


def rotary_rows(values, cosine, sine):
    half = cosine.shape[-2]
    first, second = values[..., :half, :], values[..., half : 2 * half, :]
    return jnp.concatenate(
        [first * cosine - second * sine, second * cosine + first * sine, values[..., 2 * half :, :]],
        axis=-2,
    )


def angles_of(positions):
    half = ROT_DIMS // 2
    frequency = jnp.exp(
        jnp.arange(half).astype(F32) * (-2.0 * math.log(10000.0) / ROT_DIMS)
    )
    angle = positions.astype(F32)[:, None, :] * frequency[None, :, None]
    return jnp.cos(angle), jnp.sin(angle)


MESH = pl.DeviceIdType.MESH


def dot(a, b, ca, cb):
    return lax.dot_general(a, b, (((ca,), (cb,)), ((), ())), preferred_element_type=F32)


def flip(index, weight):
    return index + weight - 2 * weight * lax.rem(index // weight, 2)


def gelu_parts(u):
    e = jnp.exp(u * u * -0.5)
    t = 1.0 / (1.0 + (0.3275911 / math.sqrt(2.0)) * jnp.abs(u))
    poly = t * (
        0.5 * 0.254829592
        + t
        * (
            0.5 * -0.284496736
            + t * (0.5 * 1.421413741 + t * (0.5 * -1.453152027 + t * (0.5 * 1.061405429)))
        )
    )
    tail = poly * e
    return jnp.where(u >= 0, 1.0 - tail, tail), e * (1.0 / math.sqrt(2.0 * math.pi))


def feed_kernel(
    x_ref,
    c_ref,
    up_ref,
    down_ref,
    bias_ref,
    ff_ref,
    gx_ref,
    gup_ref,
    gdown_ref,
    gbias_ref,
    act_ref,
    grad_ref,
):
    tokens = x_ref.shape[0]
    bias = bias_ref[...]
    sub = min(256, tokens)
    for r in range(0, tokens, sub):
        u = dot(x_ref[r : r + sub, :], up_ref[...], 1, 0) + bias
        share, density = gelu_parts(u)
        act_ref[r : r + sub, :] = (u * share).astype(BF)
        da = dot(c_ref[r : r + sub, :], down_ref[...], 1, 1)
        grad_ref[r : r + sub, :] = (da * (share + u * density)).astype(BF)

    @pl.when(pl.program_id(0) == 0)
    def _():
        ff_ref[...] = jnp.zeros_like(ff_ref)
        gx_ref[...] = jnp.zeros_like(gx_ref)

    act, grad = act_ref[...], grad_ref[...]
    ff_ref[...] += dot(act, down_ref[...], 1, 0)
    gx_ref[...] += dot(grad, up_ref[...], 1, 1)
    gdown_ref[...] = dot(act, c_ref[...], 0, 0).astype(BF)
    gup_ref[...] = dot(x_ref[...], grad, 0, 0).astype(BF)
    gbias_ref[...] = jnp.sum(grad.astype(F32), axis=0, keepdims=True)


FEED_STEPS = 6


def feed_forward(x, cot, up_weight, up_bias, down_weight):
    tokens, d = x.shape
    ff = up_weight.shape[1]
    wide = ff // FEED_STEPS
    whole = pl.BlockSpec((tokens, d), lambda i: (0, 0))
    by_column = pl.BlockSpec((d, wide), lambda i: (0, i))
    by_row = pl.BlockSpec((wide, d), lambda i: (i, 0))
    line = pl.BlockSpec((1, wide), lambda i: (0, i))
    return pl.pallas_call(
        feed_kernel,
        grid=(FEED_STEPS,),
        out_shape=[
            jax.ShapeDtypeStruct((tokens, d), F32),
            jax.ShapeDtypeStruct((tokens, d), F32),
            jax.ShapeDtypeStruct((d, ff), BF),
            jax.ShapeDtypeStruct((ff, d), BF),
            jax.ShapeDtypeStruct((1, ff), F32),
        ],
        in_specs=[whole, whole, by_column, by_row, line],
        out_specs=[whole, whole, by_column, by_row, line],
        scratch_shapes=[pltpu.VMEM((tokens, wide), BF), pltpu.VMEM((tokens, wide), BF)],
        compiler_params=pltpu.CompilerParams(vmem_limit_bytes=56 * 2**20),
        cost_estimate=pl.CostEstimate(
            flops=12 * tokens * d * ff,
            bytes_accessed=16 * d * ff,
            transcendentals=tokens * ff,
        ),
        name="feed_forward",
    )(x, cot, up_weight, down_weight, up_bias)


KEYS = 256


def shipped(upper_index, ring, tiles):
    more = upper_index + 1
    return (tiles * (2 * upper_index + 1 - ring) + more) // (2 * more)


def attention_kernel(
    seqs,
    groups,
    q_ref,
    g_ref,
    all_ref,
    att_ref,
    dq_ref,
    slot_ref,
    kvt_ref,
    flat_ref,
    rows_ref,
    dkv_ref,
    s_ref,
    p_ref,
    qs_ref,
    gs_ref,
    qin_ref,
    gin_ref,
    atts_ref,
    dqs_ref,
    stage_ref,
    half_ref,
    load_sem,
    own_sem,
    in_send,
    in_recv,
    out_send,
    out_recv,
    core_send,
    core_recv,
    slot_send,
    slot_recv,
):
    tiles, width, rows = q_ref.shape
    ring = all_ref.shape[0]
    chips = ring // 2
    heads = width // HEAD_DIM
    lanes = heads * rows
    length = ring * rows
    me = lax.axis_index("seq")
    chip, core = me // 2, lax.rem(me, 2)
    upper = me // chips
    partner = ring - 1 - me
    count = shipped(me + (1 - upper) * (partner - me), ring, tiles)

    def to(index):
        return {"seq": index}

    barrier = pltpu.get_barrier_semaphore()

    def greet(index):
        pl.semaphore_signal(barrier, inc=1, device_id=to(index), device_id_type=MESH)

    greet(partner)
    greet(flip(me, 1))
    for m in range(1, chips):
        greet(lax.rem(me + 2 * m, ring))
    pl.semaphore_wait(barrier, chips + 1)

    def load(s, slot):
        return pltpu.make_async_copy(
            all_ref.at[:, pl.ds(pl.multiple_of(s * 2 * HEAD_DIM, 2 * HEAD_DIM), 2 * HEAD_DIM), :],
            kvt_ref.at[slot],
            load_sem.at[slot],
        )

    load(0, 0).start()

    def place(k):
        return lax.rem(k, seqs) * groups + k // seqs

    def remote(src, dst, sems, which, k, index):
        return pltpu.make_async_remote_copy(
            src_ref=src,
            dst_ref=dst,
            send_sem=sems[0].at[which, k],
            recv_sem=sems[1].at[which, k],
            device_id=to(index),
            device_id_type=MESH,
        )

    def q_in(k):
        return remote(q_ref.at[place(k)], qin_ref.at[k], (in_send, in_recv), 0, k, partner)

    def g_in(k):
        return remote(g_ref.at[place(k)], gin_ref.at[k], (in_send, in_recv), 1, k, partner)

    def att_out(k):
        return remote(atts_ref.at[k], att_ref.at[place(k)], (out_send, out_recv), 0, k, partner)

    def dq_out(k):
        return remote(dqs_ref.at[k], dq_ref.at[place(k)], (out_send, out_recv), 1, k, partner)

    def start_in(k, carry):
        q_in(k).start()
        g_in(k).start()
        return carry

    lax.fori_loop(0, count * upper, start_in, 0)

    def core_out(s):
        return pltpu.make_async_remote_copy(
            src_ref=stage_ref.at[s, :, 1 - core],
            dst_ref=half_ref.at[s],
            send_sem=core_send.at[s],
            recv_sem=core_recv.at[s],
            device_id=to(flip(me, 1)),
            device_id_type=MESH,
        )

    def slot_out(s, m):
        target = lax.rem(chip + m, chips)
        return pltpu.make_async_remote_copy(
            src_ref=half_ref.at[s, target],
            dst_ref=slot_ref.at[s, m],
            send_sem=slot_send.at[s, m],
            recv_sem=slot_recv.at[s, m],
            device_id=to(2 * target + core),
            device_id_type=MESH,
        )

    def slot_own(s):
        return pltpu.make_async_copy(half_ref.at[s, chip], slot_ref.at[s, 0], own_sem.at[s])

    def pass_on(s):
        core_out(s).wait_recv()

        def add(m, carry):
            half_ref[s, m] = (
                half_ref[s, m].astype(F32) + stage_ref[s, m, core].astype(F32)
            ).astype(BF)
            return carry

        lax.fori_loop(0, chips, add, 0)
        slot_own(s).start()
        for m in range(1, chips):
            slot_out(s, m).start()

    qs_ref[...] = jnp.zeros_like(qs_ref)
    gs_ref[...] = jnp.zeros_like(gs_ref)

    def at(b, n=1):
        return pl.ds(pl.multiple_of(b * KEYS, KEYS), n * KEYS)

    def blocks(count_blocks, body, state):
        state = lax.fori_loop(0, count_blocks // 4, lambda i, c: body(4 * i, 4, c), state)
        pairs = count_blocks // 2
        state = lax.fori_loop(
            count_blocks // 4 * 2, pairs, lambda i, c: body(2 * i, 2, c), state
        )
        return lax.fori_loop(2 * pairs, count_blocks, lambda i, c: body(i, 1, c), state)

    def tile(q_tile, g_tile, att_tile, dq_tile, position):
        start = position * rows
        edge = start // KEYS
        shift = lax.rem(start, KEYS)
        for h in range(heads):
            qs_ref[0:HEAD_DIM, h * rows : (h + 1) * rows] = q_tile[
                h * HEAD_DIM : (h + 1) * HEAD_DIM, :
            ]
        s = dot(rows_ref[at(edge), :], qs_ref[...], 1, 0)
        column = lax.rem(lax.broadcasted_iota(jnp.int32, (1, lanes), 1), rows) + shift
        keep = lax.broadcasted_iota(jnp.int32, (KEYS, lanes), 0) <= column
        s = jnp.where(keep, s, -1e30)
        s_ref[at(edge), :] = s

        def top_of(s, n):
            return jnp.max(s.reshape(n * KEYS // 8, 8, lanes), axis=0)

        def scores(b, n, top):
            s = dot(rows_ref[at(b, n), :], qs_ref[...], 1, 0)
            s_ref[at(b, n), :] = s
            return jnp.maximum(top, top_of(s, n))

        top = jnp.max(blocks(edge, scores, top_of(s, 1)), axis=0, keepdims=True)

        def forward(b, n, state):
            total, out = state
            p = jnp.exp2(s_ref[at(b, n), :] - top)
            low = p.astype(BF)
            p_ref[at(b, n), :] = low
            return (
                total + jnp.sum(p.reshape(n * KEYS // 8, 8, lanes), axis=0),
                out + dot(flat_ref[HEAD_DIM : 2 * HEAD_DIM, at(b, n)], low, 1, 0),
            )

        total, out = blocks(
            edge + 1, forward, (jnp.zeros((8, lanes), F32), jnp.zeros((HEAD_DIM, lanes), F32))
        )
        inverse = 1.0 / jnp.sum(total, axis=0, keepdims=True)
        out = out * inverse
        for h in range(heads):
            att_tile[h * HEAD_DIM : (h + 1) * HEAD_DIM, :] = out[
                :, h * rows : (h + 1) * rows
            ].astype(BF)
        g = jnp.concatenate(
            [g_tile[h * HEAD_DIM : (h + 1) * HEAD_DIM, :] for h in range(heads)], axis=1
        )
        scaled = (g.astype(F32) * inverse).astype(BF)
        gs_ref[HEAD_DIM : 2 * HEAD_DIM, :] = scaled
        delta = jnp.sum(scaled.astype(F32) * out, axis=0, keepdims=True)

        def backward(b, n, dq):
            p = p_ref[at(b, n), :]
            dp = dot(rows_ref[at(b, n), :], gs_ref[...], 1, 0)
            ds = (p.astype(F32) * (dp - delta)).astype(BF)
            dkv_ref[at(b, n), :] += dot(p, gs_ref[...], 1, 1) + dot(ds, qs_ref[...], 1, 1)
            return dq + dot(flat_ref[0:HEAD_DIM, at(b, n)], ds, 1, 0)

        dq = blocks(edge + 1, backward, jnp.zeros((HEAD_DIM, lanes), F32))
        dq = dq * (HEAD_DIM**-0.5)
        for h in range(heads):
            dq_tile[h * HEAD_DIM : (h + 1) * HEAD_DIM, :] = dq[
                :, h * rows : (h + 1) * rows
            ].astype(BF)

    per_block = KEYS // rows

    def sequence(s, carry):
        slot = lax.rem(s, 2)
        load(s, slot).wait()
        pl.when(s + 1 < seqs)(lambda: load(s + 1, 1 - slot).start())
        dkv_ref[...] = jnp.zeros_like(dkv_ref)

        def turn(b, c):
            wide = jnp.concatenate(
                [kvt_ref[slot, b * per_block + i] for i in range(per_block)], axis=1
            )
            flat_ref[:, at(b)] = wide
            rows_ref[at(b), :] = wide.T
            return c

        lax.fori_loop(0, length // KEYS, turn, 0)
        given = (count - s + seqs - 1) // seqs
        own = groups - upper * given
        taken = (1 - upper) * given
        later = jnp.minimum(s, 1)

        def work(u, c):
            v = u - taken * later
            mine = (v >= 0) & (v < own)

            @pl.when(mine)
            def _():
                t = s * groups + upper * given + v
                tile(q_ref.at[t], g_ref.at[t], att_ref.at[t], dq_ref.at[t], me)

            @pl.when(jnp.logical_not(mine))
            def _():
                k = (u - own * (1 - later)) * seqs + s
                q_in(k).wait_recv()
                g_in(k).wait_recv()
                tile(qin_ref.at[k], gin_ref.at[k], atts_ref.at[k], dqs_ref.at[k], partner)
                att_out(k).start()
                dq_out(k).start()

            pl.when((u == 0) & (s > 0))(lambda: pass_on(s - 1))
            return c

        lax.fori_loop(0, own + taken, work, 0)
        stage_ref[s] = dkv_ref[...].reshape(chips, 2, rows, 2 * HEAD_DIM).astype(BF)
        core_out(s).start()
        return carry

    lax.fori_loop(0, seqs, sequence, 0)
    pass_on(seqs - 1)

    def end_given(k, c):
        q_in(k).wait_send()
        g_in(k).wait_send()
        att_out(k).wait_recv()
        dq_out(k).wait_recv()
        return c

    def end_taken(k, c):
        att_out(k).wait_send()
        dq_out(k).wait_send()
        return c

    lax.fori_loop(0, count * upper, end_given, 0)
    lax.fori_loop(0, count * (1 - upper), end_taken, 0)

    def end(s, c):
        core_out(s).wait_send()
        slot_own(s).wait()
        for m in range(1, chips):
            slot_out(s, m).wait()
        return c

    lax.fori_loop(0, seqs, end, 0)


def attention(q, g, kv_all, seqs):
    tiles, width, rows = q.shape
    ring = kv_all.shape[0]
    chips = ring // 2
    length = ring * rows
    lanes = width // HEAD_DIM * rows
    most = max(shipped(i, ring, tiles) for i in range(chips, ring))
    vmem = pl.BlockSpec(memory_space=pltpu.VMEM)
    anywhere = pl.BlockSpec(memory_space=pl.ANY)
    pair = 2 * HEAD_DIM
    dma = pltpu.SemaphoreType.DMA
    return pl.pallas_call(
        functools.partial(attention_kernel, seqs, tiles // seqs),
        out_shape=[
            jax.ShapeDtypeStruct(q.shape, BF),
            jax.ShapeDtypeStruct(q.shape, BF),
            jax.ShapeDtypeStruct((seqs, chips, rows, pair), BF),
        ],
        in_specs=[vmem, vmem, anywhere],
        out_specs=[vmem, vmem, anywhere],
        scratch_shapes=[
            pltpu.VMEM((2, ring, pair, rows), BF),
            pltpu.VMEM((pair, length), BF),
            pltpu.VMEM((length, pair), BF),
            pltpu.VMEM((length, pair), F32),
            pltpu.VMEM((length, lanes), F32),
            pltpu.VMEM((length, lanes), BF),
            pltpu.VMEM((pair, lanes), BF),
            pltpu.VMEM((pair, lanes), BF),
            pltpu.VMEM((most, width, rows), BF),
            pltpu.VMEM((most, width, rows), BF),
            pltpu.VMEM((most, width, rows), BF),
            pltpu.VMEM((most, width, rows), BF),
            pltpu.VMEM((seqs, chips, 2, rows, pair), BF),
            pltpu.VMEM((seqs, chips, rows, pair), BF),
            dma((2,)),
            dma((seqs,)),
            dma((2, most)),
            dma((2, most)),
            dma((2, most)),
            dma((2, most)),
            dma((seqs,)),
            dma((seqs,)),
            dma((seqs, chips)),
            dma((seqs, chips)),
        ],
        compiler_params=pltpu.CompilerParams(
            collective_id=2, has_side_effects=True, vmem_limit_bytes=58 * 2**20
        ),
        cost_estimate=pl.CostEstimate(
            flops=12 * tiles * rows * width * length * 4,
            bytes_accessed=8 * q.size,
            transcendentals=tiles * lanes * length // 2,
        ),
        name="attention",
    )(q, g, kv_all)


def bit_orders(dp, ring):
    seq_bits = [("seq", 1 << b) for b in range(ring.bit_length() - 1)]
    dp_bits = [("dp", 1 << b) for b in range(dp.bit_length() - 1)]
    far = seq_bits[2:]
    return (seq_bits[:2] + dp_bits + far, seq_bits[:1] + dp_bits + seq_bits[1:2] + far)

def side_of(bit):
    axis, weight = bit
    return lax.rem(lax.axis_index(axis) // weight, 2)

def partner_of(bit):
    axis, weight = bit
    me = lax.axis_index(axis)
    return {axis: me + weight - 2 * weight * side_of(bit)}

def add_rows(dst, a, b, dst_at, a_at, rows, step):
    def body(i, carry):
        r = pl.multiple_of(i * step, step)
        dst[pl.ds(dst_at + r, step), :] = a[pl.ds(a_at + r, step), :] + b[pl.ds(r, step), :]
        return carry
    lax.fori_loop(0, rows // step, body, 0)

def sum_kernel(orders, x_ref, out_ref, *scratch):
    parts = len(orders)
    stages = len(orders[0])
    rows, cols = x_ref.shape
    wide = cols // parts
    acc, recv, sems = scratch[:parts], scratch[parts:2*parts], scratch[2*parts:]
    send_sem, recv_sem = sems
    barrier = pltpu.get_barrier_semaphore()
    for bit in orders[0]:
        pl.semaphore_signal(barrier, inc=1, device_id=partner_of(bit), device_id_type=MESH)
    pl.semaphore_wait(barrier, stages)
    def copy(p, s, src, dst, bit):
        return pltpu.make_async_remote_copy(src_ref=src, dst_ref=dst, send_sem=send_sem.at[p, s], recv_sem=recv_sem.at[p, s],
            device_id=partner_of(bit), device_id_type=MESH)
    columns = [pl.ds(p * wide, wide) for p in range(parts)]
    start = [0] * parts
    whole = [0] * parts
    live = {}
    base = [0]
    for s in range(stages): base.append(base[-1] + rows // 2 ** min(s + 1, stages - 1))
    def launch(p, s):
        bit = orders[p][s]
        if s < stages - 1:
            half = rows // 2 ** (s + 1)
            other = pl.multiple_of(start[p] + (1 - side_of(bit)) * half, half)
            src = x_ref.at[pl.ds(other, half), columns[p]] if s == 0 else acc[p].at[pl.ds(other, half), :]
        else:
            half = rows // 2 ** s
            src = acc[p].at[pl.ds(pl.multiple_of(start[p], half), half), :]
        live[p] = copy(p, s, src, recv[p].at[pl.ds(base[s], half), :], bit)
        live[p].start()
    for p in range(parts): launch(p, 0)
    for s in range(stages):
        for p in range(parts):
            bit = orders[p][s]
            live[p].wait()
            half = rows // 2 ** min(s + 1, stages - 1)
            step = 16 if half % 64 else 64
            got = recv[p].at[pl.ds(base[s], half), :]
            if s == 0:
                mine = side_of(bit) * half
                whole[p] = mine
                add_rows(acc[p], x_ref.at[:, columns[p]], got, 0, pl.multiple_of(mine, half), half, step)
                start[p] = 0
            elif s < stages - 1:
                mine = pl.multiple_of(start[p] + side_of(bit) * half, half)
                add_rows(acc[p], acc[p], got, mine, mine, half, step)
                whole[p] = whole[p] + side_of(bit) * half
                start[p] = start[p] + side_of(bit) * half
            else:
                at = pl.multiple_of(start[p], half)
                add_rows(out_ref.at[:, columns[p]], acc[p], got, pl.multiple_of(whole[p], half), at, half, step)
            if s < stages - 1: launch(p, s + 1)
    def spread(p, s):
        bit = orders[p][s]
        half = rows // 2 ** (s + 1)
        src = out_ref.at[pl.ds(pl.multiple_of(whole[p], half), half), columns[p]]
        live[p] = copy(p, 2 * stages - 2 - s, src, src, bit)
        live[p].start()
    for p in range(parts): spread(p, stages - 2)
    for s in range(stages - 2, -1, -1):
        for p in range(parts):
            live[p].wait()
            whole[p] = whole[p] - side_of(orders[p][s]) * (rows // 2 ** (s + 1))
            if s: spread(p, s - 1)

def total_of(x, dp, ring, collective_id):
    orders = bit_orders(dp, ring)
    rows, cols = x.shape
    parts, stages = len(orders), len(orders[0])
    wide = cols // parts
    got = sum(rows // 2 ** min(s + 1, stages - 1) for s in range(stages))
    whole = pl.BlockSpec(memory_space=pltpu.VMEM)
    return pl.pallas_call(functools.partial(sum_kernel, orders),
        out_shape=jax.ShapeDtypeStruct(x.shape, BF), in_specs=[whole], out_specs=whole,
        scratch_shapes=[pltpu.VMEM((rows // 2, wide), BF)] * parts + [pltpu.VMEM((got, wide), BF)] * parts
        + [pltpu.SemaphoreType.DMA((parts, 2 * stages - 1))] * 2,
        compiler_params=pltpu.CompilerParams(collective_id=collective_id, has_side_effects=True, vmem_limit_bytes=56*2**20),
        name="total")(x)


def local(
    hidden_in,
    positions,
    ln1_gain,
    ln1_bias,
    ln2_gain,
    ln2_bias,
    query_projection,
    query_bias,
    shared_key_weight,
    shared_key_bias,
    shared_value_weight,
    shared_value_bias,
    output_weight,
    output_bias,
    up_weight,
    up_bias,
    down_weight,
    down_bias,
    cotangent,
):
    seq_count, local_len = hidden_in.shape[0], hidden_in.shape[1]
    ring = lax.axis_size("seq")
    groups = ring // seq_count
    per_group = HEADS // groups
    width = per_group * HEAD_DIM
    hidden = hidden_in.astype(F32)
    cosine, sine = angles_of(positions)
    normed_a, pull_a = jax.vjp(layer_norm, hidden, ln1_gain, ln1_bias)
    normed_m, pull_m = jax.vjp(layer_norm, hidden, ln2_gain, ln2_bias)
    normed_a = normed_a.astype(BF)
    normed_m = normed_m.astype(BF)

    tokens = seq_count * local_len
    kv_weight = jnp.concatenate([shared_key_weight, shared_value_weight], axis=1)
    kv_bias = jnp.concatenate([shared_key_bias, shared_value_bias])
    kv_pre = jnp.einsum("stc,cw->swt", normed_a, kv_weight, preferred_element_type=F32)
    kv_pre = kv_pre + kv_bias[:, None]
    kv_low = jnp.concatenate(
        [rotary_rows(kv_pre[:, :HEAD_DIM], cosine, sine), kv_pre[:, HEAD_DIM:]], axis=1
    ).astype(BF)
    kv_all = lax.all_gather(kv_low.reshape(-1, local_len), "seq")
    query_pre = jnp.einsum("stc,cw->swt", normed_a, query_projection, preferred_element_type=F32)
    query_pre = (query_pre + query_bias[:, None]).reshape(seq_count, HEADS, HEAD_DIM, local_len)
    query_low = (rotary_rows(query_pre, cosine[:, None], sine[:, None]) * (LOG2E / 8.0)).astype(BF)
    query_tiles = query_low.reshape(-1, width, local_len)
    grad_attended = jnp.einsum(
        "stc,wc->swt", cotangent, output_weight, preferred_element_type=F32
    ).astype(BF)
    grad_tiles = grad_attended.reshape(-1, width, local_len)

    feedforward, grad_normed_m, grad_w_up, grad_w_down, grad_b_up = feed_forward(
        normed_m.reshape(tokens, D),
        cotangent.reshape(tokens, D),
        up_weight,
        up_bias[None],
        down_weight,
    )
    feedforward = feedforward.reshape(hidden.shape)
    grad_normed_m = grad_normed_m.reshape(hidden.shape)
    grad_b_up = grad_b_up[0]
    grad_b_down = jnp.sum(cotangent.astype(F32), axis=(0, 1))
    query_tiles, grad_tiles, kv_all, grad_w_up, grad_w_down = lax.optimization_barrier(
        (query_tiles, grad_tiles, kv_all, grad_w_up, grad_w_down)
    )
    grad_w_down = lax.psum(grad_w_down, ("dp", "seq"))
    out, dq, dkv = attention(query_tiles, grad_tiles, kv_all, seq_count)
    out, dq, dkv, grad_w_up, grad_w_down = lax.optimization_barrier(
        (out, dq, dkv, grad_w_up, grad_w_down)
    )
    grad_w_up = lax.psum(grad_w_up, ("dp", "seq"))
    attended = out.reshape(seq_count, D, local_len)
    query_back = dq.reshape(seq_count, HEADS, HEAD_DIM, local_len)
    kv_grad = jnp.sum(dkv.astype(F32), axis=1)
    kv_scale = jnp.concatenate([jnp.full((HEAD_DIM,), 1.0 / LOG2E), jnp.ones((HEAD_DIM,))])
    kv_grad = (kv_grad * kv_scale).astype(BF).astype(F32).transpose(0, 2, 1)

    attention_out = jnp.einsum(
        "swt,wc->stc", attended, output_weight, preferred_element_type=F32
    )
    layer_out = hidden + attention_out + feedforward + (output_bias + down_bias)
    grad_w_out = jnp.einsum("swt,stc->wc", attended, cotangent, preferred_element_type=F32)

    kv_raw = jnp.concatenate(
        [rotary_rows(kv_grad[:, :HEAD_DIM], cosine, -sine), kv_grad[:, HEAD_DIM:]], axis=1
    ).astype(BF)
    query_raw = (
        rotary_rows(query_back.astype(F32), cosine[:, None], -sine[:, None])
        .astype(BF)
        .reshape(seq_count, D, local_len)
    )
    raw = jnp.concatenate([query_raw, kv_raw], axis=1)
    weight = jnp.concatenate([query_projection, kv_weight], axis=1)
    grad_w_qkv = jnp.einsum("stc,swt->cw", normed_a, raw, preferred_element_type=F32)
    grad_b_qkv = jnp.sum(raw.astype(F32), axis=(0, 2))
    grad_normed_a = jnp.einsum("swt,cw->stc", raw, weight, preferred_element_type=F32)
    grad_hidden_a, grad_ln1_gain, grad_ln1_bias = pull_a(grad_normed_a)
    grad_hidden_m, grad_ln2_gain, grad_ln2_bias = pull_m(grad_normed_m)
    input_grad = cotangent.astype(F32) + grad_hidden_a + grad_hidden_m

    vectors = jnp.concatenate(
        [
            grad_ln1_gain,
            grad_ln1_bias,
            grad_ln2_gain,
            grad_ln2_bias,
            grad_b_qkv,
            grad_b_up,
            grad_b_down,
        ]
    )
    dp = lax.axis_size("dp")
    unit = 16 * dp * ring // 2
    square = D * (2 * D + 2 * HEAD_DIM)
    filled = square // D + -(-vectors.size // D)
    padded = -(-filled // unit) * unit
    rest = jnp.concatenate(
        [
            grad_w_qkv[:, :D],
            grad_w_out,
            grad_w_qkv[:, D:].T,
            jnp.pad(vectors, (0, (padded * D - square) - vectors.size)).reshape(-1, D),
        ],
        axis=0,
    ).astype(BF)
    rest = total_of(rest, dp, ring, 3)
    rest, grad_w_up = lax.optimization_barrier((rest, grad_w_up))
    rest = rest.astype(F32)
    vectors = rest[square // D :].reshape(-1)
    rest_kv = rest[2 * D : 2 * D + 2 * HEAD_DIM]
    qkv = D + 2 * HEAD_DIM
    ff = up_weight.shape[1]
    b_qkv = vectors[4 * D : 4 * D + qkv]
    b_up = vectors[4 * D + qkv : 4 * D + qkv + ff]
    b_down = vectors[4 * D + qkv + ff : 4 * D + qkv + ff + D]
    return (
        layer_out,
        input_grad,
        vectors[:D],
        vectors[D : 2 * D],
        vectors[2 * D : 3 * D],
        vectors[3 * D : 4 * D],
        rest[:D],
        b_qkv[:D],
        rest_kv[:HEAD_DIM].T,
        b_qkv[D : D + HEAD_DIM],
        rest_kv[HEAD_DIM:].T,
        b_qkv[D + HEAD_DIM :],
        rest[D : 2 * D],
        b_down,
        grad_w_up.astype(F32),
        b_up,
        grad_w_down.astype(F32),
        b_down,
    )


def solution(mesh):
    rows = P("dp", "seq", None)
    placed = (rows, P("dp", "seq")) + (P(),) * 16 + (rows,)
    return jax.shard_map(
        local,
        mesh=mesh,
        in_specs=placed,
        out_specs=(rows, rows) + (P(),) * 16,
        check_vma=False,
    )
```

```python
import functools
import math

import jax
import jax.numpy as jnp
from jax import lax
from jax.experimental import pallas as pl
from jax.experimental.pallas import tpu as pltpu
from jax.sharding import PartitionSpec as P

D = 768
HEADS = 12
HEAD_DIM = 64
ROT_DIMS = 16
BF = jnp.bfloat16
F32 = jnp.float32
LOG2E = math.log2(math.e)


def layer_norm(values, gain, bias):
    center = values - jnp.mean(values, axis=-1, keepdims=True)
    spread = jnp.mean(center * center, axis=-1, keepdims=True)
    return center * lax.rsqrt(spread + 1e-05) * gain + bias


def rotary_rows(values, cosine, sine):
    half = cosine.shape[-2]
    first, second = values[..., :half, :], values[..., half : 2 * half, :]
    return jnp.concatenate(
        [first * cosine - second * sine, second * cosine + first * sine, values[..., 2 * half :, :]],
        axis=-2,
    )


def angles_of(positions):
    half = ROT_DIMS // 2
    frequency = jnp.exp(
        jnp.arange(half).astype(F32) * (-2.0 * math.log(10000.0) / ROT_DIMS)
    )
    angle = positions.astype(F32)[:, None, :] * frequency[None, :, None]
    return jnp.cos(angle), jnp.sin(angle)


MESH = pl.DeviceIdType.MESH


def dot(a, b, ca, cb):
    return lax.dot_general(a, b, (((ca,), (cb,)), ((), ())), preferred_element_type=F32)


def flip(index, weight):
    return index + weight - 2 * weight * lax.rem(index // weight, 2)


def gelu_parts(u):
    e = jnp.exp(u * u * -0.5)
    t = 1.0 / (1.0 + (0.3275911 / math.sqrt(2.0)) * jnp.abs(u))
    poly = t * (
        0.5 * 0.254829592
        + t
        * (
            0.5 * -0.284496736
            + t * (0.5 * 1.421413741 + t * (0.5 * -1.453152027 + t * (0.5 * 1.061405429)))
        )
    )
    tail = poly * e
    return jnp.where(u >= 0, 1.0 - tail, tail), e * (1.0 / math.sqrt(2.0 * math.pi))


def feed_kernel(
    x_ref,
    c_ref,
    up_ref,
    down_ref,
    bias_ref,
    ff_ref,
    gx_ref,
    gup_ref,
    gdown_ref,
    gbias_ref,
    act_ref,
    grad_ref,
):
    tokens = x_ref.shape[0]
    bias = bias_ref[...]
    sub = min(256, tokens)
    for r in range(0, tokens, sub):
        u = dot(x_ref[r : r + sub, :], up_ref[...], 1, 0) + bias
        share, density = gelu_parts(u)
        act_ref[r : r + sub, :] = (u * share).astype(BF)
        da = dot(c_ref[r : r + sub, :], down_ref[...], 1, 1)
        grad_ref[r : r + sub, :] = (da * (share + u * density)).astype(BF)

    @pl.when(pl.program_id(0) == 0)
    def _():
        ff_ref[...] = jnp.zeros_like(ff_ref)
        gx_ref[...] = jnp.zeros_like(gx_ref)

    act, grad = act_ref[...], grad_ref[...]
    ff_ref[...] += dot(act, down_ref[...], 1, 0)
    gx_ref[...] += dot(grad, up_ref[...], 1, 1)
    gdown_ref[...] = dot(act, c_ref[...], 0, 0).astype(BF)
    gup_ref[...] = dot(x_ref[...], grad, 0, 0).astype(BF)
    gbias_ref[...] = jnp.sum(grad.astype(F32), axis=0, keepdims=True)


FEED_STEPS = 6


def feed_forward(x, cot, up_weight, up_bias, down_weight):
    tokens, d = x.shape
    ff = up_weight.shape[1]
    wide = ff // FEED_STEPS
    whole = pl.BlockSpec((tokens, d), lambda i: (0, 0))
    by_column = pl.BlockSpec((d, wide), lambda i: (0, i))
    by_row = pl.BlockSpec((wide, d), lambda i: (i, 0))
    line = pl.BlockSpec((1, wide), lambda i: (0, i))
    return pl.pallas_call(
        feed_kernel,
        grid=(FEED_STEPS,),
        out_shape=[
            jax.ShapeDtypeStruct((tokens, d), F32),
            jax.ShapeDtypeStruct((tokens, d), F32),
            jax.ShapeDtypeStruct((d, ff), BF),
            jax.ShapeDtypeStruct((ff, d), BF),
            jax.ShapeDtypeStruct((1, ff), F32),
        ],
        in_specs=[whole, whole, by_column, by_row, line],
        out_specs=[whole, whole, by_column, by_row, line],
        scratch_shapes=[pltpu.VMEM((tokens, wide), BF), pltpu.VMEM((tokens, wide), BF)],
        compiler_params=pltpu.CompilerParams(vmem_limit_bytes=56 * 2**20),
        cost_estimate=pl.CostEstimate(
            flops=12 * tokens * d * ff,
            bytes_accessed=16 * d * ff,
            transcendentals=tokens * ff,
        ),
        name="feed_forward",
    )(x, cot, up_weight, down_weight, up_bias)


KEYS = 256


def shipped(upper_index, ring, tiles):
    more = upper_index + 2
    return (tiles * (2 * upper_index + 1 - ring) + more) // (2 * more)


class Exchange:
    def __init__(self, index, order, array, out, acc, recv, first, wide, sems):
        self.index, self.order, self.sems = index, order, sems
        self.array, self.out, self.acc, self.recv = array, out, acc, recv
        self.columns = pl.ds(first, wide)
        self.rows = array.shape[0]
        self.halvings = halvings_of(self.rows, len(order))
        self.waits = len(order) + self.halvings

    def size(self, s):
        return self.rows >> min(s, self.halvings)

    def base(self, s):
        return sum(self.size(t + 1) for t in range(s))

    def start(self, s, first=1):
        at = 0
        for t in range(first, min(s, self.halvings)):
            at = at + side_of(self.order[t]) * self.size(t + 1)
        return at

    def copy(self, k):
        stages = len(self.order)
        if k < stages:
            bit = self.order[k]
            size = self.size(k + 1)
            other = self.start(k) + ((1 - side_of(bit)) * size if k < self.halvings else 0)
            rows = pl.ds(pl.multiple_of(other, size), size)
            src = (self.array if k == 0 else self.acc).at[rows, self.columns]
            dst = self.recv.at[pl.ds(self.base(k), size), self.columns]
        else:
            t = self.waits - 1 - k
            bit = self.order[t]
            size = self.size(t + 1)
            rows = pl.ds(pl.multiple_of(self.start(t + 1, 0), size), size)
            src = dst = self.out.at[rows, self.columns]
        return pltpu.make_async_remote_copy(
            src_ref=src,
            dst_ref=dst,
            send_sem=self.sems[0].at[self.index, k],
            recv_sem=self.sems[1].at[self.index, k],
            device_id=partner_of(bit),
            device_id_type=MESH,
        )

    def fill(self):
        half = self.size(1)
        rows = pl.ds(pl.multiple_of(side_of(self.order[0]) * half, half), half)
        return pltpu.make_async_copy(
            self.array.at[rows, self.columns],
            self.acc.at[:, self.columns],
            self.sems[2].at[self.index],
        )

    def empty(self):
        size = self.size(self.halvings)
        rows = pl.ds(pl.multiple_of(self.start(self.halvings), size), size)
        to = pl.ds(pl.multiple_of(self.start(self.halvings, 0), size), size)
        return pltpu.make_async_copy(
            self.acc.at[rows, self.columns],
            self.out.at[to, self.columns],
            self.sems[3].at[self.index],
        )

    def begin(self):
        self.fill().start()
        self.copy(0).start()

    def take(self, k):
        self.copy(k).wait()
        if k < len(self.order):
            if k == 0:
                self.fill().wait()
            size = self.size(k + 1)
            start = self.start(k + 1)
            step = 16
            base = self.base(k)

            def add(i, carry):
                r = pl.multiple_of(i * step, step)
                mine = pl.ds(pl.multiple_of(start + r, step), step)
                self.acc[mine, self.columns] = (
                    self.acc[mine, self.columns] + self.recv[pl.ds(base + r, step), self.columns]
                )
                return carry

            lax.fori_loop(0, size // step, add, 0)
            if k == len(self.order) - 1:
                self.empty().start()
                self.empty().wait()
        if k + 1 < self.waits:
            self.copy(k + 1).start()


def halvings_of(rows, stages):
    count = 0
    while count < stages - 1 and rows % (32 << count) == 0:
        count += 1
    return count


def exchange_rows(rows, stages):
    count = halvings_of(rows, stages)
    return sum(rows >> min(s + 1, count) for s in range(stages))


def attention_kernel(
    seqs,
    groups,
    orders,
    q_ref,
    g_ref,
    all_ref,
    down_ref,
    up_ref,
    att_ref,
    dq_ref,
    slot_ref,
    down_sum_ref,
    up_sum_ref,
    kvt_ref,
    flat_ref,
    rows_ref,
    dkv_ref,
    s_ref,
    p_ref,
    qs_ref,
    gs_ref,
    qin_ref,
    gin_ref,
    atts_ref,
    dqs_ref,
    stage_ref,
    half_ref,
    load_sem,
    own_sem,
    in_send,
    in_recv,
    out_send,
    out_recv,
    core_send,
    core_recv,
    slot_send,
    slot_recv,
    down_acc_ref,
    up_acc_ref,
    down_recv_ref,
    up_recv_ref,
    graw_ref,
    sum_send,
    sum_recv,
    fill_sem,
    empty_sem,
):
    tiles, width, rows = q_ref.shape
    ring = all_ref.shape[0]
    chips = ring // 2
    heads = width // HEAD_DIM
    lanes = heads * rows
    length = ring * rows
    me = lax.axis_index("seq")
    chip, core = me // 2, lax.rem(me, 2)
    upper = me // chips
    partner = ring - 1 - me
    count = shipped(me + (1 - upper) * (partner - me), ring, tiles)

    def to(index):
        return {"seq": index}

    barrier = pltpu.get_barrier_semaphore()

    def greet(index):
        pl.semaphore_signal(barrier, inc=1, device_id=to(index), device_id_type=MESH)

    greet(partner)
    greet(flip(me, 1))
    for m in range(1, chips):
        greet(lax.rem(me + 2 * m, ring))
    across = [bit for bit in orders[0] if bit[0] == "dp"]
    for bit in across:
        pl.semaphore_signal(
            barrier, inc=1, device_id=partner_of(bit), device_id_type=MESH
        )
    pl.semaphore_wait(barrier, chips + 1 + len(across))

    def load(s, slot):
        return pltpu.make_async_copy(
            all_ref.at[:, pl.ds(pl.multiple_of(s * 2 * HEAD_DIM, 2 * HEAD_DIM), 2 * HEAD_DIM), :],
            kvt_ref.at[slot],
            load_sem.at[slot],
        )

    load(0, 0).start()

    def place(k):
        return lax.rem(k, seqs) * groups + k // seqs

    def remote(src, dst, sems, which, k, index):
        return pltpu.make_async_remote_copy(
            src_ref=src,
            dst_ref=dst,
            send_sem=sems[0].at[which, k],
            recv_sem=sems[1].at[which, k],
            device_id=to(index),
            device_id_type=MESH,
        )

    def q_in(k):
        return remote(q_ref.at[place(k)], qin_ref.at[k], (in_send, in_recv), 0, k, partner)

    def g_in(k):
        return remote(g_ref.at[place(k)], gin_ref.at[k], (in_send, in_recv), 1, k, partner)

    def att_out(k):
        return remote(atts_ref.at[k], att_ref.at[place(k)], (out_send, out_recv), 0, k, partner)

    def dq_out(k):
        return remote(dqs_ref.at[k], dq_ref.at[place(k)], (out_send, out_recv), 1, k, partner)

    def given_of(s):
        return (count - s + seqs - 1) // seqs

    def start_in(s):
        def one(i, carry):
            q_in(i * seqs + s).start()
            g_in(i * seqs + s).start()
            return carry

        lax.fori_loop(0, upper * given_of(s), one, 0)

    start_in(0)

    sems = (sum_send, sum_recv, fill_sem, empty_sem)
    half_down, half_up = down_ref.shape[1] // 2, up_ref.shape[1] // 2
    teams = []
    for i in range(2):
        teams.append(
            [
                Exchange(
                    2 * i, orders[0], down_ref, down_sum_ref, down_acc_ref, down_recv_ref,
                    i * half_down, half_down, sems,
                ),
                Exchange(
                    2 * i + 1, orders[1], up_ref, up_sum_ref, up_acc_ref, up_recv_ref,
                    i * half_up, half_up, sems,
                ),
            ]
        )
    most_waits = [max(e.waits for e in team) for team in teams]
    acts = sorted(
        [(k + 0.75 * i, i, k) for i in range(2) for k in range(most_waits[i])]
    )
    acts = [(i, k) for _, i, k in acts]
    for team in teams:
        for e in team:
            e.begin()

    def act(number, carry):
        for n, (i, k) in enumerate(acts):
            def run(i=i, k=k):
                for e in teams[i]:
                    if k < e.waits:
                        e.take(k)

            pl.when(number == n)(run)
        return carry

    def cost_of(position):
        return position * rows // KEYS + 2

    total_cost = (tiles - upper * count) * cost_of(me) + (1 - upper) * count * cost_of(partner)

    def advance(acted, progress):
        due = jnp.minimum(progress * (len(acts) + 1) // total_cost, len(acts))
        lax.fori_loop(acted, due, act, 0)
        return jnp.maximum(acted, due)

    def core_out(s):
        return pltpu.make_async_remote_copy(
            src_ref=stage_ref.at[lax.rem(s, 2), :, 1 - core],
            dst_ref=half_ref.at[s],
            send_sem=core_send.at[s],
            recv_sem=core_recv.at[s],
            device_id=to(flip(me, 1)),
            device_id_type=MESH,
        )

    def slot_out(s, m):
        target = lax.rem(chip + m, chips)
        return pltpu.make_async_remote_copy(
            src_ref=half_ref.at[s, target],
            dst_ref=slot_ref.at[s, m],
            send_sem=slot_send.at[s, m],
            recv_sem=slot_recv.at[s, m],
            device_id=to(2 * target + core),
            device_id_type=MESH,
        )

    def slot_own(s):
        return pltpu.make_async_copy(half_ref.at[s, chip], slot_ref.at[s, 0], own_sem.at[s])

    def pass_on(s):
        core_out(s).wait()

        def add(m, carry):
            half_ref[s, m] = (
                half_ref[s, m].astype(F32) + stage_ref[lax.rem(s, 2), m, core].astype(F32)
            ).astype(BF)
            return carry

        lax.fori_loop(0, chips, add, 0)
        slot_own(s).start()
        for m in range(1, chips):
            slot_out(s, m).start()

    qs_ref[...] = jnp.zeros_like(qs_ref)
    gs_ref[...] = jnp.zeros_like(gs_ref)

    def at(b, n=1):
        return pl.ds(pl.multiple_of(b * KEYS, KEYS), n * KEYS)

    def blocks(count_blocks, body, state):
        state = lax.fori_loop(0, count_blocks // 4, lambda i, c: body(4 * i, 4, c), state)
        pairs = count_blocks // 2
        state = lax.fori_loop(
            count_blocks // 4 * 2, pairs, lambda i, c: body(2 * i, 2, c), state
        )
        return lax.fori_loop(2 * pairs, count_blocks, lambda i, c: body(i, 1, c), state)

    def spread(tile, out):
        for h in range(heads):
            tile[h * HEAD_DIM : (h + 1) * HEAD_DIM, :] = out[:, h * rows : (h + 1) * rows].astype(
                BF
            )

    def gather(tile, out):
        for h in range(heads):
            out[0:HEAD_DIM, h * rows : (h + 1) * rows] = tile[
                h * HEAD_DIM : (h + 1) * HEAD_DIM, :
            ]

    def tile(mine, t, k, position, acted, progress):
        start = position * rows
        edge = start // KEYS
        shift = lax.rem(start, KEYS)
        other = jnp.logical_not(mine)

        @pl.when(mine)
        def _():
            gather(q_ref.at[t], qs_ref)
            gather(g_ref.at[t], graw_ref)

        @pl.when(other)
        def _():
            q_in(k).wait_recv()
            g_in(k).wait_recv()
            gather(qin_ref.at[k], qs_ref)
            gather(gin_ref.at[k], graw_ref)

        s = dot(rows_ref[at(edge), :], qs_ref[...], 1, 0)
        column = lax.rem(lax.broadcasted_iota(jnp.int32, (1, lanes), 1), rows) + shift
        keep = lax.broadcasted_iota(jnp.int32, (KEYS, lanes), 0) <= column
        s = jnp.where(keep, s, -1e30)
        s_ref[at(edge), :] = s

        def top_of(s, n):
            return jnp.max(s.reshape(n * KEYS // 8, 8, lanes), axis=0)

        def scores(b, n, top):
            s = dot(rows_ref[at(b, n), :], qs_ref[...], 1, 0)
            s_ref[at(b, n), :] = s
            return jnp.maximum(top, top_of(s, n))

        top = jnp.max(blocks(edge, scores, top_of(s, 1)), axis=0, keepdims=True)

        def forward(b, n, state):
            total, out = state
            p = jnp.exp2(s_ref[at(b, n), :] - top)
            low = p.astype(BF)
            p_ref[at(b, n), :] = low
            return (
                total + jnp.sum(p.reshape(n * KEYS // 8, 8, lanes), axis=0),
                out + dot(flat_ref[HEAD_DIM : 2 * HEAD_DIM, at(b, n)], low, 1, 0),
            )

        total, out = blocks(
            edge + 1, forward, (jnp.zeros((8, lanes), F32), jnp.zeros((HEAD_DIM, lanes), F32))
        )
        inverse = 1.0 / jnp.sum(total, axis=0, keepdims=True)
        out = out * inverse
        pl.when(mine)(lambda: spread(att_ref.at[t], out))

        @pl.when(other)
        def _():
            spread(atts_ref.at[k], out)
            att_out(k).start()

        acted = advance(acted, progress + (edge + 2) // 2)
        g = graw_ref[...]
        scaled = (g.astype(F32) * inverse).astype(BF)
        gs_ref[HEAD_DIM : 2 * HEAD_DIM, :] = scaled
        delta = jnp.sum(scaled.astype(F32) * out, axis=0, keepdims=True)

        def backward(b, n, dq):
            p = p_ref[at(b, n), :]
            dp = dot(rows_ref[at(b, n), :], gs_ref[...], 1, 0)
            ds = (p.astype(F32) * (dp - delta)).astype(BF)
            dkv_ref[at(b, n), :] += dot(p, gs_ref[...], 1, 1) + dot(ds, qs_ref[...], 1, 1)
            return dq + dot(flat_ref[0:HEAD_DIM, at(b, n)], ds, 1, 0)

        dq = blocks(edge + 1, backward, jnp.zeros((HEAD_DIM, lanes), F32))
        dq = dq * (HEAD_DIM**-0.5)
        pl.when(mine)(lambda: spread(dq_ref.at[t], dq))

        @pl.when(other)
        def _():
            spread(dqs_ref.at[k], dq)
            dq_out(k).start()

        progress = progress + edge + 2
        return advance(acted, progress), progress

    per_block = KEYS // rows

    def sequence(s, state):
        slot = lax.rem(s, 2)
        load(s, slot).wait()
        pl.when(s + 1 < seqs)(lambda: load(s + 1, 1 - slot).start())
        dkv_ref[...] = jnp.zeros_like(dkv_ref)

        def turn(b, c):
            wide = jnp.concatenate(
                [kvt_ref[slot, b * per_block + i] for i in range(per_block)], axis=1
            )
            flat_ref[:, at(b)] = wide
            rows_ref[at(b), :] = wide.T
            return c

        lax.fori_loop(0, length // KEYS, turn, 0)
        given = given_of(s)
        own = groups - upper * given
        taken = (1 - upper) * given
        later = jnp.minimum(s, 1)

        def work(u, state):
            acted, progress = state
            v = u - taken * later
            mine = (v >= 0) & (v < own)
            t = s * groups + upper * given + jnp.clip(v, 0, own - 1)
            k = jnp.clip(u - own * (1 - later), 0, jnp.maximum(taken - 1, 0)) * seqs + s
            position = jnp.where(mine, me, partner)
            state = tile(mine, t, k, position, acted, progress)
            pl.when((u == 0) & (s > 0))(lambda: pass_on(s - 1))
            pl.when((u == 0) & (s + 1 < seqs))(lambda: start_in(s + 1))
            return state

        state = lax.fori_loop(0, own + taken, work, state)
        stage_ref[slot] = dkv_ref[...].reshape(chips, 2, rows, 2 * HEAD_DIM).astype(BF)
        core_out(s).start()
        return state

    acted, _ = lax.fori_loop(0, seqs, sequence, (jnp.int32(0), jnp.int32(0)))
    pass_on(seqs - 1)
    lax.fori_loop(acted, len(acts), act, 0)

    def end_given(k, c):
        q_in(k).wait_send()
        g_in(k).wait_send()
        att_out(k).wait_recv()
        dq_out(k).wait_recv()
        return c

    def end_taken(k, c):
        att_out(k).wait_send()
        dq_out(k).wait_send()
        return c

    lax.fori_loop(0, count * upper, end_given, 0)
    lax.fori_loop(0, count * (1 - upper), end_taken, 0)

    def end(s, c):
        slot_own(s).wait()
        for m in range(1, chips):
            slot_out(s, m).wait()
        return c

    lax.fori_loop(0, seqs, end, 0)


def attention(q, g, kv_all, down, up, seqs, dp):
    tiles, width, rows = q.shape
    ring = kv_all.shape[0]
    chips = ring // 2
    length = ring * rows
    lanes = width // HEAD_DIM * rows
    most = max(shipped(i, ring, tiles) for i in range(chips, ring))
    vmem = pl.BlockSpec(memory_space=pltpu.VMEM)
    anywhere = pl.BlockSpec(memory_space=pl.ANY)
    pair = 2 * HEAD_DIM
    dma = pltpu.SemaphoreType.DMA
    orders = bit_orders(dp, ring)
    stages = len(orders[0])
    return pl.pallas_call(
        functools.partial(attention_kernel, seqs, tiles // seqs, orders),
        out_shape=[
            jax.ShapeDtypeStruct(q.shape, BF),
            jax.ShapeDtypeStruct(q.shape, BF),
            jax.ShapeDtypeStruct((seqs, chips, rows, pair), BF),
            jax.ShapeDtypeStruct(down.shape, BF),
            jax.ShapeDtypeStruct(up.shape, BF),
        ],
        in_specs=[vmem, vmem, anywhere, anywhere, anywhere],
        out_specs=[vmem, vmem, anywhere, anywhere, anywhere],
        scratch_shapes=[
            pltpu.VMEM((2, ring, pair, rows), BF),
            pltpu.VMEM((pair, length), BF),
            pltpu.VMEM((length, pair), BF),
            pltpu.VMEM((length, pair), F32),
            pltpu.VMEM((length, lanes), F32),
            pltpu.VMEM((length, lanes), BF),
            pltpu.VMEM((pair, lanes), BF),
            pltpu.VMEM((pair, lanes), BF),
            pltpu.VMEM((most, width, rows), BF),
            pltpu.VMEM((most, width, rows), BF),
            pltpu.VMEM((most, width, rows), BF),
            pltpu.VMEM((most, width, rows), BF),
            pltpu.VMEM((2, chips, 2, rows, pair), BF),
            pltpu.VMEM((seqs, chips, rows, pair), BF),
            dma((2,)),
            dma((seqs,)),
            dma((2, most)),
            dma((2, most)),
            dma((2, most)),
            dma((2, most)),
            dma((seqs,)),
            dma((seqs,)),
            dma((seqs, chips)),
            dma((seqs, chips)),
            pltpu.VMEM((down.shape[0] // 2, down.shape[1]), BF),
            pltpu.VMEM((up.shape[0] // 2, up.shape[1]), BF),
            pltpu.VMEM((exchange_rows(down.shape[0], stages), down.shape[1]), BF),
            pltpu.VMEM((exchange_rows(up.shape[0], stages), up.shape[1]), BF),
            pltpu.VMEM((HEAD_DIM, lanes), BF),
            dma((4, 2 * stages)),
            dma((4, 2 * stages)),
            dma((4,)),
            dma((4,)),
        ],
        compiler_params=pltpu.CompilerParams(
            collective_id=2, has_side_effects=True, vmem_limit_bytes=60 * 2**20
        ),
        cost_estimate=pl.CostEstimate(
            flops=12 * tiles * rows * width * length * 4,
            bytes_accessed=8 * q.size,
            transcendentals=tiles * lanes * length // 2,
        ),
        name="attention",
    )(q, g, kv_all, down, up)


def bit_orders(dp, ring):
    seq_bits = [("seq", 1 << b) for b in range(ring.bit_length() - 1)]
    dp_bits = [("dp", 1 << b) for b in range(dp.bit_length() - 1)]
    far = seq_bits[2:]
    return (seq_bits[:2] + dp_bits + far, seq_bits[:1] + dp_bits + seq_bits[1:2] + far)

def side_of(bit):
    axis, weight = bit
    return lax.rem(lax.axis_index(axis) // weight, 2)

def partner_of(bit):
    axis, weight = bit
    me = lax.axis_index(axis)
    return {axis: me + weight - 2 * weight * side_of(bit)}

def add_rows(dst, a, b, dst_at, a_at, rows, step):
    def body(i, carry):
        r = pl.multiple_of(i * step, step)
        dst[pl.ds(dst_at + r, step), :] = a[pl.ds(a_at + r, step), :] + b[pl.ds(r, step), :]
        return carry
    lax.fori_loop(0, rows // step, body, 0)

def sum_kernel(orders, x_ref, out_ref, *scratch):
    parts = len(orders)
    stages = len(orders[0])
    rows, cols = x_ref.shape
    wide = cols // parts
    acc, recv, sems = scratch[:parts], scratch[parts:2*parts], scratch[2*parts:]
    send_sem, recv_sem = sems
    barrier = pltpu.get_barrier_semaphore()
    for bit in orders[0]:
        pl.semaphore_signal(barrier, inc=1, device_id=partner_of(bit), device_id_type=MESH)
    pl.semaphore_wait(barrier, stages)
    def copy(p, s, src, dst, bit):
        return pltpu.make_async_remote_copy(src_ref=src, dst_ref=dst, send_sem=send_sem.at[p, s], recv_sem=recv_sem.at[p, s],
            device_id=partner_of(bit), device_id_type=MESH)
    columns = [pl.ds(p * wide, wide) for p in range(parts)]
    start = [0] * parts
    whole = [0] * parts
    live = {}
    base = [0]
    for s in range(stages): base.append(base[-1] + rows // 2 ** min(s + 1, stages - 1))
    def launch(p, s):
        bit = orders[p][s]
        if s < stages - 1:
            half = rows // 2 ** (s + 1)
            other = pl.multiple_of(start[p] + (1 - side_of(bit)) * half, half)
            src = x_ref.at[pl.ds(other, half), columns[p]] if s == 0 else acc[p].at[pl.ds(other, half), :]
        else:
            half = rows // 2 ** s
            src = acc[p].at[pl.ds(pl.multiple_of(start[p], half), half), :]
        live[p] = copy(p, s, src, recv[p].at[pl.ds(base[s], half), :], bit)
        live[p].start()
    for p in range(parts): launch(p, 0)
    for s in range(stages):
        for p in range(parts):
            bit = orders[p][s]
            live[p].wait()
            half = rows // 2 ** min(s + 1, stages - 1)
            step = 16 if half % 64 else 64
            got = recv[p].at[pl.ds(base[s], half), :]
            if s == 0:
                mine = side_of(bit) * half
                whole[p] = mine
                add_rows(acc[p], x_ref.at[:, columns[p]], got, 0, pl.multiple_of(mine, half), half, step)
                start[p] = 0
            elif s < stages - 1:
                mine = pl.multiple_of(start[p] + side_of(bit) * half, half)
                add_rows(acc[p], acc[p], got, mine, mine, half, step)
                whole[p] = whole[p] + side_of(bit) * half
                start[p] = start[p] + side_of(bit) * half
            else:
                at = pl.multiple_of(start[p], half)
                add_rows(out_ref.at[:, columns[p]], acc[p], got, pl.multiple_of(whole[p], half), at, half, step)
            if s < stages - 1: launch(p, s + 1)
    def spread(p, s):
        bit = orders[p][s]
        half = rows // 2 ** (s + 1)
        src = out_ref.at[pl.ds(pl.multiple_of(whole[p], half), half), columns[p]]
        live[p] = copy(p, 2 * stages - 2 - s, src, src, bit)
        live[p].start()
    for p in range(parts): spread(p, stages - 2)
    for s in range(stages - 2, -1, -1):
        for p in range(parts):
            live[p].wait()
            whole[p] = whole[p] - side_of(orders[p][s]) * (rows // 2 ** (s + 1))
            if s: spread(p, s - 1)

def total_of(x, dp, ring, collective_id):
    orders = bit_orders(dp, ring)
    rows, cols = x.shape
    parts, stages = len(orders), len(orders[0])
    wide = cols // parts
    got = sum(rows // 2 ** min(s + 1, stages - 1) for s in range(stages))
    whole = pl.BlockSpec(memory_space=pltpu.VMEM)
    return pl.pallas_call(functools.partial(sum_kernel, orders),
        out_shape=jax.ShapeDtypeStruct(x.shape, BF), in_specs=[whole], out_specs=whole,
        scratch_shapes=[pltpu.VMEM((rows // 2, wide), BF)] * parts + [pltpu.VMEM((got, wide), BF)] * parts
        + [pltpu.SemaphoreType.DMA((parts, 2 * stages - 1))] * 2,
        compiler_params=pltpu.CompilerParams(collective_id=collective_id, has_side_effects=True, vmem_limit_bytes=56*2**20),
        name="total")(x)


def local(
    hidden_in,
    positions,
    ln1_gain,
    ln1_bias,
    ln2_gain,
    ln2_bias,
    query_projection,
    query_bias,
    shared_key_weight,
    shared_key_bias,
    shared_value_weight,
    shared_value_bias,
    output_weight,
    output_bias,
    up_weight,
    up_bias,
    down_weight,
    down_bias,
    cotangent,
):
    seq_count, local_len = hidden_in.shape[0], hidden_in.shape[1]
    ring = lax.axis_size("seq")
    groups = ring // seq_count
    per_group = HEADS // groups
    width = per_group * HEAD_DIM
    hidden = hidden_in.astype(F32)
    cosine, sine = angles_of(positions)
    normed_a, pull_a = jax.vjp(layer_norm, hidden, ln1_gain, ln1_bias)
    normed_m, pull_m = jax.vjp(layer_norm, hidden, ln2_gain, ln2_bias)
    normed_a = normed_a.astype(BF)
    normed_m = normed_m.astype(BF)

    tokens = seq_count * local_len
    kv_weight = jnp.concatenate([shared_key_weight, shared_value_weight], axis=1)
    kv_bias = jnp.concatenate([shared_key_bias, shared_value_bias])
    kv_pre = jnp.einsum("stc,cw->swt", normed_a, kv_weight, preferred_element_type=F32)
    kv_pre = kv_pre + kv_bias[:, None]
    kv_low = jnp.concatenate(
        [rotary_rows(kv_pre[:, :HEAD_DIM], cosine, sine), kv_pre[:, HEAD_DIM:]], axis=1
    ).astype(BF)
    kv_all = lax.all_gather(kv_low.reshape(-1, local_len), "seq")
    query_pre = jnp.einsum("stc,cw->swt", normed_a, query_projection, preferred_element_type=F32)
    query_pre = (query_pre + query_bias[:, None]).reshape(seq_count, HEADS, HEAD_DIM, local_len)
    query_low = (rotary_rows(query_pre, cosine[:, None], sine[:, None]) * (LOG2E / 8.0)).astype(BF)
    query_tiles = query_low.reshape(-1, width, local_len)
    grad_attended = jnp.einsum(
        "stc,wc->swt", cotangent, output_weight, preferred_element_type=F32
    ).astype(BF)
    grad_tiles = grad_attended.reshape(-1, width, local_len)

    feedforward, grad_normed_m, grad_w_up, grad_w_down, grad_b_up = feed_forward(
        normed_m.reshape(tokens, D),
        cotangent.reshape(tokens, D),
        up_weight,
        up_bias[None],
        down_weight,
    )
    feedforward = feedforward.reshape(hidden.shape)
    grad_normed_m = grad_normed_m.reshape(hidden.shape)
    grad_b_up = grad_b_up[0]
    grad_b_down = jnp.sum(cotangent.astype(F32), axis=(0, 1))
    query_tiles, grad_tiles, kv_all, grad_w_up, grad_w_down = lax.optimization_barrier(
        (query_tiles, grad_tiles, kv_all, grad_w_up, grad_w_down)
    )
    dp = lax.axis_size("dp")
    out, dq, dkv, grad_w_down, grad_w_up = attention(
        query_tiles, grad_tiles, kv_all, grad_w_down, grad_w_up, seq_count, dp
    )
    attended = out.reshape(seq_count, D, local_len)
    query_back = dq.reshape(seq_count, HEADS, HEAD_DIM, local_len)
    kv_grad = jnp.sum(dkv.astype(F32), axis=1)
    kv_scale = jnp.concatenate([jnp.full((HEAD_DIM,), 1.0 / LOG2E), jnp.ones((HEAD_DIM,))])
    kv_grad = (kv_grad * kv_scale).astype(BF).astype(F32).transpose(0, 2, 1)

    attention_out = jnp.einsum(
        "swt,wc->stc", attended, output_weight, preferred_element_type=F32
    )
    layer_out = hidden + attention_out + feedforward + (output_bias + down_bias)
    grad_w_out = jnp.einsum("swt,stc->wc", attended, cotangent, preferred_element_type=F32)

    kv_raw = jnp.concatenate(
        [rotary_rows(kv_grad[:, :HEAD_DIM], cosine, -sine), kv_grad[:, HEAD_DIM:]], axis=1
    ).astype(BF)
    query_raw = (
        rotary_rows(query_back.astype(F32), cosine[:, None], -sine[:, None])
        .astype(BF)
        .reshape(seq_count, D, local_len)
    )
    raw = jnp.concatenate([query_raw, kv_raw], axis=1)
    weight = jnp.concatenate([query_projection, kv_weight], axis=1)
    grad_w_qkv = jnp.einsum("stc,swt->cw", normed_a, raw, preferred_element_type=F32)
    grad_b_qkv = jnp.sum(raw.astype(F32), axis=(0, 2))
    grad_normed_a = jnp.einsum("swt,cw->stc", raw, weight, preferred_element_type=F32)
    grad_hidden_a, grad_ln1_gain, grad_ln1_bias = pull_a(grad_normed_a)
    grad_hidden_m, grad_ln2_gain, grad_ln2_bias = pull_m(grad_normed_m)
    input_grad = cotangent.astype(F32) + grad_hidden_a + grad_hidden_m

    vectors = jnp.concatenate(
        [
            grad_ln1_gain,
            grad_ln1_bias,
            grad_ln2_gain,
            grad_ln2_bias,
            grad_b_qkv,
            grad_b_up,
            grad_b_down,
        ]
    )
    dp = lax.axis_size("dp")
    unit = 16 * dp * ring // 2
    square = D * (2 * D + 2 * HEAD_DIM)
    filled = square // D + -(-vectors.size // D)
    padded = -(-filled // unit) * unit
    rest = jnp.concatenate(
        [
            grad_w_qkv[:, :D],
            grad_w_out,
            grad_w_qkv[:, D:].T,
            jnp.pad(vectors, (0, (padded * D - square) - vectors.size)).reshape(-1, D),
        ],
        axis=0,
    ).astype(BF)
    rest = total_of(rest, dp, ring, 3)
    rest = rest.astype(F32)
    vectors = rest[square // D :].reshape(-1)
    rest_kv = rest[2 * D : 2 * D + 2 * HEAD_DIM]
    qkv = D + 2 * HEAD_DIM
    ff = up_weight.shape[1]
    b_qkv = vectors[4 * D : 4 * D + qkv]
    b_up = vectors[4 * D + qkv : 4 * D + qkv + ff]
    b_down = vectors[4 * D + qkv + ff : 4 * D + qkv + ff + D]
    return (
        layer_out,
        input_grad,
        vectors[:D],
        vectors[D : 2 * D],
        vectors[2 * D : 3 * D],
        vectors[3 * D : 4 * D],
        rest[:D],
        b_qkv[:D],
        rest_kv[:HEAD_DIM].T,
        b_qkv[D : D + HEAD_DIM],
        rest_kv[HEAD_DIM:].T,
        b_qkv[D + HEAD_DIM :],
        rest[D : 2 * D],
        b_down,
        grad_w_up.astype(F32),
        b_up,
        grad_w_down.astype(F32),
        b_down,
    )


def solution(mesh):
    rows = P("dp", "seq", None)
    placed = (rows, P("dp", "seq")) + (P(),) * 16 + (rows,)
    return jax.shard_map(
        local,
        mesh=mesh,
        in_specs=placed,
        out_specs=(rows, rows) + (P(),) * 16,
        check_vma=False,
    )
```

```python
import functools
import math

import jax
import jax.numpy as jnp
from jax import lax
from jax.experimental import pallas as pl
from jax.experimental.pallas import tpu as pltpu
from jax.sharding import PartitionSpec as P

D = 768
HEADS = 12
HEAD_DIM = 64
ROT_DIMS = 16
BF = jnp.bfloat16
F32 = jnp.float32
LOG2E = math.log2(math.e)


def layer_norm(values, gain, bias):
    center = values - jnp.mean(values, axis=-1, keepdims=True)
    spread = jnp.mean(center * center, axis=-1, keepdims=True)
    return center * lax.rsqrt(spread + 1e-05) * gain + bias


def rotary_rows(values, cosine, sine):
    half = cosine.shape[-2]
    first, second = values[..., :half, :], values[..., half : 2 * half, :]
    return jnp.concatenate(
        [first * cosine - second * sine, second * cosine + first * sine, values[..., 2 * half :, :]],
        axis=-2,
    )


def angles_of(positions):
    half = ROT_DIMS // 2
    frequency = jnp.exp(
        jnp.arange(half).astype(F32) * (-2.0 * math.log(10000.0) / ROT_DIMS)
    )
    angle = positions.astype(F32)[:, None, :] * frequency[None, :, None]
    return jnp.cos(angle), jnp.sin(angle)


MESH = pl.DeviceIdType.MESH


def dot(a, b, ca, cb):
    return lax.dot_general(a, b, (((ca,), (cb,)), ((), ())), preferred_element_type=F32)


def flip(index, weight):
    return index + weight - 2 * weight * lax.rem(index // weight, 2)


def gelu_parts(u):
    e = jnp.exp(u * u * -0.5)
    t = 1.0 / (1.0 + (0.3275911 / math.sqrt(2.0)) * jnp.abs(u))
    poly = t * (
        0.5 * 0.254829592
        + t
        * (
            0.5 * -0.284496736
            + t * (0.5 * 1.421413741 + t * (0.5 * -1.453152027 + t * (0.5 * 1.061405429)))
        )
    )
    tail = poly * e
    return jnp.where(u >= 0, 1.0 - tail, tail), e * (1.0 / math.sqrt(2.0 * math.pi))


def feed_kernel(
    x_ref,
    c_ref,
    up_ref,
    down_ref,
    bias_ref,
    ff_ref,
    gx_ref,
    gup_ref,
    gdown_ref,
    gbias_ref,
    act_ref,
    grad_ref,
):
    tokens = x_ref.shape[0]
    bias = bias_ref[...]
    sub = min(256, tokens)
    for r in range(0, tokens, sub):
        u = dot(x_ref[r : r + sub, :], up_ref[...], 1, 0) + bias
        share, density = gelu_parts(u)
        act_ref[r : r + sub, :] = (u * share).astype(BF)
        da = dot(c_ref[r : r + sub, :], down_ref[...], 1, 1)
        grad_ref[r : r + sub, :] = (da * (share + u * density)).astype(BF)

    @pl.when(pl.program_id(0) == 0)
    def _():
        ff_ref[...] = jnp.zeros_like(ff_ref)
        gx_ref[...] = jnp.zeros_like(gx_ref)

    act, grad = act_ref[...], grad_ref[...]
    ff_ref[...] += dot(act, down_ref[...], 1, 0)
    gx_ref[...] += dot(grad, up_ref[...], 1, 1)
    gdown_ref[...] = dot(act, c_ref[...], 0, 0).astype(BF)
    gup_ref[...] = dot(x_ref[...], grad, 0, 0).astype(BF)
    gbias_ref[...] = jnp.sum(grad.astype(F32), axis=0, keepdims=True)


FEED_STEPS = 6


def feed_forward(x, cot, up_weight, up_bias, down_weight):
    tokens, d = x.shape
    ff = up_weight.shape[1]
    wide = ff // FEED_STEPS
    whole = pl.BlockSpec((tokens, d), lambda i: (0, 0))
    by_column = pl.BlockSpec((d, wide), lambda i: (0, i))
    by_row = pl.BlockSpec((wide, d), lambda i: (i, 0))
    line = pl.BlockSpec((1, wide), lambda i: (0, i))
    return pl.pallas_call(
        feed_kernel,
        grid=(FEED_STEPS,),
        out_shape=[
            jax.ShapeDtypeStruct((tokens, d), F32),
            jax.ShapeDtypeStruct((tokens, d), F32),
            jax.ShapeDtypeStruct((FEED_STEPS * d, wide), BF),
            jax.ShapeDtypeStruct((ff, d), BF),
            jax.ShapeDtypeStruct((1, ff), F32),
        ],
        in_specs=[whole, whole, by_column, by_row, line],
        out_specs=[whole, whole, pl.BlockSpec((d, wide), lambda i: (i, 0)), by_row, line],
        scratch_shapes=[pltpu.VMEM((tokens, wide), BF), pltpu.VMEM((tokens, wide), BF)],
        compiler_params=pltpu.CompilerParams(vmem_limit_bytes=56 * 2**20),
        cost_estimate=pl.CostEstimate(
            flops=12 * tokens * d * ff,
            bytes_accessed=16 * d * ff,
            transcendentals=tokens * ff,
        ),
        name="feed_forward",
    )(x, cot, up_weight, down_weight, up_bias)


KEYS = 256


def shipped(upper_index, ring, tiles):
    more = upper_index + 2
    return (tiles * (2 * upper_index + 1 - ring) + more) // (2 * more)


class Exchange:
    def __init__(self, index, order, array, out, acc, recv, first, wide, sems):
        self.index, self.order, self.sems = index, order, sems
        self.array, self.out, self.acc, self.recv = array, out, acc, recv
        self.columns = pl.ds(first, wide)
        self.rows = array.shape[0]
        self.halvings = halvings_of(self.rows, len(order))
        self.waits = len(order)

    def size(self, s):
        return self.rows >> min(s, self.halvings)

    def base(self, s):
        return sum(self.size(t + 1) for t in range(s))

    def start(self, s, first=1):
        at = 0
        for t in range(first, min(s, self.halvings)):
            at = at + side_of(self.order[t]) * self.size(t + 1)
        return at

    def copy(self, k):
        bit = self.order[k]
        size = self.size(k + 1)
        other = self.start(k) + ((1 - side_of(bit)) * size if k < self.halvings else 0)
        rows = pl.ds(pl.multiple_of(other, size), size)
        src = (self.array if k == 0 else self.acc).at[rows, self.columns]
        dst = self.recv.at[pl.ds(self.base(k), size), self.columns]
        return pltpu.make_async_remote_copy(
            src_ref=src,
            dst_ref=dst,
            send_sem=self.sems[0].at[self.index, k],
            recv_sem=self.sems[1].at[self.index, k],
            device_id=partner_of(bit),
            device_id_type=MESH,
        )

    def fill(self):
        half = self.size(1)
        rows = pl.ds(pl.multiple_of(side_of(self.order[0]) * half, half), half)
        return pltpu.make_async_copy(
            self.array.at[rows, self.columns],
            self.acc.at[:, self.columns],
            self.sems[2].at[self.index],
        )

    def empty(self):
        size = self.size(self.halvings)
        rows = pl.ds(pl.multiple_of(self.start(self.halvings), size), size)
        return pltpu.make_async_copy(
            self.acc.at[rows, self.columns],
            self.out.at[:, self.columns],
            self.sems[3].at[self.index],
        )

    def begin(self):
        self.fill().start()
        self.copy(0).start()

    def take(self, k):
        self.copy(k).wait()
        if k == 0:
            self.fill().wait()
        size = self.size(k + 1)
        start = self.start(k + 1)
        step = next(n for n in (128, 96, 64, 48, 32, 16) if size % n == 0)
        base = self.base(k)

        def add(i, carry):
            r = pl.multiple_of(i * step, step)
            mine = pl.ds(pl.multiple_of(start + r, step), step)
            self.acc[mine, self.columns] = (
                self.acc[mine, self.columns] + self.recv[pl.ds(base + r, step), self.columns]
            )
            return carry

        lax.fori_loop(0, size // step, add, 0)
        if k == len(self.order) - 1:
            self.empty().start()
            self.empty().wait()
        if k + 1 < self.waits:
            self.copy(k + 1).start()


def owners(rows, order, dp, ring):
    halved = order[: halvings_of(rows, len(order))]
    found = []
    for segment in range(1 << len(halved)):
        place = {"dp": 0, "seq": 0}
        for t, (axis, weight) in enumerate(halved):
            place[axis] += weight * (segment >> (len(halved) - 1 - t) & 1)
        found.append(place["dp"] * ring + place["seq"])
    return found


def unpack_kernel(
    down_from, up_from, down_ref, up_ref, down_out, up_out,
    down_low, up_low, down_wide, up_wide, down_in, up_in, down_sent, up_sent,
):
    rows, wide = up_ref.shape[1:]
    piece = math.gcd(rows, up_out.shape[0])
    tall = down_ref.shape[1]
    come = [
        pltpu.make_async_copy(down_ref.at[d], down_low.at[i], down_in.at[i])
        for i, d in enumerate(down_from)
    ], [
        pltpu.make_async_copy(up_ref.at[d], up_low.at[i], up_in.at[i])
        for i, d in enumerate(up_from)
    ]
    for copy in come[0] + come[1]:
        copy.start()
    gone = []
    for i, copy in enumerate(come[0]):
        copy.wait()
        down_wide[i] = down_low[i].astype(F32)
        gone.append(
            pltpu.make_async_copy(
                down_wide.at[i], down_out.at[pl.ds(i * tall, tall), :], down_sent.at[i]
            )
        )
        gone[-1].start()
    for i, copy in enumerate(come[1]):
        copy.wait()
        up_wide[i] = up_low[i].astype(F32)
        for j in range(rows // piece):
            at = i * rows + j * piece
            gone.append(
                pltpu.make_async_copy(
                    up_wide.at[i, pl.ds(j * piece, piece)],
                    up_out.at[
                        pl.ds(at % up_out.shape[0], piece),
                        pl.ds(at // up_out.shape[0] * wide, wide),
                    ],
                    up_sent.at[i, j],
                )
            )
            gone[-1].start()
    for copy in gone:
        copy.wait()


def unpack(down_part, up_part, down_shape, up_shape, orders, dp, ring):
    down_all = lax.all_gather(down_part, ("dp", "seq"))
    up_all = lax.all_gather(up_part, ("dp", "seq"))
    wide = up_part.shape[1]
    down_from = owners(down_shape[0], orders[0], dp, ring)
    up_from = owners(up_shape[0] * up_shape[1] // wide, orders[1], dp, ring)
    anywhere = pl.BlockSpec(memory_space=pl.ANY)
    dma = pltpu.SemaphoreType.DMA
    pieces = up_part.shape[0] // math.gcd(up_part.shape[0], up_shape[0])
    size = down_shape[0] * down_shape[1]
    return pl.pallas_call(
        functools.partial(unpack_kernel, down_from, up_from),
        out_shape=[jax.ShapeDtypeStruct(down_shape, F32), jax.ShapeDtypeStruct(up_shape, F32)],
        in_specs=[anywhere] * 2,
        out_specs=[anywhere] * 2,
        scratch_shapes=[
            pltpu.VMEM((len(down_from),) + down_part.shape, BF),
            pltpu.VMEM((len(up_from),) + up_part.shape, BF),
            pltpu.VMEM((len(down_from),) + down_part.shape, F32),
            pltpu.VMEM((len(up_from),) + up_part.shape, F32),
            dma((len(down_from),)),
            dma((len(up_from),)),
            dma((len(down_from),)),
            dma((len(up_from), pieces)),
        ],
        compiler_params=pltpu.CompilerParams(vmem_limit_bytes=48 * 2**20),
        cost_estimate=pl.CostEstimate(flops=4 * size, bytes_accessed=12 * size, transcendentals=0),
        name="unpack",
    )(down_all, up_all)


def halvings_of(rows, stages):
    count = 0
    while count < stages and rows % (32 << count) == 0:
        count += 1
    return count


def exchange_rows(rows, stages):
    count = halvings_of(rows, stages)
    return sum(rows >> min(s + 1, count) for s in range(stages))


def attention_kernel(
    seqs,
    groups,
    orders,
    q_ref,
    g_ref,
    all_ref,
    down_ref,
    up_ref,
    att_ref,
    dq_ref,
    slot_ref,
    down_sum_ref,
    up_sum_ref,
    kvt_ref,
    flat_ref,
    rows_ref,
    dkv_ref,
    s_ref,
    p_ref,
    qs_ref,
    gs_ref,
    qin_ref,
    gin_ref,
    atts_ref,
    dqs_ref,
    stage_ref,
    half_ref,
    load_sem,
    own_sem,
    in_send,
    in_recv,
    out_send,
    out_recv,
    core_send,
    core_recv,
    slot_send,
    slot_recv,
    down_acc_ref,
    up_acc_ref,
    down_recv_ref,
    up_recv_ref,
    graw_ref,
    sum_send,
    sum_recv,
    fill_sem,
    empty_sem,
):
    tiles, width, rows = q_ref.shape
    ring = all_ref.shape[0]
    chips = ring // 2
    heads = width // HEAD_DIM
    lanes = heads * rows
    length = ring * rows
    me = lax.axis_index("seq")
    chip, core = me // 2, lax.rem(me, 2)
    upper = me // chips
    partner = ring - 1 - me
    count = shipped(me + (1 - upper) * (partner - me), ring, tiles)

    def to(index):
        return {"seq": index}

    barrier = pltpu.get_barrier_semaphore()

    def greet(index):
        pl.semaphore_signal(barrier, inc=1, device_id=to(index), device_id_type=MESH)

    greet(partner)
    greet(flip(me, 1))
    for m in range(1, chips):
        greet(lax.rem(me + 2 * m, ring))
    across = [bit for bit in orders[0] if bit[0] == "dp"]
    for bit in across:
        pl.semaphore_signal(
            barrier, inc=1, device_id=partner_of(bit), device_id_type=MESH
        )
    pl.semaphore_wait(barrier, chips + 1 + len(across))

    def load(s, slot):
        return pltpu.make_async_copy(
            all_ref.at[:, pl.ds(pl.multiple_of(s * 2 * HEAD_DIM, 2 * HEAD_DIM), 2 * HEAD_DIM), :],
            kvt_ref.at[slot],
            load_sem.at[slot],
        )

    load(0, 0).start()

    def place(k):
        return lax.rem(k, seqs) * groups + k // seqs

    def remote(src, dst, sems, which, k, index):
        return pltpu.make_async_remote_copy(
            src_ref=src,
            dst_ref=dst,
            send_sem=sems[0].at[which, k],
            recv_sem=sems[1].at[which, k],
            device_id=to(index),
            device_id_type=MESH,
        )

    def q_in(k):
        return remote(q_ref.at[place(k)], qin_ref.at[k], (in_send, in_recv), 0, k, partner)

    def g_in(k):
        return remote(g_ref.at[place(k)], gin_ref.at[k], (in_send, in_recv), 1, k, partner)

    def att_out(k):
        return remote(atts_ref.at[k], att_ref.at[place(k)], (out_send, out_recv), 0, k, partner)

    def dq_out(k):
        return remote(dqs_ref.at[k], dq_ref.at[place(k)], (out_send, out_recv), 1, k, partner)

    def given_of(s):
        return (count - s + seqs - 1) // seqs

    def start_in(s):
        def one(i, carry):
            q_in(i * seqs + s).start()
            g_in(i * seqs + s).start()
            return carry

        lax.fori_loop(0, upper * given_of(s), one, 0)

    start_in(0)

    sems = (sum_send, sum_recv, fill_sem, empty_sem)
    half_down, half_up = down_ref.shape[1] // 2, up_ref.shape[1] // 2
    teams = []
    for i in range(2):
        teams.append(
            [
                Exchange(
                    2 * i, orders[0], down_ref, down_sum_ref, down_acc_ref, down_recv_ref,
                    i * half_down, half_down, sems,
                ),
                Exchange(
                    2 * i + 1, orders[1], up_ref, up_sum_ref, up_acc_ref, up_recv_ref,
                    i * half_up, half_up, sems,
                ),
            ]
        )
    most_waits = [max(e.waits for e in team) for team in teams]
    acts = sorted(
        [(k + 1.5 * i, i, k) for i in range(2) for k in range(most_waits[i])]
    )
    acts = [(i, k) for _, i, k in acts]
    for team in teams:
        for e in team:
            e.begin()

    def act(number, carry):
        for n, (i, k) in enumerate(acts):
            def run(i=i, k=k):
                for e in teams[i]:
                    if k < e.waits:
                        e.take(k)

            pl.when(number == n)(run)
        return carry

    def cost_of(position):
        return position * rows // KEYS + 2

    total_cost = (tiles - upper * count) * cost_of(me) + (1 - upper) * count * cost_of(partner)

    def advance(acted, progress):
        due = jnp.minimum(progress * (len(acts) + 1) // total_cost, len(acts))
        lax.fori_loop(acted, due, act, 0)
        return jnp.maximum(acted, due)

    def core_out(s):
        return pltpu.make_async_remote_copy(
            src_ref=stage_ref.at[lax.rem(s, 2), :, 1 - core],
            dst_ref=half_ref.at[s],
            send_sem=core_send.at[s],
            recv_sem=core_recv.at[s],
            device_id=to(flip(me, 1)),
            device_id_type=MESH,
        )

    def slot_out(s, m):
        target = lax.rem(chip + m, chips)
        return pltpu.make_async_remote_copy(
            src_ref=half_ref.at[s, target],
            dst_ref=slot_ref.at[s, m],
            send_sem=slot_send.at[s, m],
            recv_sem=slot_recv.at[s, m],
            device_id=to(2 * target + core),
            device_id_type=MESH,
        )

    def slot_own(s):
        return pltpu.make_async_copy(half_ref.at[s, chip], slot_ref.at[s, 0], own_sem.at[s])

    def pass_on(s):
        core_out(s).wait()

        def add(m, carry):
            half_ref[s, m] = (
                half_ref[s, m].astype(F32) + stage_ref[lax.rem(s, 2), m, core].astype(F32)
            ).astype(BF)
            return carry

        lax.fori_loop(0, chips, add, 0)
        slot_own(s).start()
        for m in range(1, chips):
            slot_out(s, m).start()

    qs_ref[...] = jnp.zeros_like(qs_ref)
    gs_ref[...] = jnp.zeros_like(gs_ref)

    def at(b, n=1):
        return pl.ds(pl.multiple_of(b * KEYS, KEYS), n * KEYS)

    def blocks(count_blocks, body, state):
        state = lax.fori_loop(0, count_blocks // 4, lambda i, c: body(4 * i, 4, c), state)
        pairs = count_blocks // 2
        state = lax.fori_loop(
            count_blocks // 4 * 2, pairs, lambda i, c: body(2 * i, 2, c), state
        )
        return lax.fori_loop(2 * pairs, count_blocks, lambda i, c: body(i, 1, c), state)

    def spread(tile, out):
        for h in range(heads):
            tile[h * HEAD_DIM : (h + 1) * HEAD_DIM, :] = out[:, h * rows : (h + 1) * rows].astype(
                BF
            )

    def gather(tile, out):
        for h in range(heads):
            out[0:HEAD_DIM, h * rows : (h + 1) * rows] = tile[
                h * HEAD_DIM : (h + 1) * HEAD_DIM, :
            ]

    def tile(mine, t, k, position, acted, progress):
        start = position * rows
        edge = start // KEYS
        shift = lax.rem(start, KEYS)
        other = jnp.logical_not(mine)

        @pl.when(mine)
        def _():
            gather(q_ref.at[t], qs_ref)
            gather(g_ref.at[t], graw_ref)

        @pl.when(other)
        def _():
            q_in(k).wait_recv()
            g_in(k).wait_recv()
            gather(qin_ref.at[k], qs_ref)
            gather(gin_ref.at[k], graw_ref)

        s = dot(rows_ref[at(edge), :], qs_ref[...], 1, 0)
        column = lax.rem(lax.broadcasted_iota(jnp.int32, (1, lanes), 1), rows) + shift
        keep = lax.broadcasted_iota(jnp.int32, (KEYS, lanes), 0) <= column
        s = jnp.where(keep, s, -1e30)
        s_ref[at(edge), :] = s

        def top_of(s, n):
            return jnp.max(s.reshape(n * KEYS // 8, 8, lanes), axis=0)

        def scores(b, n, top):
            s = dot(rows_ref[at(b, n), :], qs_ref[...], 1, 0)
            s_ref[at(b, n), :] = s
            return jnp.maximum(top, top_of(s, n))

        top = jnp.max(blocks(edge, scores, top_of(s, 1)), axis=0, keepdims=True)

        def forward(b, n, state):
            total, out = state
            p = jnp.exp2(s_ref[at(b, n), :] - top)
            low = p.astype(BF)
            p_ref[at(b, n), :] = low
            return (
                total + jnp.sum(p.reshape(n * KEYS // 8, 8, lanes), axis=0),
                out + dot(flat_ref[HEAD_DIM : 2 * HEAD_DIM, at(b, n)], low, 1, 0),
            )

        total, out = blocks(
            edge + 1, forward, (jnp.zeros((8, lanes), F32), jnp.zeros((HEAD_DIM, lanes), F32))
        )
        inverse = 1.0 / jnp.sum(total, axis=0, keepdims=True)
        out = out * inverse
        pl.when(mine)(lambda: spread(att_ref.at[t], out))

        @pl.when(other)
        def _():
            spread(atts_ref.at[k], out)
            att_out(k).start()

        acted = advance(acted, progress + (edge + 2) // 2)
        g = graw_ref[...]
        scaled = (g.astype(F32) * inverse).astype(BF)
        gs_ref[HEAD_DIM : 2 * HEAD_DIM, :] = scaled
        delta = jnp.sum(scaled.astype(F32) * out, axis=0, keepdims=True)

        def backward(b, n, dq):
            p = p_ref[at(b, n), :]
            dp = dot(rows_ref[at(b, n), :], gs_ref[...], 1, 0)
            ds = (p.astype(F32) * (dp - delta)).astype(BF)
            dkv_ref[at(b, n), :] += dot(p, gs_ref[...], 1, 1) + dot(ds, qs_ref[...], 1, 1)
            return dq + dot(flat_ref[0:HEAD_DIM, at(b, n)], ds, 1, 0)

        dq = blocks(edge + 1, backward, jnp.zeros((HEAD_DIM, lanes), F32))
        dq = dq * (HEAD_DIM**-0.5)
        pl.when(mine)(lambda: spread(dq_ref.at[t], dq))

        @pl.when(other)
        def _():
            spread(dqs_ref.at[k], dq)
            dq_out(k).start()

        progress = progress + edge + 2
        return advance(acted, progress), progress

    per_block = KEYS // rows

    def sequence(s, state):
        slot = lax.rem(s, 2)
        load(s, slot).wait()
        pl.when(s + 1 < seqs)(lambda: load(s + 1, 1 - slot).start())
        dkv_ref[...] = jnp.zeros_like(dkv_ref)

        def turn(b, c):
            wide = jnp.concatenate(
                [kvt_ref[slot, b * per_block + i] for i in range(per_block)], axis=1
            )
            flat_ref[:, at(b)] = wide
            rows_ref[at(b), :] = wide.T
            return c

        lax.fori_loop(0, length // KEYS, turn, 0)
        given = given_of(s)
        own = groups - upper * given
        taken = (1 - upper) * given
        later = jnp.minimum(s, 1)

        def work(u, state):
            acted, progress = state
            v = u - taken * later
            mine = (v >= 0) & (v < own)
            t = s * groups + upper * given + jnp.clip(v, 0, own - 1)
            k = jnp.clip(u - own * (1 - later), 0, jnp.maximum(taken - 1, 0)) * seqs + s
            position = jnp.where(mine, me, partner)
            state = tile(mine, t, k, position, acted, progress)
            pl.when((u == 0) & (s > 0))(lambda: pass_on(s - 1))
            pl.when((u == 0) & (s + 1 < seqs))(lambda: start_in(s + 1))
            return state

        state = lax.fori_loop(0, own + taken, work, state)
        stage_ref[slot] = dkv_ref[...].reshape(chips, 2, rows, 2 * HEAD_DIM).astype(BF)
        core_out(s).start()
        return state

    acted, _ = lax.fori_loop(0, seqs, sequence, (jnp.int32(0), jnp.int32(0)))
    pass_on(seqs - 1)
    lax.fori_loop(acted, len(acts), act, 0)

    def end_given(k, c):
        q_in(k).wait_send()
        g_in(k).wait_send()
        att_out(k).wait_recv()
        dq_out(k).wait_recv()
        return c

    def end_taken(k, c):
        att_out(k).wait_send()
        dq_out(k).wait_send()
        return c

    lax.fori_loop(0, count * upper, end_given, 0)
    lax.fori_loop(0, count * (1 - upper), end_taken, 0)

    def end(s, c):
        slot_own(s).wait()
        for m in range(1, chips):
            slot_out(s, m).wait()
        return c

    lax.fori_loop(0, seqs, end, 0)


def attention(q, g, kv_all, down, up, seqs, dp):
    tiles, width, rows = q.shape
    ring = kv_all.shape[0]
    chips = ring // 2
    length = ring * rows
    lanes = width // HEAD_DIM * rows
    most = max(shipped(i, ring, tiles) for i in range(chips, ring))
    vmem = pl.BlockSpec(memory_space=pltpu.VMEM)
    anywhere = pl.BlockSpec(memory_space=pl.ANY)
    pair = 2 * HEAD_DIM
    dma = pltpu.SemaphoreType.DMA
    orders = bit_orders(dp, ring)
    stages = len(orders[0])
    return pl.pallas_call(
        functools.partial(attention_kernel, seqs, tiles // seqs, orders),
        out_shape=[
            jax.ShapeDtypeStruct(q.shape, BF),
            jax.ShapeDtypeStruct(q.shape, BF),
            jax.ShapeDtypeStruct((seqs, chips, rows, pair), BF),
            *(
                jax.ShapeDtypeStruct((a.shape[0] >> halvings_of(a.shape[0], stages), a.shape[1]), BF)
                for a in (down, up)
            ),
        ],
        in_specs=[vmem, vmem, anywhere, anywhere, anywhere],
        out_specs=[vmem, vmem, anywhere, anywhere, anywhere],
        scratch_shapes=[
            pltpu.VMEM((2, ring, pair, rows), BF),
            pltpu.VMEM((pair, length), BF),
            pltpu.VMEM((length, pair), BF),
            pltpu.VMEM((length, pair), F32),
            pltpu.VMEM((length, lanes), F32),
            pltpu.VMEM((length, lanes), BF),
            pltpu.VMEM((pair, lanes), BF),
            pltpu.VMEM((pair, lanes), BF),
            pltpu.VMEM((most, width, rows), BF),
            pltpu.VMEM((most, width, rows), BF),
            pltpu.VMEM((most, width, rows), BF),
            pltpu.VMEM((most, width, rows), BF),
            pltpu.VMEM((2, chips, 2, rows, pair), BF),
            pltpu.VMEM((seqs, chips, rows, pair), BF),
            dma((2,)),
            dma((seqs,)),
            dma((2, most)),
            dma((2, most)),
            dma((2, most)),
            dma((2, most)),
            dma((seqs,)),
            dma((seqs,)),
            dma((seqs, chips)),
            dma((seqs, chips)),
            pltpu.VMEM((down.shape[0] // 2, down.shape[1]), BF),
            pltpu.VMEM((up.shape[0] // 2, up.shape[1]), BF),
            pltpu.VMEM((exchange_rows(down.shape[0], stages), down.shape[1]), BF),
            pltpu.VMEM((exchange_rows(up.shape[0], stages), up.shape[1]), BF),
            pltpu.VMEM((HEAD_DIM, lanes), BF),
            dma((4, stages)),
            dma((4, stages)),
            dma((4,)),
            dma((4,)),
        ],
        compiler_params=pltpu.CompilerParams(
            collective_id=2, has_side_effects=True, vmem_limit_bytes=60 * 2**20
        ),
        cost_estimate=pl.CostEstimate(
            flops=12 * tiles * rows * width * length * 4,
            bytes_accessed=8 * q.size,
            transcendentals=tiles * lanes * length // 2,
        ),
        name="attention",
    )(q, g, kv_all, down, up)


def bit_orders(dp, ring):
    seq_bits = [("seq", 1 << b) for b in range(ring.bit_length() - 1)]
    dp_bits = [("dp", 1 << b) for b in range(dp.bit_length() - 1)]
    far = seq_bits[2:]
    return (seq_bits[:2] + dp_bits + far, seq_bits[:1] + dp_bits + seq_bits[1:2] + far)

def side_of(bit):
    axis, weight = bit
    return lax.rem(lax.axis_index(axis) // weight, 2)

def partner_of(bit):
    axis, weight = bit
    me = lax.axis_index(axis)
    return {axis: me + weight - 2 * weight * side_of(bit)}

def add_rows(dst, a, b, dst_at, a_at, rows, step):
    def body(i, carry):
        r = pl.multiple_of(i * step, step)
        dst[pl.ds(dst_at + r, step), :] = a[pl.ds(a_at + r, step), :] + b[pl.ds(r, step), :]
        return carry
    lax.fori_loop(0, rows // step, body, 0)

def sum_kernel(orders, x_ref, out_ref, *scratch):
    parts = len(orders)
    stages = len(orders[0])
    rows, cols = x_ref.shape
    wide = cols // parts
    acc, recv, sems = scratch[:parts], scratch[parts:2*parts], scratch[2*parts:]
    send_sem, recv_sem = sems
    barrier = pltpu.get_barrier_semaphore()
    for bit in orders[0]:
        pl.semaphore_signal(barrier, inc=1, device_id=partner_of(bit), device_id_type=MESH)
    pl.semaphore_wait(barrier, stages)
    def copy(p, s, src, dst, bit):
        return pltpu.make_async_remote_copy(src_ref=src, dst_ref=dst, send_sem=send_sem.at[p, s], recv_sem=recv_sem.at[p, s],
            device_id=partner_of(bit), device_id_type=MESH)
    columns = [pl.ds(p * wide, wide) for p in range(parts)]
    start = [0] * parts
    whole = [0] * parts
    live = {}
    base = [0]
    for s in range(stages): base.append(base[-1] + rows // 2 ** min(s + 1, stages - 1))
    def launch(p, s):
        bit = orders[p][s]
        if s < stages - 1:
            half = rows // 2 ** (s + 1)
            other = pl.multiple_of(start[p] + (1 - side_of(bit)) * half, half)
            src = x_ref.at[pl.ds(other, half), columns[p]] if s == 0 else acc[p].at[pl.ds(other, half), :]
        else:
            half = rows // 2 ** s
            src = acc[p].at[pl.ds(pl.multiple_of(start[p], half), half), :]
        live[p] = copy(p, s, src, recv[p].at[pl.ds(base[s], half), :], bit)
        live[p].start()
    for p in range(parts): launch(p, 0)
    for s in range(stages):
        for p in range(parts):
            bit = orders[p][s]
            live[p].wait()
            half = rows // 2 ** min(s + 1, stages - 1)
            step = 16 if half % 64 else 64
            got = recv[p].at[pl.ds(base[s], half), :]
            if s == 0:
                mine = side_of(bit) * half
                whole[p] = mine
                add_rows(acc[p], x_ref.at[:, columns[p]], got, 0, pl.multiple_of(mine, half), half, step)
                start[p] = 0
            elif s < stages - 1:
                mine = pl.multiple_of(start[p] + side_of(bit) * half, half)
                add_rows(acc[p], acc[p], got, mine, mine, half, step)
                whole[p] = whole[p] + side_of(bit) * half
                start[p] = start[p] + side_of(bit) * half
            else:
                at = pl.multiple_of(start[p], half)
                add_rows(out_ref.at[:, columns[p]], acc[p], got, pl.multiple_of(whole[p], half), at, half, step)
            if s < stages - 1: launch(p, s + 1)
    def spread(p, s):
        bit = orders[p][s]
        half = rows // 2 ** (s + 1)
        src = out_ref.at[pl.ds(pl.multiple_of(whole[p], half), half), columns[p]]
        live[p] = copy(p, 2 * stages - 2 - s, src, src, bit)
        live[p].start()
    for p in range(parts): spread(p, stages - 2)
    for s in range(stages - 2, -1, -1):
        for p in range(parts):
            live[p].wait()
            whole[p] = whole[p] - side_of(orders[p][s]) * (rows // 2 ** (s + 1))
            if s: spread(p, s - 1)

def total_of(x, dp, ring, collective_id):
    orders = bit_orders(dp, ring)
    rows, cols = x.shape
    parts, stages = len(orders), len(orders[0])
    wide = cols // parts
    got = sum(rows // 2 ** min(s + 1, stages - 1) for s in range(stages))
    whole = pl.BlockSpec(memory_space=pltpu.VMEM)
    return pl.pallas_call(functools.partial(sum_kernel, orders),
        out_shape=jax.ShapeDtypeStruct(x.shape, BF), in_specs=[whole], out_specs=whole,
        scratch_shapes=[pltpu.VMEM((rows // 2, wide), BF)] * parts + [pltpu.VMEM((got, wide), BF)] * parts
        + [pltpu.SemaphoreType.DMA((parts, 2 * stages - 1))] * 2,
        compiler_params=pltpu.CompilerParams(collective_id=collective_id, has_side_effects=True, vmem_limit_bytes=56*2**20),
        name="total")(x)


def local(
    hidden_in,
    positions,
    ln1_gain,
    ln1_bias,
    ln2_gain,
    ln2_bias,
    query_projection,
    query_bias,
    shared_key_weight,
    shared_key_bias,
    shared_value_weight,
    shared_value_bias,
    output_weight,
    output_bias,
    up_weight,
    up_bias,
    down_weight,
    down_bias,
    cotangent,
):
    seq_count, local_len = hidden_in.shape[0], hidden_in.shape[1]
    ring = lax.axis_size("seq")
    groups = ring // seq_count
    per_group = HEADS // groups
    width = per_group * HEAD_DIM
    hidden = hidden_in.astype(F32)
    cosine, sine = angles_of(positions)
    normed_a, pull_a = jax.vjp(layer_norm, hidden, ln1_gain, ln1_bias)
    normed_m, pull_m = jax.vjp(layer_norm, hidden, ln2_gain, ln2_bias)
    normed_a = normed_a.astype(BF)
    normed_m = normed_m.astype(BF)

    tokens = seq_count * local_len
    kv_weight = jnp.concatenate([shared_key_weight, shared_value_weight], axis=1)
    kv_bias = jnp.concatenate([shared_key_bias, shared_value_bias])
    kv_pre = jnp.einsum("stc,cw->swt", normed_a, kv_weight, preferred_element_type=F32)
    kv_pre = kv_pre + kv_bias[:, None]
    kv_low = jnp.concatenate(
        [rotary_rows(kv_pre[:, :HEAD_DIM], cosine, sine), kv_pre[:, HEAD_DIM:]], axis=1
    ).astype(BF)
    kv_all = lax.all_gather(kv_low.reshape(-1, local_len), "seq")
    query_pre = jnp.einsum("stc,cw->swt", normed_a, query_projection, preferred_element_type=F32)
    query_pre = (query_pre + query_bias[:, None]).reshape(seq_count, HEADS, HEAD_DIM, local_len)
    query_low = (rotary_rows(query_pre, cosine[:, None], sine[:, None]) * (LOG2E / 8.0)).astype(BF)
    query_tiles = query_low.reshape(-1, width, local_len)
    grad_attended = jnp.einsum(
        "stc,wc->swt", cotangent, output_weight, preferred_element_type=F32
    ).astype(BF)
    grad_tiles = grad_attended.reshape(-1, width, local_len)

    feedforward, grad_normed_m, grad_w_up, grad_w_down, grad_b_up = feed_forward(
        normed_m.reshape(tokens, D),
        cotangent.reshape(tokens, D),
        up_weight,
        up_bias[None],
        down_weight,
    )
    feedforward = feedforward.reshape(hidden.shape)
    grad_normed_m = grad_normed_m.reshape(hidden.shape)
    grad_b_up = grad_b_up[0]
    grad_b_down = jnp.sum(cotangent.astype(F32), axis=(0, 1))
    query_tiles, grad_tiles, kv_all, grad_w_up, grad_w_down = lax.optimization_barrier(
        (query_tiles, grad_tiles, kv_all, grad_w_up, grad_w_down)
    )
    dp = lax.axis_size("dp")
    orders = bit_orders(dp, ring)
    out, dq, dkv, part_down, part_up = attention(
        query_tiles, grad_tiles, kv_all, grad_w_down, grad_w_up, seq_count, dp
    )
    grad_w_down, grad_w_up = unpack(
        part_down, part_up, down_weight.shape, up_weight.shape, orders, dp, ring
    )
    attended = out.reshape(seq_count, D, local_len)
    query_back = dq.reshape(seq_count, HEADS, HEAD_DIM, local_len)
    kv_grad = jnp.sum(dkv.astype(F32), axis=1)
    kv_scale = jnp.concatenate([jnp.full((HEAD_DIM,), 1.0 / LOG2E), jnp.ones((HEAD_DIM,))])
    kv_grad = (kv_grad * kv_scale).astype(BF).astype(F32).transpose(0, 2, 1)

    attention_out = jnp.einsum(
        "swt,wc->stc", attended, output_weight, preferred_element_type=F32
    )
    layer_out = hidden + attention_out + feedforward + (output_bias + down_bias)
    grad_w_out = jnp.einsum("swt,stc->wc", attended, cotangent, preferred_element_type=F32)

    kv_raw = jnp.concatenate(
        [rotary_rows(kv_grad[:, :HEAD_DIM], cosine, -sine), kv_grad[:, HEAD_DIM:]], axis=1
    ).astype(BF)
    query_raw = (
        rotary_rows(query_back.astype(F32), cosine[:, None], -sine[:, None])
        .astype(BF)
        .reshape(seq_count, D, local_len)
    )
    raw = jnp.concatenate([query_raw, kv_raw], axis=1)
    weight = jnp.concatenate([query_projection, kv_weight], axis=1)
    grad_w_qkv = jnp.einsum("stc,swt->cw", normed_a, raw, preferred_element_type=F32)
    grad_b_qkv = jnp.sum(raw.astype(F32), axis=(0, 2))
    grad_normed_a = jnp.einsum("swt,cw->stc", raw, weight, preferred_element_type=F32)
    grad_hidden_a, grad_ln1_gain, grad_ln1_bias = pull_a(grad_normed_a)
    grad_hidden_m, grad_ln2_gain, grad_ln2_bias = pull_m(grad_normed_m)
    input_grad = cotangent.astype(F32) + grad_hidden_a + grad_hidden_m

    vectors = jnp.concatenate(
        [
            grad_ln1_gain,
            grad_ln1_bias,
            grad_ln2_gain,
            grad_ln2_bias,
            grad_b_qkv,
            grad_b_up,
            grad_b_down,
        ]
    )
    dp = lax.axis_size("dp")
    unit = 16 * dp * ring // 2
    square = D * (2 * D + 2 * HEAD_DIM)
    filled = square // D + -(-vectors.size // D)
    padded = -(-filled // unit) * unit
    rest = jnp.concatenate(
        [
            grad_w_qkv[:, :D],
            grad_w_out,
            grad_w_qkv[:, D:].T,
            jnp.pad(vectors, (0, (padded * D - square) - vectors.size)).reshape(-1, D),
        ],
        axis=0,
    ).astype(BF)
    rest = total_of(rest, dp, ring, 3)
    rest = rest.astype(F32)
    vectors = rest[square // D :].reshape(-1)
    rest_kv = rest[2 * D : 2 * D + 2 * HEAD_DIM]
    qkv = D + 2 * HEAD_DIM
    ff = up_weight.shape[1]
    b_qkv = vectors[4 * D : 4 * D + qkv]
    b_up = vectors[4 * D + qkv : 4 * D + qkv + ff]
    b_down = vectors[4 * D + qkv + ff : 4 * D + qkv + ff + D]
    return (
        layer_out,
        input_grad,
        vectors[:D],
        vectors[D : 2 * D],
        vectors[2 * D : 3 * D],
        vectors[3 * D : 4 * D],
        rest[:D],
        b_qkv[:D],
        rest_kv[:HEAD_DIM].T,
        b_qkv[D : D + HEAD_DIM],
        rest_kv[HEAD_DIM:].T,
        b_qkv[D + HEAD_DIM :],
        rest[D : 2 * D],
        b_down,
        grad_w_up,
        b_up,
        grad_w_down,
        b_down,
    )


def solution(mesh):
    rows = P("dp", "seq", None)
    placed = (rows, P("dp", "seq")) + (P(),) * 16 + (rows,)
    return jax.shard_map(
        local,
        mesh=mesh,
        in_specs=placed,
        out_specs=(rows, rows) + (P(),) * 16,
        check_vma=False,
    )
```

```python
import functools
import math

import jax
import jax.numpy as jnp
from jax import lax
from jax.experimental import pallas as pl
from jax.experimental.pallas import tpu as pltpu
from jax.sharding import PartitionSpec as P

D = 768
HEADS = 12
HEAD_DIM = 64
ROT_DIMS = 16
BF = jnp.bfloat16
F32 = jnp.float32
LOG2E = math.log2(math.e)


def layer_norm(values, gain, bias):
    center = values - jnp.mean(values, axis=-1, keepdims=True)
    spread = jnp.mean(center * center, axis=-1, keepdims=True)
    return center * lax.rsqrt(spread + 1e-05) * gain + bias


def rotary_rows(values, cosine, sine):
    half = cosine.shape[-2]
    first, second = values[..., :half, :], values[..., half : 2 * half, :]
    return jnp.concatenate(
        [first * cosine - second * sine, second * cosine + first * sine, values[..., 2 * half :, :]],
        axis=-2,
    )


def angles_of(positions):
    half = ROT_DIMS // 2
    frequency = jnp.exp(
        jnp.arange(half).astype(F32) * (-2.0 * math.log(10000.0) / ROT_DIMS)
    )
    angle = positions.astype(F32)[:, None, :] * frequency[None, :, None]
    return jnp.cos(angle), jnp.sin(angle)


MESH = pl.DeviceIdType.MESH


def dot(a, b, ca, cb):
    return lax.dot_general(a, b, (((ca,), (cb,)), ((), ())), preferred_element_type=F32)


def flip(index, weight):
    return index + weight - 2 * weight * lax.rem(index // weight, 2)


def gelu_parts(u):
    e = jnp.exp(u * u * -0.5)
    t = 1.0 / (1.0 + (0.3275911 / math.sqrt(2.0)) * jnp.abs(u))
    poly = t * (
        0.5 * 0.254829592
        + t
        * (
            0.5 * -0.284496736
            + t * (0.5 * 1.421413741 + t * (0.5 * -1.453152027 + t * (0.5 * 1.061405429)))
        )
    )
    tail = poly * e
    return jnp.where(u >= 0, 1.0 - tail, tail), e * (1.0 / math.sqrt(2.0 * math.pi))


def feed_kernel(
    x_ref,
    c_ref,
    up_ref,
    down_ref,
    bias_ref,
    ff_ref,
    gx_ref,
    gup_ref,
    gdown_ref,
    gbias_ref,
    act_ref,
    grad_ref,
):
    tokens = x_ref.shape[0]
    bias = bias_ref[...]
    sub = min(256, tokens)
    for r in range(0, tokens, sub):
        u = dot(x_ref[r : r + sub, :], up_ref[...], 1, 0) + bias
        share, density = gelu_parts(u)
        act_ref[r : r + sub, :] = (u * share).astype(BF)
        da = dot(c_ref[r : r + sub, :], down_ref[...], 1, 1)
        grad_ref[r : r + sub, :] = (da * (share + u * density)).astype(BF)

    @pl.when(pl.program_id(0) == 0)
    def _():
        ff_ref[...] = jnp.zeros_like(ff_ref)
        gx_ref[...] = jnp.zeros_like(gx_ref)

    act, grad = act_ref[...], grad_ref[...]
    ff_ref[...] += dot(act, down_ref[...], 1, 0)
    gx_ref[...] += dot(grad, up_ref[...], 1, 1)
    gdown_ref[...] = dot(act, c_ref[...], 0, 0).astype(BF)
    gup_ref[...] = dot(x_ref[...], grad, 0, 0).astype(BF)
    gbias_ref[...] = jnp.sum(grad.astype(F32), axis=0, keepdims=True)


def feed_forward(x, cot, up_weight, up_bias, down_weight):
    tokens, d = x.shape
    ff = up_weight.shape[1]
    wide = d
    steps = ff // wide
    whole = pl.BlockSpec((tokens, d), lambda i: (0, 0))
    by_column = pl.BlockSpec((d, wide), lambda i: (0, i))
    by_row = pl.BlockSpec((wide, d), lambda i: (i, 0))
    line = pl.BlockSpec((1, wide), lambda i: (0, i))
    return pl.pallas_call(
        feed_kernel,
        grid=(steps,),
        out_shape=[
            jax.ShapeDtypeStruct((tokens, d), F32),
            jax.ShapeDtypeStruct((tokens, d), F32),
            jax.ShapeDtypeStruct((ff, d), BF),
            jax.ShapeDtypeStruct((ff, d), BF),
            jax.ShapeDtypeStruct((1, ff), F32),
        ],
        in_specs=[whole, whole, by_column, by_row, line],
        out_specs=[whole, whole, pl.BlockSpec((d, wide), lambda i: (i, 0)), by_row, line],
        scratch_shapes=[pltpu.VMEM((tokens, wide), BF), pltpu.VMEM((tokens, wide), BF)],
        compiler_params=pltpu.CompilerParams(vmem_limit_bytes=56 * 2**20),
        cost_estimate=pl.CostEstimate(
            flops=12 * tokens * d * ff,
            bytes_accessed=16 * d * ff,
            transcendentals=tokens * ff,
        ),
        name="feed_forward",
    )(x, cot, up_weight, down_weight, up_bias)


KEYS = 256


def shipped(upper_index, ring, tiles):
    more = upper_index + 2
    return (tiles * (2 * upper_index + 1 - ring) + more) // (2 * more)


class Exchange:
    def __init__(self, index, order, array, out, acc, recv, first, wide, sems):
        self.index, self.order, self.sems = index, order, sems
        self.array, self.out, self.acc, self.recv = array, out, acc, recv
        self.columns = pl.ds(first, wide)
        self.rows = array.shape[0]
        self.halvings = halvings_of(self.rows, len(order))
        self.waits = len(order)

    def size(self, s):
        return self.rows >> min(s, self.halvings)

    def base(self, s):
        return sum(self.size(t + 1) for t in range(s))

    def start(self, s, first=1):
        at = 0
        for t in range(first, min(s, self.halvings)):
            at = at + side_of(self.order[t]) * self.size(t + 1)
        return at

    def copy(self, k):
        bit = self.order[k]
        size = self.size(k + 1)
        other = self.start(k) + ((1 - side_of(bit)) * size if k < self.halvings else 0)
        rows = pl.ds(pl.multiple_of(other, size), size)
        src = (self.array if k == 0 else self.acc).at[rows, self.columns]
        dst = self.recv.at[pl.ds(self.base(k), size), self.columns]
        return pltpu.make_async_remote_copy(
            src_ref=src,
            dst_ref=dst,
            send_sem=self.sems[0].at[self.index, k],
            recv_sem=self.sems[1].at[self.index, k],
            device_id=partner_of(bit),
            device_id_type=MESH,
        )

    def fill(self):
        half = self.size(1)
        rows = pl.ds(pl.multiple_of(side_of(self.order[0]) * half, half), half)
        return pltpu.make_async_copy(
            self.array.at[rows, self.columns],
            self.acc.at[:, self.columns],
            self.sems[2].at[self.index],
        )

    def empty(self):
        size = self.size(self.halvings)
        rows = pl.ds(pl.multiple_of(self.start(self.halvings), size), size)
        return pltpu.make_async_copy(
            self.acc.at[rows, self.columns],
            self.out.at[:, self.columns],
            self.sems[3].at[self.index],
        )

    def begin(self):
        self.fill().start()
        self.copy(0).start()

    def take(self, k):
        self.copy(k).wait()
        if k == 0:
            self.fill().wait()
        size = self.size(k + 1)
        start = self.start(k + 1)
        step = next(n for n in (128, 96, 64, 48, 32, 16) if size % n == 0)
        base = self.base(k)

        def add(i, carry):
            r = pl.multiple_of(i * step, step)
            mine = pl.ds(pl.multiple_of(start + r, step), step)
            self.acc[mine, self.columns] = (
                self.acc[mine, self.columns] + self.recv[pl.ds(base + r, step), self.columns]
            )
            return carry

        lax.fori_loop(0, size // step, add, 0)
        if k == len(self.order) - 1:
            self.empty().start()
            self.empty().wait()
        if k + 1 < self.waits:
            self.copy(k + 1).start()


def owners(rows, order, dp, ring):
    halved = order[: halvings_of(rows, len(order))]
    found = []
    for segment in range(1 << len(halved)):
        place = {"dp": 0, "seq": 0}
        for t, (axis, weight) in enumerate(halved):
            place[axis] += weight * (segment >> (len(halved) - 1 - t) & 1)
        found.append(place["dp"] * ring + place["seq"])
    return found


def unpack_kernel(froms, all_ref, down_out, up_out, low, wide, come_sem, sent_sem):
    count = len(froms[0])
    tall, across = all_ref.shape[2:]
    come = [
        [
            pltpu.make_async_copy(all_ref.at[d, a], low.at[a, i], come_sem.at[a, i])
            for i, d in enumerate(froms[a])
        ]
        for a in range(2)
    ]
    for copy in come[0] + come[1]:
        copy.start()
    gone = []
    for a in range(2):
        for i in range(count):
            come[a][i].wait()
            wide[a, i] = low[a, i].astype(F32)
            at = i * tall
            if a == 0:
                to = down_out.at[pl.ds(at, tall), :]
            else:
                block = at // across
                to = up_out.at[pl.ds(at - block * across, tall), pl.ds(block * across, across)]
            gone.append(pltpu.make_async_copy(wide.at[a, i], to, sent_sem.at[a, i]))
            gone[-1].start()
    for copy in gone:
        copy.wait()


def unpack(parts, down_shape, up_shape, orders, dp, ring):
    everyone = lax.all_gather(parts, ("dp", "seq"))
    froms = [owners(down_shape[0], order, dp, ring) for order in orders]
    anywhere = pl.BlockSpec(memory_space=pl.ANY)
    dma = pltpu.SemaphoreType.DMA
    size = down_shape[0] * down_shape[1]
    count = len(froms[0])
    return pl.pallas_call(
        functools.partial(unpack_kernel, froms),
        out_shape=[jax.ShapeDtypeStruct(down_shape, F32), jax.ShapeDtypeStruct(up_shape, F32)],
        in_specs=[anywhere],
        out_specs=[anywhere] * 2,
        scratch_shapes=[
            pltpu.VMEM((2, count) + parts.shape[1:], BF),
            pltpu.VMEM((2, count) + parts.shape[1:], F32),
            dma((2, count)),
            dma((2, count)),
        ],
        compiler_params=pltpu.CompilerParams(vmem_limit_bytes=48 * 2**20),
        cost_estimate=pl.CostEstimate(flops=4 * size, bytes_accessed=12 * size, transcendentals=0),
        name="unpack",
    )(everyone)


def halvings_of(rows, stages):
    count = 0
    while count < stages and rows % (32 << count) == 0:
        count += 1
    return count


def exchange_rows(rows, stages):
    count = halvings_of(rows, stages)
    return sum(rows >> min(s + 1, count) for s in range(stages))


def attention_kernel(
    seqs,
    groups,
    orders,
    q_ref,
    g_ref,
    all_ref,
    down_ref,
    up_ref,
    att_ref,
    dq_ref,
    slot_ref,
    sum_ref,
    kvt_ref,
    flat_ref,
    rows_ref,
    dkv_ref,
    s_ref,
    p_ref,
    qs_ref,
    gs_ref,
    qin_ref,
    gin_ref,
    atts_ref,
    dqs_ref,
    stage_ref,
    half_ref,
    load_sem,
    own_sem,
    in_send,
    in_recv,
    out_send,
    out_recv,
    core_send,
    core_recv,
    slot_send,
    slot_recv,
    down_acc_ref,
    up_acc_ref,
    down_recv_ref,
    up_recv_ref,
    graw_ref,
    sum_send,
    sum_recv,
    fill_sem,
    empty_sem,
):
    tiles, width, rows = q_ref.shape
    ring = all_ref.shape[0]
    chips = ring // 2
    heads = width // HEAD_DIM
    lanes = heads * rows
    length = ring * rows
    me = lax.axis_index("seq")
    chip, core = me // 2, lax.rem(me, 2)
    upper = me // chips
    partner = ring - 1 - me
    count = shipped(me + (1 - upper) * (partner - me), ring, tiles)

    def to(index):
        return {"seq": index}

    barrier = pltpu.get_barrier_semaphore()

    def greet(index):
        pl.semaphore_signal(barrier, inc=1, device_id=to(index), device_id_type=MESH)

    greet(partner)
    greet(flip(me, 1))
    for m in range(1, chips):
        greet(lax.rem(me + 2 * m, ring))
    across = [bit for bit in orders[0] if bit[0] == "dp"]
    for bit in across:
        pl.semaphore_signal(
            barrier, inc=1, device_id=partner_of(bit), device_id_type=MESH
        )
    pl.semaphore_wait(barrier, chips + 1 + len(across))

    def load(s, slot):
        return pltpu.make_async_copy(
            all_ref.at[:, pl.ds(pl.multiple_of(s * 2 * HEAD_DIM, 2 * HEAD_DIM), 2 * HEAD_DIM), :],
            kvt_ref.at[slot],
            load_sem.at[slot],
        )

    load(0, 0).start()

    def place(k):
        return lax.rem(k, seqs) * groups + k // seqs

    def remote(src, dst, sems, which, k, index):
        return pltpu.make_async_remote_copy(
            src_ref=src,
            dst_ref=dst,
            send_sem=sems[0].at[which, k],
            recv_sem=sems[1].at[which, k],
            device_id=to(index),
            device_id_type=MESH,
        )

    def q_in(k):
        return remote(q_ref.at[place(k)], qin_ref.at[k], (in_send, in_recv), 0, k, partner)

    def g_in(k):
        return remote(g_ref.at[place(k)], gin_ref.at[k], (in_send, in_recv), 1, k, partner)

    def att_out(k):
        return remote(atts_ref.at[k], att_ref.at[place(k)], (out_send, out_recv), 0, k, partner)

    def dq_out(k):
        return remote(dqs_ref.at[k], dq_ref.at[place(k)], (out_send, out_recv), 1, k, partner)

    def given_of(s):
        return (count - s + seqs - 1) // seqs

    def start_in(s):
        def one(i, carry):
            q_in(i * seqs + s).start()
            g_in(i * seqs + s).start()
            return carry

        lax.fori_loop(0, upper * given_of(s), one, 0)

    start_in(0)

    sems = (sum_send, sum_recv, fill_sem, empty_sem)
    half_down, half_up = down_ref.shape[1] // 2, up_ref.shape[1] // 2
    teams = []
    for i in range(2):
        teams.append(
            [
                Exchange(
                    2 * i, orders[0], down_ref, sum_ref.at[0], down_acc_ref, down_recv_ref,
                    i * half_down, half_down, sems,
                ),
                Exchange(
                    2 * i + 1, orders[1], up_ref, sum_ref.at[1], up_acc_ref, up_recv_ref,
                    i * half_up, half_up, sems,
                ),
            ]
        )
    most_waits = [max(e.waits for e in team) for team in teams]
    acts = sorted(
        [(k + 1.5 * i, i, k) for i in range(2) for k in range(most_waits[i])]
    )
    acts = [(i, k) for _, i, k in acts]
    for team in teams:
        for e in team:
            e.begin()

    def act(number, carry):
        for n, (i, k) in enumerate(acts):
            def run(i=i, k=k):
                for e in teams[i]:
                    if k < e.waits:
                        e.take(k)

            pl.when(number == n)(run)
        return carry

    def cost_of(position):
        return position * rows // KEYS + 2

    total_cost = (tiles - upper * count) * cost_of(me) + (1 - upper) * count * cost_of(partner)

    def advance(acted, progress):
        due = jnp.minimum(progress * (len(acts) + 1) // total_cost, len(acts))
        lax.fori_loop(acted, due, act, 0)
        return jnp.maximum(acted, due)

    def core_out(s):
        return pltpu.make_async_remote_copy(
            src_ref=stage_ref.at[lax.rem(s, 2), :, 1 - core],
            dst_ref=half_ref.at[s],
            send_sem=core_send.at[s],
            recv_sem=core_recv.at[s],
            device_id=to(flip(me, 1)),
            device_id_type=MESH,
        )

    def slot_out(s, m):
        target = lax.rem(chip + m, chips)
        return pltpu.make_async_remote_copy(
            src_ref=half_ref.at[s, target],
            dst_ref=slot_ref.at[s, m],
            send_sem=slot_send.at[s, m],
            recv_sem=slot_recv.at[s, m],
            device_id=to(2 * target + core),
            device_id_type=MESH,
        )

    def slot_own(s):
        return pltpu.make_async_copy(half_ref.at[s, chip], slot_ref.at[s, 0], own_sem.at[s])

    def pass_on(s):
        core_out(s).wait()

        def add(m, carry):
            half_ref[s, m] = (
                half_ref[s, m].astype(F32) + stage_ref[lax.rem(s, 2), m, core].astype(F32)
            ).astype(BF)
            return carry

        lax.fori_loop(0, chips, add, 0)
        slot_own(s).start()
        for m in range(1, chips):
            slot_out(s, m).start()

    qs_ref[...] = jnp.zeros_like(qs_ref)
    gs_ref[...] = jnp.zeros_like(gs_ref)

    def at(b, n=1):
        return pl.ds(pl.multiple_of(b * KEYS, KEYS), n * KEYS)

    def blocks(count_blocks, body, state):
        state = lax.fori_loop(0, count_blocks // 4, lambda i, c: body(4 * i, 4, c), state)
        pairs = count_blocks // 2
        state = lax.fori_loop(
            count_blocks // 4 * 2, pairs, lambda i, c: body(2 * i, 2, c), state
        )
        return lax.fori_loop(2 * pairs, count_blocks, lambda i, c: body(i, 1, c), state)

    def spread(tile, out):
        for h in range(heads):
            tile[h * HEAD_DIM : (h + 1) * HEAD_DIM, :] = out[:, h * rows : (h + 1) * rows].astype(
                BF
            )

    def gather(tile, out):
        for h in range(heads):
            out[0:HEAD_DIM, h * rows : (h + 1) * rows] = tile[
                h * HEAD_DIM : (h + 1) * HEAD_DIM, :
            ]

    def tile(mine, t, k, position, acted, progress):
        start = position * rows
        edge = start // KEYS
        shift = lax.rem(start, KEYS)
        other = jnp.logical_not(mine)

        @pl.when(mine)
        def _():
            gather(q_ref.at[t], qs_ref)
            gather(g_ref.at[t], graw_ref)

        @pl.when(other)
        def _():
            q_in(k).wait_recv()
            g_in(k).wait_recv()
            gather(qin_ref.at[k], qs_ref)
            gather(gin_ref.at[k], graw_ref)

        s = dot(rows_ref[at(edge), :], qs_ref[...], 1, 0)
        column = lax.rem(lax.broadcasted_iota(jnp.int32, (1, lanes), 1), rows) + shift
        keep = lax.broadcasted_iota(jnp.int32, (KEYS, lanes), 0) <= column
        s = jnp.where(keep, s, -1e30)
        s_ref[at(edge), :] = s

        def top_of(s, n):
            return jnp.max(s.reshape(n * KEYS // 8, 8, lanes), axis=0)

        def scores(b, n, top):
            s = dot(rows_ref[at(b, n), :], qs_ref[...], 1, 0)
            s_ref[at(b, n), :] = s
            return jnp.maximum(top, top_of(s, n))

        top = jnp.max(blocks(edge, scores, top_of(s, 1)), axis=0, keepdims=True)

        def forward(b, n, state):
            total, out = state
            p = jnp.exp2(s_ref[at(b, n), :] - top)
            low = p.astype(BF)
            p_ref[at(b, n), :] = low
            return (
                total + jnp.sum(p.reshape(n * KEYS // 8, 8, lanes), axis=0),
                out + dot(flat_ref[HEAD_DIM : 2 * HEAD_DIM, at(b, n)], low, 1, 0),
            )

        total, out = blocks(
            edge + 1, forward, (jnp.zeros((8, lanes), F32), jnp.zeros((HEAD_DIM, lanes), F32))
        )
        inverse = 1.0 / jnp.sum(total, axis=0, keepdims=True)
        out = out * inverse
        pl.when(mine)(lambda: spread(att_ref.at[t], out))

        @pl.when(other)
        def _():
            spread(atts_ref.at[k], out)
            att_out(k).start()

        acted = advance(acted, progress + (edge + 2) // 2)
        g = graw_ref[...]
        scaled = (g.astype(F32) * inverse).astype(BF)
        gs_ref[HEAD_DIM : 2 * HEAD_DIM, :] = scaled
        delta = jnp.sum(scaled.astype(F32) * out, axis=0, keepdims=True)

        def backward(b, n, dq):
            p = p_ref[at(b, n), :]
            dp = dot(rows_ref[at(b, n), :], gs_ref[...], 1, 0)
            ds = (p.astype(F32) * (dp - delta)).astype(BF)
            dkv_ref[at(b, n), :] += dot(p, gs_ref[...], 1, 1) + dot(ds, qs_ref[...], 1, 1)
            return dq + dot(flat_ref[0:HEAD_DIM, at(b, n)], ds, 1, 0)

        dq = blocks(edge + 1, backward, jnp.zeros((HEAD_DIM, lanes), F32))
        dq = dq * (HEAD_DIM**-0.5)
        pl.when(mine)(lambda: spread(dq_ref.at[t], dq))

        @pl.when(other)
        def _():
            spread(dqs_ref.at[k], dq)
            dq_out(k).start()

        progress = progress + edge + 2
        return advance(acted, progress), progress

    per_block = KEYS // rows

    def sequence(s, state):
        slot = lax.rem(s, 2)
        load(s, slot).wait()
        pl.when(s + 1 < seqs)(lambda: load(s + 1, 1 - slot).start())
        dkv_ref[...] = jnp.zeros_like(dkv_ref)

        def turn(b, c):
            wide = jnp.concatenate(
                [kvt_ref[slot, b * per_block + i] for i in range(per_block)], axis=1
            )
            flat_ref[:, at(b)] = wide
            rows_ref[at(b), :] = wide.T
            return c

        lax.fori_loop(0, length // KEYS, turn, 0)
        given = given_of(s)
        own = groups - upper * given
        taken = (1 - upper) * given
        later = jnp.minimum(s, 1)

        def work(u, state):
            acted, progress = state
            v = u - taken * later
            mine = (v >= 0) & (v < own)
            t = s * groups + upper * given + jnp.clip(v, 0, own - 1)
            k = jnp.clip(u - own * (1 - later), 0, jnp.maximum(taken - 1, 0)) * seqs + s
            position = jnp.where(mine, me, partner)
            state = tile(mine, t, k, position, acted, progress)
            pl.when((u == 0) & (s > 0))(lambda: pass_on(s - 1))
            pl.when((u == 0) & (s + 1 < seqs))(lambda: start_in(s + 1))
            return state

        state = lax.fori_loop(0, own + taken, work, state)
        stage_ref[slot] = dkv_ref[...].reshape(chips, 2, rows, 2 * HEAD_DIM).astype(BF)
        core_out(s).start()
        return state

    acted, _ = lax.fori_loop(0, seqs, sequence, (jnp.int32(0), jnp.int32(0)))
    pass_on(seqs - 1)
    lax.fori_loop(acted, len(acts), act, 0)

    def end_given(k, c):
        q_in(k).wait_send()
        g_in(k).wait_send()
        att_out(k).wait_recv()
        dq_out(k).wait_recv()
        return c

    def end_taken(k, c):
        att_out(k).wait_send()
        dq_out(k).wait_send()
        return c

    lax.fori_loop(0, count * upper, end_given, 0)
    lax.fori_loop(0, count * (1 - upper), end_taken, 0)

    def end(s, c):
        slot_own(s).wait()
        for m in range(1, chips):
            slot_out(s, m).wait()
        return c

    lax.fori_loop(0, seqs, end, 0)


def attention(q, g, kv_all, down, up, seqs, dp):
    tiles, width, rows = q.shape
    ring = kv_all.shape[0]
    chips = ring // 2
    length = ring * rows
    lanes = width // HEAD_DIM * rows
    most = max(shipped(i, ring, tiles) for i in range(chips, ring))
    vmem = pl.BlockSpec(memory_space=pltpu.VMEM)
    anywhere = pl.BlockSpec(memory_space=pl.ANY)
    pair = 2 * HEAD_DIM
    dma = pltpu.SemaphoreType.DMA
    orders = bit_orders(dp, ring)
    stages = len(orders[0])
    return pl.pallas_call(
        functools.partial(attention_kernel, seqs, tiles // seqs, orders),
        out_shape=[
            jax.ShapeDtypeStruct(q.shape, BF),
            jax.ShapeDtypeStruct(q.shape, BF),
            jax.ShapeDtypeStruct((seqs, chips, rows, pair), BF),
            jax.ShapeDtypeStruct(
                (2, down.shape[0] >> halvings_of(down.shape[0], stages), down.shape[1]), BF
            ),
        ],
        in_specs=[vmem, vmem, anywhere, anywhere, anywhere],
        out_specs=[vmem, vmem, anywhere, anywhere],
        scratch_shapes=[
            pltpu.VMEM((2, ring, pair, rows), BF),
            pltpu.VMEM((pair, length), BF),
            pltpu.VMEM((length, pair), BF),
            pltpu.VMEM((length, pair), F32),
            pltpu.VMEM((length, lanes), F32),
            pltpu.VMEM((length, lanes), BF),
            pltpu.VMEM((pair, lanes), BF),
            pltpu.VMEM((pair, lanes), BF),
            pltpu.VMEM((most, width, rows), BF),
            pltpu.VMEM((most, width, rows), BF),
            pltpu.VMEM((most, width, rows), BF),
            pltpu.VMEM((most, width, rows), BF),
            pltpu.VMEM((2, chips, 2, rows, pair), BF),
            pltpu.VMEM((seqs, chips, rows, pair), BF),
            dma((2,)),
            dma((seqs,)),
            dma((2, most)),
            dma((2, most)),
            dma((2, most)),
            dma((2, most)),
            dma((seqs,)),
            dma((seqs,)),
            dma((seqs, chips)),
            dma((seqs, chips)),
            pltpu.VMEM((down.shape[0] // 2, down.shape[1]), BF),
            pltpu.VMEM((up.shape[0] // 2, up.shape[1]), BF),
            pltpu.VMEM((exchange_rows(down.shape[0], stages), down.shape[1]), BF),
            pltpu.VMEM((exchange_rows(up.shape[0], stages), up.shape[1]), BF),
            pltpu.VMEM((HEAD_DIM, lanes), BF),
            dma((4, stages)),
            dma((4, stages)),
            dma((4,)),
            dma((4,)),
        ],
        compiler_params=pltpu.CompilerParams(
            collective_id=2, has_side_effects=True, vmem_limit_bytes=60 * 2**20
        ),
        cost_estimate=pl.CostEstimate(
            flops=12 * tiles * rows * width * length * 4,
            bytes_accessed=8 * q.size,
            transcendentals=tiles * lanes * length // 2,
        ),
        name="attention",
    )(q, g, kv_all, down, up)


def bit_orders(dp, ring):
    seq_bits = [("seq", 1 << b) for b in range(ring.bit_length() - 1)]
    dp_bits = [("dp", 1 << b) for b in range(dp.bit_length() - 1)]
    far = seq_bits[2:]
    return (seq_bits[:2] + dp_bits + far, seq_bits[:1] + dp_bits + seq_bits[1:2] + far)

def side_of(bit):
    axis, weight = bit
    return lax.rem(lax.axis_index(axis) // weight, 2)

def partner_of(bit):
    axis, weight = bit
    me = lax.axis_index(axis)
    return {axis: me + weight - 2 * weight * side_of(bit)}

def add_rows(dst, a, b, dst_at, a_at, rows, step):
    def body(i, carry):
        r = pl.multiple_of(i * step, step)
        dst[pl.ds(dst_at + r, step), :] = a[pl.ds(a_at + r, step), :] + b[pl.ds(r, step), :]
        return carry
    lax.fori_loop(0, rows // step, body, 0)

def sum_kernel(orders, x_ref, out_ref, *scratch):
    parts = len(orders)
    stages = len(orders[0])
    rows, cols = x_ref.shape
    wide = cols // parts
    acc, recv, sems = scratch[:parts], scratch[parts:2*parts], scratch[2*parts:]
    send_sem, recv_sem = sems
    barrier = pltpu.get_barrier_semaphore()
    for bit in orders[0]:
        pl.semaphore_signal(barrier, inc=1, device_id=partner_of(bit), device_id_type=MESH)
    pl.semaphore_wait(barrier, stages)
    def copy(p, s, src, dst, bit):
        return pltpu.make_async_remote_copy(src_ref=src, dst_ref=dst, send_sem=send_sem.at[p, s], recv_sem=recv_sem.at[p, s],
            device_id=partner_of(bit), device_id_type=MESH)
    columns = [pl.ds(p * wide, wide) for p in range(parts)]
    start = [0] * parts
    whole = [0] * parts
    live = {}
    base = [0]
    for s in range(stages): base.append(base[-1] + rows // 2 ** min(s + 1, stages - 1))
    def launch(p, s):
        bit = orders[p][s]
        if s < stages - 1:
            half = rows // 2 ** (s + 1)
            other = pl.multiple_of(start[p] + (1 - side_of(bit)) * half, half)
            src = x_ref.at[pl.ds(other, half), columns[p]] if s == 0 else acc[p].at[pl.ds(other, half), :]
        else:
            half = rows // 2 ** s
            src = acc[p].at[pl.ds(pl.multiple_of(start[p], half), half), :]
        live[p] = copy(p, s, src, recv[p].at[pl.ds(base[s], half), :], bit)
        live[p].start()
    for p in range(parts): launch(p, 0)
    for s in range(stages):
        for p in range(parts):
            bit = orders[p][s]
            live[p].wait()
            half = rows // 2 ** min(s + 1, stages - 1)
            step = 16 if half % 64 else 64
            got = recv[p].at[pl.ds(base[s], half), :]
            if s == 0:
                mine = side_of(bit) * half
                whole[p] = mine
                add_rows(acc[p], x_ref.at[:, columns[p]], got, 0, pl.multiple_of(mine, half), half, step)
                start[p] = 0
            elif s < stages - 1:
                mine = pl.multiple_of(start[p] + side_of(bit) * half, half)
                add_rows(acc[p], acc[p], got, mine, mine, half, step)
                whole[p] = whole[p] + side_of(bit) * half
                start[p] = start[p] + side_of(bit) * half
            else:
                at = pl.multiple_of(start[p], half)
                add_rows(out_ref.at[:, columns[p]], acc[p], got, pl.multiple_of(whole[p], half), at, half, step)
            if s < stages - 1: launch(p, s + 1)
    def spread(p, s):
        bit = orders[p][s]
        half = rows // 2 ** (s + 1)
        src = out_ref.at[pl.ds(pl.multiple_of(whole[p], half), half), columns[p]]
        live[p] = copy(p, 2 * stages - 2 - s, src, src, bit)
        live[p].start()
    for p in range(parts): spread(p, stages - 2)
    for s in range(stages - 2, -1, -1):
        for p in range(parts):
            live[p].wait()
            whole[p] = whole[p] - side_of(orders[p][s]) * (rows // 2 ** (s + 1))
            if s: spread(p, s - 1)

def total_of(x, dp, ring, collective_id):
    orders = bit_orders(dp, ring)
    rows, cols = x.shape
    parts, stages = len(orders), len(orders[0])
    wide = cols // parts
    got = sum(rows // 2 ** min(s + 1, stages - 1) for s in range(stages))
    whole = pl.BlockSpec(memory_space=pltpu.VMEM)
    return pl.pallas_call(functools.partial(sum_kernel, orders),
        out_shape=jax.ShapeDtypeStruct(x.shape, BF), in_specs=[whole], out_specs=whole,
        scratch_shapes=[pltpu.VMEM((rows // 2, wide), BF)] * parts + [pltpu.VMEM((got, wide), BF)] * parts
        + [pltpu.SemaphoreType.DMA((parts, 2 * stages - 1))] * 2,
        compiler_params=pltpu.CompilerParams(collective_id=collective_id, has_side_effects=True, vmem_limit_bytes=56*2**20),
        name="total")(x)


def normal(h):
    center = h - jnp.mean(h, axis=-1, keepdims=True)
    spread = jnp.mean(center * center, axis=-1, keepdims=True)
    inverse = lax.rsqrt(spread + 1e-05)
    return center * inverse, inverse


def norm_gradient(q, gain, n, inverse):
    scaled = q * gain
    inner = jnp.mean(scaled * n, axis=-1, keepdims=True)
    return inverse * (scaled - jnp.mean(scaled, axis=-1, keepdims=True) - n * inner)


def turned_back(rows, cosine, sine):
    half = cosine.shape[0]
    first, second = rows[:half], rows[half : 2 * half]
    return jnp.concatenate(
        [first * cosine + second * sine, second * cosine - first * sine, rows[2 * half :]], axis=0
    )


def finish_kernel(
    att_ref,
    dq_ref,
    slot_ref,
    cos_ref,
    sin_ref,
    h_ref,
    c_ref,
    ff_ref,
    gm_ref,
    norms_ref,
    weight_ref,
    out_weight_ref,
    up_bias_ref,
    layer_ref,
    input_ref,
    rest_ref,
    raw_ref,
    acc_ref,
    lines_ref,
):
    step = pl.program_id(0)
    d = h_ref.shape[1]
    rows = h_ref.shape[0]
    wide = weight_ref.shape[1]

    @pl.when(step == 0)
    def _():
        acc_ref[...] = jnp.zeros_like(acc_ref)
        lines_ref[...] = jnp.zeros_like(lines_ref)
        for i in range(up_bias_ref.shape[1] // d):
            lines_ref[8 + i : 9 + i, :] = up_bias_ref[:, i * d : (i + 1) * d]

    hidden = h_ref[...].astype(F32)
    low_c = c_ref[...]
    cot = low_c.astype(F32)
    n, inverse = normal(hidden)
    gain1, bias1 = norms_ref[0:1, :], norms_ref[1:2, :]
    gain2, bias_out = norms_ref[2:3, :], norms_ref[3:4, :]
    normed = (n * gain1 + bias1).astype(BF)
    att = att_ref[0]
    layer_ref[...] = hidden + dot(att, out_weight_ref[...], 0, 0) + ff_ref[...] + bias_out
    acc_ref[wide : wide + d, :] += dot(att, low_c, 1, 0)
    cosine, sine = cos_ref[0], sin_ref[0]
    for h in range(d // HEAD_DIM):
        at = slice(h * HEAD_DIM, (h + 1) * HEAD_DIM)
        raw_ref[at, :] = turned_back(dq_ref[0, at, :].astype(F32), cosine, sine).astype(BF)
    kv = slot_ref[0, 0].astype(F32)
    for m in range(1, slot_ref.shape[1]):
        kv = kv + slot_ref[0, m].astype(F32)
    lane = lax.broadcasted_iota(jnp.int32, (1, 2 * HEAD_DIM), 1)
    kv = (kv * jnp.where(lane < HEAD_DIM, 1.0 / LOG2E, 1.0)).astype(BF).astype(F32).T
    raw_ref[d : d + HEAD_DIM, :] = turned_back(kv[:HEAD_DIM], cosine, sine).astype(BF)
    raw_ref[d + HEAD_DIM :, :] = kv[HEAD_DIM:].astype(BF)
    raw = raw_ref[...]
    acc_ref[0:wide, :] += dot(raw, normed, 1, 0)
    sums = dot(jnp.ones((8, rows), BF), raw, 1, 1)
    lines_ref[4:5, :] += sums[0:1, :d]
    lines_ref[5:6, 0 : wide - d] += sums[0:1, d:]
    ga = dot(raw, weight_ref[...], 0, 1)
    gm = gm_ref[...]
    lines_ref[0:1, :] += jnp.sum(ga * n, axis=0, keepdims=True)
    lines_ref[1:2, :] += jnp.sum(ga, axis=0, keepdims=True)
    lines_ref[2:3, :] += jnp.sum(gm * n, axis=0, keepdims=True)
    lines_ref[3:4, :] += jnp.sum(gm, axis=0, keepdims=True)
    lines_ref[6:7, :] += jnp.sum(cot, axis=0, keepdims=True)
    input_ref[...] = (
        cot + norm_gradient(ga, gain1, n, inverse) + norm_gradient(gm, gain2, n, inverse)
    )

    @pl.when(step == pl.num_programs(0) - 1)
    def _():
        rest_ref[0:d, :] = acc_ref[0:d, :].T.astype(BF)
        rest_ref[d : 2 * d, :] = acc_ref[wide : wide + d, :].astype(BF)
        rest_ref[2 * d : d + wide, :] = acc_ref[d:wide, :].astype(BF)
        rest_ref[d + wide : d + wide + 16, :] = lines_ref[...].astype(BF)
        rest_ref[d + wide + 16 :, :] = jnp.zeros((rest_ref.shape[0] - d - wide - 16, d), BF)


def finish(att, dq, slots, cosine, sine, hidden, cot, ff, gm, norms, weight, out_weight, up_bias, padded):
    seqs, d, rows = att.shape
    wide = weight.shape[1]
    by_seq = pl.BlockSpec((1, d, rows), lambda i: (i, 0, 0))
    angle = pl.BlockSpec((1,) + cosine.shape[1:], lambda i: (i, 0, 0))
    by_row = pl.BlockSpec((rows, d), lambda i: (i, 0))

    def all_of(a):
        return pl.BlockSpec(a.shape, lambda i: (0,) * a.ndim)

    return pl.pallas_call(
        finish_kernel,
        grid=(seqs,),
        out_shape=[
            jax.ShapeDtypeStruct(hidden.shape, F32),
            jax.ShapeDtypeStruct(hidden.shape, F32),
            jax.ShapeDtypeStruct((padded, d), BF),
        ],
        in_specs=[
            by_seq,
            by_seq,
            pl.BlockSpec((1,) + slots.shape[1:], lambda i: (i, 0, 0, 0)),
            angle,
            angle,
            by_row,
            by_row,
            by_row,
            by_row,
            all_of(norms),
            all_of(weight),
            all_of(out_weight),
            all_of(up_bias),
        ],
        out_specs=[by_row, by_row, pl.BlockSpec((padded, d), lambda i: (0, 0))],
        scratch_shapes=[
            pltpu.VMEM((wide, rows), BF),
            pltpu.VMEM((wide + d, d), F32),
            pltpu.VMEM((16, d), F32),
        ],
        compiler_params=pltpu.CompilerParams(vmem_limit_bytes=48 * 2**20),
        cost_estimate=pl.CostEstimate(
            flops=12 * seqs * rows * d * d, bytes_accessed=26 * seqs * rows * d, transcendentals=0
        ),
        name="finish",
    )(att, dq, slots, cosine, sine, hidden, cot, ff, gm, norms, weight, out_weight, up_bias)


def local(
    hidden_in,
    positions,
    ln1_gain,
    ln1_bias,
    ln2_gain,
    ln2_bias,
    query_projection,
    query_bias,
    shared_key_weight,
    shared_key_bias,
    shared_value_weight,
    shared_value_bias,
    output_weight,
    output_bias,
    up_weight,
    up_bias,
    down_weight,
    down_bias,
    cotangent,
):
    seq_count, local_len = hidden_in.shape[0], hidden_in.shape[1]
    ring = lax.axis_size("seq")
    groups = ring // seq_count
    per_group = HEADS // groups
    width = per_group * HEAD_DIM
    hidden = hidden_in.astype(F32)
    cosine, sine = angles_of(positions)
    normed_a = layer_norm(hidden, ln1_gain, ln1_bias).astype(BF)
    normed_m = layer_norm(hidden, ln2_gain, ln2_bias).astype(BF)

    tokens = seq_count * local_len
    kv_weight = jnp.concatenate([shared_key_weight, shared_value_weight], axis=1)
    kv_bias = jnp.concatenate([shared_key_bias, shared_value_bias])
    kv_pre = jnp.einsum("stc,cw->swt", normed_a, kv_weight, preferred_element_type=F32)
    kv_pre = kv_pre + kv_bias[:, None]
    kv_low = jnp.concatenate(
        [rotary_rows(kv_pre[:, :HEAD_DIM], cosine, sine), kv_pre[:, HEAD_DIM:]], axis=1
    ).astype(BF)
    kv_all = lax.all_gather(kv_low.reshape(-1, local_len), "seq")
    query_pre = jnp.einsum("stc,cw->swt", normed_a, query_projection, preferred_element_type=F32)
    query_pre = (query_pre + query_bias[:, None]).reshape(seq_count, HEADS, HEAD_DIM, local_len)
    query_low = (rotary_rows(query_pre, cosine[:, None], sine[:, None]) * (LOG2E / 8.0)).astype(BF)
    query_tiles = query_low.reshape(-1, width, local_len)
    grad_attended = jnp.einsum(
        "stc,wc->swt", cotangent, output_weight, preferred_element_type=F32
    ).astype(BF)
    grad_tiles = grad_attended.reshape(-1, width, local_len)

    feedforward, grad_normed_m, grad_w_up, grad_w_down, grad_b_up = feed_forward(
        normed_m.reshape(tokens, D),
        cotangent.reshape(tokens, D),
        up_weight,
        up_bias[None],
        down_weight,
    )
    query_tiles, grad_tiles, kv_all, grad_w_up, grad_w_down = lax.optimization_barrier(
        (query_tiles, grad_tiles, kv_all, grad_w_up, grad_w_down)
    )
    dp = lax.axis_size("dp")
    orders = bit_orders(dp, ring)
    out, dq, dkv, parts = attention(
        query_tiles, grad_tiles, kv_all, grad_w_down, grad_w_up, seq_count, dp
    )
    grad_w_down, grad_w_up = unpack(
        parts, down_weight.shape, up_weight.shape, orders, dp, ring
    )
    qkv = D + 2 * HEAD_DIM
    ff = up_weight.shape[1]
    unit = 16 * dp * ring // 2
    padded = -(-(D + qkv + 16) // unit) * unit
    norms = jnp.concatenate(
        [ln1_gain[None], ln1_bias[None], ln2_gain[None], (output_bias + down_bias)[None]]
        + [jnp.zeros((4, D), F32)],
        axis=0,
    )
    layer_out, input_grad, rest = finish(
        out.reshape(seq_count, D, local_len),
        dq.reshape(seq_count, D, local_len),
        dkv,
        cosine,
        sine,
        hidden_in.reshape(tokens, D),
        cotangent.reshape(tokens, D),
        feedforward,
        grad_normed_m,
        norms,
        jnp.concatenate([query_projection, kv_weight], axis=1),
        output_weight,
        grad_b_up,
        padded,
    )
    rest = total_of(rest, dp, ring, 3)
    kv_rows = rest[2 * D : D + qkv].astype(F32)
    lines = rest[D + qkv : D + qkv + 16].astype(F32)
    return (
        layer_out.reshape(hidden.shape),
        input_grad.reshape(hidden.shape),
        lines[0],
        lines[1],
        lines[2],
        lines[3],
        rest[:D].astype(F32),
        lines[4],
        kv_rows[:HEAD_DIM].T,
        lines[5, :HEAD_DIM],
        kv_rows[HEAD_DIM:].T,
        lines[5, HEAD_DIM : 2 * HEAD_DIM],
        rest[D : 2 * D].astype(F32),
        lines[6],
        grad_w_up,
        lines[8 : 8 + ff // D].reshape(ff),
        grad_w_down,
        lines[6],
    )


def solution(mesh):
    rows = P("dp", "seq", None)
    placed = (rows, P("dp", "seq")) + (P(),) * 16 + (rows,)
    return jax.shard_map(
        local,
        mesh=mesh,
        in_specs=placed,
        out_specs=(rows, rows) + (P(),) * 16,
        check_vma=False,
    )
```

```python
import functools
import math

import jax
import jax.numpy as jnp
from jax import lax
from jax.experimental import pallas as pl
from jax.experimental.pallas import tpu as pltpu
from jax.sharding import PartitionSpec as P

D = 768
HEADS = 12
HEAD_DIM = 64
ROT_DIMS = 16
BF = jnp.bfloat16
F32 = jnp.float32
LOG2E = math.log2(math.e)


def layer_norm(values, gain, bias):
    center = values - jnp.mean(values, axis=-1, keepdims=True)
    spread = jnp.mean(center * center, axis=-1, keepdims=True)
    return center * lax.rsqrt(spread + 1e-05) * gain + bias


def rotary_rows(values, cosine, sine):
    half = cosine.shape[-2]
    first, second = values[..., :half, :], values[..., half : 2 * half, :]
    return jnp.concatenate(
        [first * cosine - second * sine, second * cosine + first * sine, values[..., 2 * half :, :]],
        axis=-2,
    )


def angles_of(positions):
    half = ROT_DIMS // 2
    frequency = jnp.exp(
        jnp.arange(half).astype(F32) * (-2.0 * math.log(10000.0) / ROT_DIMS)
    )
    angle = positions.astype(F32)[:, None, :] * frequency[None, :, None]
    return jnp.cos(angle), jnp.sin(angle)


MESH = pl.DeviceIdType.MESH


def dot(a, b, ca, cb):
    return lax.dot_general(a, b, (((ca,), (cb,)), ((), ())), preferred_element_type=F32)


def flip(index, weight):
    return index + weight - 2 * weight * lax.rem(index // weight, 2)


def gelu_parts(u):
    e = jnp.exp(u * u * -0.5)
    t = 1.0 / (1.0 + (0.3275911 / math.sqrt(2.0)) * jnp.abs(u))
    poly = t * (
        0.5 * 0.254829592
        + t
        * (
            0.5 * -0.284496736
            + t * (0.5 * 1.421413741 + t * (0.5 * -1.453152027 + t * (0.5 * 1.061405429)))
        )
    )
    tail = poly * e
    return jnp.where(u >= 0, 1.0 - tail, tail), e * (1.0 / math.sqrt(2.0 * math.pi))


def feed_kernel(
    x_ref,
    c_ref,
    up_ref,
    down_ref,
    bias_ref,
    ff_ref,
    gx_ref,
    gup_ref,
    gdown_ref,
    gbias_ref,
    act_ref,
    grad_ref,
):
    tokens = x_ref.shape[0]
    bias = bias_ref[...]
    sub = min(256, tokens)
    for r in range(0, tokens, sub):
        u = dot(x_ref[r : r + sub, :], up_ref[...], 1, 0) + bias
        share, density = gelu_parts(u)
        act_ref[r : r + sub, :] = (u * share).astype(BF)
        da = dot(c_ref[r : r + sub, :], down_ref[...], 1, 1)
        grad_ref[r : r + sub, :] = (da * (share + u * density)).astype(BF)

    @pl.when(pl.program_id(0) == 0)
    def _():
        ff_ref[...] = jnp.zeros_like(ff_ref)
        gx_ref[...] = jnp.zeros_like(gx_ref)

    act, grad = act_ref[...], grad_ref[...]
    ff_ref[...] += dot(act, down_ref[...], 1, 0)
    gx_ref[...] += dot(grad, up_ref[...], 1, 1)
    gdown_ref[...] = dot(act, c_ref[...], 0, 0).astype(BF)
    gup_ref[...] = dot(x_ref[...], grad, 0, 0).astype(BF)
    gbias_ref[...] = jnp.sum(grad.astype(F32), axis=0, keepdims=True)


def feed_forward(x, cot, up_weight, up_bias, down_weight):
    tokens, d = x.shape
    ff = up_weight.shape[1]
    wide = d
    steps = ff // wide
    whole = pl.BlockSpec((tokens, d), lambda i: (0, 0))
    by_column = pl.BlockSpec((d, wide), lambda i: (0, i))
    by_row = pl.BlockSpec((wide, d), lambda i: (i, 0))
    line = pl.BlockSpec((1, wide), lambda i: (0, i))
    return pl.pallas_call(
        feed_kernel,
        grid=(steps,),
        out_shape=[
            jax.ShapeDtypeStruct((tokens, d), F32),
            jax.ShapeDtypeStruct((tokens, d), F32),
            jax.ShapeDtypeStruct((ff, d), BF),
            jax.ShapeDtypeStruct((ff, d), BF),
            jax.ShapeDtypeStruct((1, ff), F32),
        ],
        in_specs=[whole, whole, by_column, by_row, line],
        out_specs=[whole, whole, pl.BlockSpec((d, wide), lambda i: (i, 0)), by_row, line],
        scratch_shapes=[pltpu.VMEM((tokens, wide), BF), pltpu.VMEM((tokens, wide), BF)],
        compiler_params=pltpu.CompilerParams(vmem_limit_bytes=56 * 2**20),
        cost_estimate=pl.CostEstimate(
            flops=12 * tokens * d * ff,
            bytes_accessed=16 * d * ff,
            transcendentals=tokens * ff,
        ),
        name="feed_forward",
    )(x, cot, up_weight, down_weight, up_bias)


KEYS = 256


def shipped(upper_index, ring, tiles):
    more = upper_index + 2
    return (tiles * (2 * upper_index + 1 - ring) + more) // (2 * more)


class Exchange:
    def __init__(self, index, order, array, out, acc, recv, first, wide, sems):
        self.index, self.order, self.sems = index, order, sems
        self.array, self.out, self.acc, self.recv = array, out, acc, recv
        self.columns = pl.ds(first, wide)
        self.rows = array.shape[0]
        self.halvings = halvings_of(self.rows, len(order))
        self.waits = len(order)

    def size(self, s):
        return self.rows >> min(s, self.halvings)

    def base(self, s):
        return sum(self.size(t + 1) for t in range(s))

    def start(self, s, first=1):
        at = 0
        for t in range(first, min(s, self.halvings)):
            at = at + side_of(self.order[t]) * self.size(t + 1)
        return at

    def copy(self, k):
        bit = self.order[k]
        size = self.size(k + 1)
        other = self.start(k) + ((1 - side_of(bit)) * size if k < self.halvings else 0)
        rows = pl.ds(pl.multiple_of(other, size), size)
        src = (self.array if k == 0 else self.acc).at[rows, self.columns]
        dst = self.recv.at[pl.ds(self.base(k), size), self.columns]
        return pltpu.make_async_remote_copy(
            src_ref=src,
            dst_ref=dst,
            send_sem=self.sems[0].at[self.index, k],
            recv_sem=self.sems[1].at[self.index, k],
            device_id=partner_of(bit),
            device_id_type=MESH,
        )

    def fill(self):
        half = self.size(1)
        rows = pl.ds(pl.multiple_of(side_of(self.order[0]) * half, half), half)
        return pltpu.make_async_copy(
            self.array.at[rows, self.columns],
            self.acc.at[:, self.columns],
            self.sems[2].at[self.index],
        )

    def empty(self):
        size = self.size(self.halvings)
        rows = pl.ds(pl.multiple_of(self.start(self.halvings), size), size)
        return pltpu.make_async_copy(
            self.acc.at[rows, self.columns],
            self.out.at[:, self.columns],
            self.sems[3].at[self.index],
        )

    def begin(self):
        self.fill().start()
        self.copy(0).start()

    def take(self, k):
        self.copy(k).wait()
        if k == 0:
            self.fill().wait()
        size = self.size(k + 1)
        start = self.start(k + 1)
        step = next(n for n in (128, 96, 64, 48, 32, 16) if size % n == 0)
        base = self.base(k)

        def add(i, carry):
            r = pl.multiple_of(i * step, step)
            mine = pl.ds(pl.multiple_of(start + r, step), step)
            self.acc[mine, self.columns] = (
                self.acc[mine, self.columns] + self.recv[pl.ds(base + r, step), self.columns]
            )
            return carry

        lax.fori_loop(0, size // step, add, 0)
        if k == len(self.order) - 1:
            self.empty().start()
            self.empty().wait()
        if k + 1 < self.waits:
            self.copy(k + 1).start()


def owners(rows, order, dp, ring):
    halved = order[: halvings_of(rows, len(order))]
    found = []
    for segment in range(1 << len(halved)):
        place = {"dp": 0, "seq": 0}
        for t, (axis, weight) in enumerate(halved):
            place[axis] += weight * (segment >> (len(halved) - 1 - t) & 1)
        found.append(place["dp"] * ring + place["seq"])
    return found


def unpack_kernel(froms, all_ref, down_out, up_out, low, wide, come_sem, sent_sem):
    count = len(froms[0])
    tall, across = all_ref.shape[2:]
    come = [
        [
            pltpu.make_async_copy(all_ref.at[d, a], low.at[a, i], come_sem.at[a, i])
            for i, d in enumerate(froms[a])
        ]
        for a in range(2)
    ]
    for copy in come[0] + come[1]:
        copy.start()
    gone = []
    for a in range(2):
        for i in range(count):
            come[a][i].wait()
            wide[a, i] = low[a, i].astype(F32)
            at = i * tall
            if a == 0:
                to = down_out.at[pl.ds(at, tall), :]
            else:
                block = at // across
                to = up_out.at[pl.ds(at - block * across, tall), pl.ds(block * across, across)]
            gone.append(pltpu.make_async_copy(wide.at[a, i], to, sent_sem.at[a, i]))
            gone[-1].start()
    for copy in gone:
        copy.wait()


def unpack(parts, down_shape, up_shape, orders, dp, ring):
    everyone = lax.all_gather(parts, ("dp", "seq"))
    froms = [owners(down_shape[0], order, dp, ring) for order in orders]
    anywhere = pl.BlockSpec(memory_space=pl.ANY)
    dma = pltpu.SemaphoreType.DMA
    size = down_shape[0] * down_shape[1]
    count = len(froms[0])
    return pl.pallas_call(
        functools.partial(unpack_kernel, froms),
        out_shape=[jax.ShapeDtypeStruct(down_shape, F32), jax.ShapeDtypeStruct(up_shape, F32)],
        in_specs=[anywhere],
        out_specs=[anywhere] * 2,
        scratch_shapes=[
            pltpu.VMEM((2, count) + parts.shape[1:], BF),
            pltpu.VMEM((2, count) + parts.shape[1:], F32),
            dma((2, count)),
            dma((2, count)),
        ],
        compiler_params=pltpu.CompilerParams(vmem_limit_bytes=48 * 2**20),
        cost_estimate=pl.CostEstimate(flops=4 * size, bytes_accessed=12 * size, transcendentals=0),
        name="unpack",
    )(everyone)


def halvings_of(rows, stages):
    count = 0
    while count < stages and rows % (32 << count) == 0:
        count += 1
    return count


def exchange_rows(rows, stages):
    count = halvings_of(rows, stages)
    return sum(rows >> min(s + 1, count) for s in range(stages))


def attention_kernel(
    seqs,
    groups,
    orders,
    q_ref,
    g_ref,
    all_ref,
    down_ref,
    up_ref,
    att_ref,
    dq_ref,
    slot_ref,
    sum_ref,
    kvt_ref,
    flat_ref,
    rows_ref,
    dkv_ref,
    s_ref,
    p_ref,
    qs_ref,
    gs_ref,
    qin_ref,
    gin_ref,
    atts_ref,
    dqs_ref,
    stage_ref,
    half_ref,
    load_sem,
    own_sem,
    in_send,
    in_recv,
    out_send,
    out_recv,
    core_send,
    core_recv,
    slot_send,
    slot_recv,
    down_acc_ref,
    up_acc_ref,
    down_recv_ref,
    up_recv_ref,
    graw_ref,
    sum_send,
    sum_recv,
    fill_sem,
    empty_sem,
):
    tiles, width, rows = q_ref.shape
    ring = all_ref.shape[0]
    chips = ring // 2
    heads = width // HEAD_DIM
    lanes = heads * rows
    length = ring * rows
    me = lax.axis_index("seq")
    chip, core = me // 2, lax.rem(me, 2)
    upper = me // chips
    partner = ring - 1 - me
    count = shipped(me + (1 - upper) * (partner - me), ring, tiles)

    def to(index):
        return {"seq": index}

    barrier = pltpu.get_barrier_semaphore()

    def greet(index):
        pl.semaphore_signal(barrier, inc=1, device_id=to(index), device_id_type=MESH)

    greet(partner)
    greet(flip(me, 1))
    for m in range(1, chips):
        greet(lax.rem(me + 2 * m, ring))
    across = [bit for bit in orders[0] if bit[0] == "dp"]
    for bit in across:
        pl.semaphore_signal(
            barrier, inc=1, device_id=partner_of(bit), device_id_type=MESH
        )
    pl.semaphore_wait(barrier, chips + 1 + len(across))

    def load(s, slot):
        return pltpu.make_async_copy(
            all_ref.at[:, pl.ds(pl.multiple_of(s * 2 * HEAD_DIM, 2 * HEAD_DIM), 2 * HEAD_DIM), :],
            kvt_ref.at[slot],
            load_sem.at[slot],
        )

    load(0, 0).start()

    def place(k):
        return lax.rem(k, seqs) * groups + k // seqs

    def remote(src, dst, sems, which, k, index):
        return pltpu.make_async_remote_copy(
            src_ref=src,
            dst_ref=dst,
            send_sem=sems[0].at[which, k],
            recv_sem=sems[1].at[which, k],
            device_id=to(index),
            device_id_type=MESH,
        )

    def q_in(k):
        return remote(q_ref.at[place(k)], qin_ref.at[k], (in_send, in_recv), 0, k, partner)

    def g_in(k):
        return remote(g_ref.at[place(k)], gin_ref.at[k], (in_send, in_recv), 1, k, partner)

    def att_out(k):
        return remote(atts_ref.at[k], att_ref.at[place(k)], (out_send, out_recv), 0, k, partner)

    def dq_out(k):
        return remote(dqs_ref.at[k], dq_ref.at[place(k)], (out_send, out_recv), 1, k, partner)

    def given_of(s):
        return (count - s + seqs - 1) // seqs

    def start_in(s):
        def one(i, carry):
            q_in(i * seqs + s).start()
            g_in(i * seqs + s).start()
            return carry

        lax.fori_loop(0, upper * given_of(s), one, 0)

    start_in(0)

    sems = (sum_send, sum_recv, fill_sem, empty_sem)
    half_down, half_up = down_ref.shape[1] // 2, up_ref.shape[1] // 2
    teams = []
    for i in range(2):
        teams.append(
            [
                Exchange(
                    2 * i, orders[0], down_ref, sum_ref.at[0], down_acc_ref, down_recv_ref,
                    i * half_down, half_down, sems,
                ),
                Exchange(
                    2 * i + 1, orders[1], up_ref, sum_ref.at[1], up_acc_ref, up_recv_ref,
                    i * half_up, half_up, sems,
                ),
            ]
        )
    most_waits = [max(e.waits for e in team) for team in teams]
    planned = ((10, 40, 58, 72, 86), (18, 58, 76, 90, 101))
    acts = []
    for i in range(2):
        for k in range(most_waits[i]):
            acts.append((planned[i][min(k, 4)] + max(0, k - 4), i, k))
    acts.sort()
    dues = [due for due, _, _ in acts]
    acts = [(i, k) for _, i, k in acts]
    for team in teams:
        for e in team:
            e.begin()

    def act(number, carry):
        for n, (i, k) in enumerate(acts):
            def run(i=i, k=k):
                for e in teams[i]:
                    if k < e.waits:
                        e.take(k)

            pl.when(number == n)(run)
        return carry

    def cost_of(position):
        return position * rows // KEYS + 2

    total_cost = (tiles - upper * count) * cost_of(me) + (1 - upper) * count * cost_of(partner)

    def advance(acted, progress):
        due = sum(jnp.where(progress * 100 >= at * total_cost, 1, 0) for at in dues)
        lax.fori_loop(acted, due, act, 0)
        return jnp.maximum(acted, due)

    def core_out(s):
        return pltpu.make_async_remote_copy(
            src_ref=stage_ref.at[lax.rem(s, 2), :, 1 - core],
            dst_ref=half_ref.at[s],
            send_sem=core_send.at[s],
            recv_sem=core_recv.at[s],
            device_id=to(flip(me, 1)),
            device_id_type=MESH,
        )

    def slot_out(s, m):
        target = lax.rem(chip + m, chips)
        return pltpu.make_async_remote_copy(
            src_ref=half_ref.at[s, target],
            dst_ref=slot_ref.at[s, m],
            send_sem=slot_send.at[s, m],
            recv_sem=slot_recv.at[s, m],
            device_id=to(2 * target + core),
            device_id_type=MESH,
        )

    def slot_own(s):
        return pltpu.make_async_copy(half_ref.at[s, chip], slot_ref.at[s, 0], own_sem.at[s])

    def pass_on(s):
        core_out(s).wait()

        def add(m, carry):
            half_ref[s, m] = (
                half_ref[s, m].astype(F32) + stage_ref[lax.rem(s, 2), m, core].astype(F32)
            ).astype(BF)
            return carry

        lax.fori_loop(0, chips, add, 0)
        slot_own(s).start()
        for m in range(1, chips):
            slot_out(s, m).start()

    qs_ref[...] = jnp.zeros_like(qs_ref)
    gs_ref[...] = jnp.zeros_like(gs_ref)

    def at(b, n=1):
        return pl.ds(pl.multiple_of(b * KEYS, KEYS), n * KEYS)

    def blocks(count_blocks, body, state):
        state = lax.fori_loop(0, count_blocks // 4, lambda i, c: body(4 * i, 4, c), state)
        pairs = count_blocks // 2
        state = lax.fori_loop(
            count_blocks // 4 * 2, pairs, lambda i, c: body(2 * i, 2, c), state
        )
        return lax.fori_loop(2 * pairs, count_blocks, lambda i, c: body(i, 1, c), state)

    def spread(tile, out):
        for h in range(heads):
            tile[h * HEAD_DIM : (h + 1) * HEAD_DIM, :] = out[:, h * rows : (h + 1) * rows].astype(
                BF
            )

    def gather(tile, out):
        for h in range(heads):
            out[0:HEAD_DIM, h * rows : (h + 1) * rows] = tile[
                h * HEAD_DIM : (h + 1) * HEAD_DIM, :
            ]

    def tile(mine, t, k, position, acted, progress):
        start = position * rows
        edge = start // KEYS
        shift = lax.rem(start, KEYS)
        other = jnp.logical_not(mine)

        @pl.when(mine)
        def _():
            gather(q_ref.at[t], qs_ref)
            gather(g_ref.at[t], graw_ref)

        @pl.when(other)
        def _():
            q_in(k).wait_recv()
            g_in(k).wait_recv()
            gather(qin_ref.at[k], qs_ref)
            gather(gin_ref.at[k], graw_ref)

        s = dot(rows_ref[at(edge), :], qs_ref[...], 1, 0)
        column = lax.rem(lax.broadcasted_iota(jnp.int32, (1, lanes), 1), rows) + shift
        keep = lax.broadcasted_iota(jnp.int32, (KEYS, lanes), 0) <= column
        s = jnp.where(keep, s, -1e30)
        s_ref[at(edge), :] = s

        def top_of(s, n):
            return jnp.max(s.reshape(n * KEYS // 8, 8, lanes), axis=0)

        def scores(b, n, top):
            s = dot(rows_ref[at(b, n), :], qs_ref[...], 1, 0)
            s_ref[at(b, n), :] = s
            return jnp.maximum(top, top_of(s, n))

        top = jnp.max(blocks(edge, scores, top_of(s, 1)), axis=0, keepdims=True)

        def forward(b, n, state):
            total, out = state
            p = jnp.exp2(s_ref[at(b, n), :] - top)
            low = p.astype(BF)
            p_ref[at(b, n), :] = low
            return (
                total + jnp.sum(p.reshape(n * KEYS // 8, 8, lanes), axis=0),
                out + dot(flat_ref[HEAD_DIM : 2 * HEAD_DIM, at(b, n)], low, 1, 0),
            )

        total, out = blocks(
            edge + 1, forward, (jnp.zeros((8, lanes), F32), jnp.zeros((HEAD_DIM, lanes), F32))
        )
        inverse = 1.0 / jnp.sum(total, axis=0, keepdims=True)
        out = out * inverse
        pl.when(mine)(lambda: spread(att_ref.at[t], out))

        @pl.when(other)
        def _():
            spread(atts_ref.at[k], out)
            att_out(k).start()

        acted = advance(acted, progress + (edge + 2) // 2)
        g = graw_ref[...]
        scaled = (g.astype(F32) * inverse).astype(BF)
        gs_ref[HEAD_DIM : 2 * HEAD_DIM, :] = scaled
        delta = jnp.sum(scaled.astype(F32) * out, axis=0, keepdims=True)

        def backward(b, n, dq):
            p = p_ref[at(b, n), :]
            dp = dot(rows_ref[at(b, n), :], gs_ref[...], 1, 0)
            ds = (p.astype(F32) * (dp - delta)).astype(BF)
            dkv_ref[at(b, n), :] += dot(p, gs_ref[...], 1, 1) + dot(ds, qs_ref[...], 1, 1)
            return dq + dot(flat_ref[0:HEAD_DIM, at(b, n)], ds, 1, 0)

        dq = blocks(edge + 1, backward, jnp.zeros((HEAD_DIM, lanes), F32))
        dq = dq * (HEAD_DIM**-0.5)
        pl.when(mine)(lambda: spread(dq_ref.at[t], dq))

        @pl.when(other)
        def _():
            spread(dqs_ref.at[k], dq)
            dq_out(k).start()

        progress = progress + edge + 2
        return advance(acted, progress), progress

    per_block = KEYS // rows

    def sequence(s, state):
        slot = lax.rem(s, 2)
        load(s, slot).wait()
        pl.when(s + 1 < seqs)(lambda: load(s + 1, 1 - slot).start())
        dkv_ref[...] = jnp.zeros_like(dkv_ref)

        def turn(b, c):
            wide = jnp.concatenate(
                [kvt_ref[slot, b * per_block + i] for i in range(per_block)], axis=1
            )
            flat_ref[:, at(b)] = wide
            rows_ref[at(b), :] = wide.T
            return c

        lax.fori_loop(0, length // KEYS, turn, 0)
        given = given_of(s)
        own = groups - upper * given
        taken = (1 - upper) * given
        later = jnp.minimum(s, 1)

        def work(u, state):
            acted, progress = state
            v = u - taken * later
            mine = (v >= 0) & (v < own)
            t = s * groups + upper * given + jnp.clip(v, 0, own - 1)
            k = jnp.clip(u - own * (1 - later), 0, jnp.maximum(taken - 1, 0)) * seqs + s
            position = jnp.where(mine, me, partner)
            state = tile(mine, t, k, position, acted, progress)
            pl.when((u == 0) & (s > 0))(lambda: pass_on(s - 1))
            pl.when((u == 0) & (s + 1 < seqs))(lambda: start_in(s + 1))
            return state

        state = lax.fori_loop(0, own + taken, work, state)
        stage_ref[slot] = dkv_ref[...].reshape(chips, 2, rows, 2 * HEAD_DIM).astype(BF)
        core_out(s).start()
        return state

    acted, _ = lax.fori_loop(0, seqs, sequence, (jnp.int32(0), jnp.int32(0)))
    pass_on(seqs - 1)
    lax.fori_loop(acted, len(acts), act, 0)

    def end_given(k, c):
        q_in(k).wait_send()
        g_in(k).wait_send()
        att_out(k).wait_recv()
        dq_out(k).wait_recv()
        return c

    def end_taken(k, c):
        att_out(k).wait_send()
        dq_out(k).wait_send()
        return c

    lax.fori_loop(0, count * upper, end_given, 0)
    lax.fori_loop(0, count * (1 - upper), end_taken, 0)

    def end(s, c):
        slot_own(s).wait()
        for m in range(1, chips):
            slot_out(s, m).wait()
        return c

    lax.fori_loop(0, seqs, end, 0)


def attention(q, g, kv_all, down, up, seqs, dp):
    tiles, width, rows = q.shape
    ring = kv_all.shape[0]
    chips = ring // 2
    length = ring * rows
    lanes = width // HEAD_DIM * rows
    most = max(shipped(i, ring, tiles) for i in range(chips, ring))
    vmem = pl.BlockSpec(memory_space=pltpu.VMEM)
    anywhere = pl.BlockSpec(memory_space=pl.ANY)
    pair = 2 * HEAD_DIM
    dma = pltpu.SemaphoreType.DMA
    orders = bit_orders(dp, ring)
    stages = len(orders[0])
    return pl.pallas_call(
        functools.partial(attention_kernel, seqs, tiles // seqs, orders),
        out_shape=[
            jax.ShapeDtypeStruct(q.shape, BF),
            jax.ShapeDtypeStruct(q.shape, BF),
            jax.ShapeDtypeStruct((seqs, chips, rows, pair), BF),
            jax.ShapeDtypeStruct(
                (2, down.shape[0] >> halvings_of(down.shape[0], stages), down.shape[1]), BF
            ),
        ],
        in_specs=[vmem, vmem, anywhere, anywhere, anywhere],
        out_specs=[vmem, vmem, anywhere, anywhere],
        scratch_shapes=[
            pltpu.VMEM((2, ring, pair, rows), BF),
            pltpu.VMEM((pair, length), BF),
            pltpu.VMEM((length, pair), BF),
            pltpu.VMEM((length, pair), F32),
            pltpu.VMEM((length, lanes), F32),
            pltpu.VMEM((length, lanes), BF),
            pltpu.VMEM((pair, lanes), BF),
            pltpu.VMEM((pair, lanes), BF),
            pltpu.VMEM((most, width, rows), BF),
            pltpu.VMEM((most, width, rows), BF),
            pltpu.VMEM((most, width, rows), BF),
            pltpu.VMEM((most, width, rows), BF),
            pltpu.VMEM((2, chips, 2, rows, pair), BF),
            pltpu.VMEM((seqs, chips, rows, pair), BF),
            dma((2,)),
            dma((seqs,)),
            dma((2, most)),
            dma((2, most)),
            dma((2, most)),
            dma((2, most)),
            dma((seqs,)),
            dma((seqs,)),
            dma((seqs, chips)),
            dma((seqs, chips)),
            pltpu.VMEM((down.shape[0] // 2, down.shape[1]), BF),
            pltpu.VMEM((up.shape[0] // 2, up.shape[1]), BF),
            pltpu.VMEM((exchange_rows(down.shape[0], stages), down.shape[1]), BF),
            pltpu.VMEM((exchange_rows(up.shape[0], stages), up.shape[1]), BF),
            pltpu.VMEM((HEAD_DIM, lanes), BF),
            dma((4, stages)),
            dma((4, stages)),
            dma((4,)),
            dma((4,)),
        ],
        compiler_params=pltpu.CompilerParams(
            collective_id=2, has_side_effects=True, vmem_limit_bytes=60 * 2**20
        ),
        cost_estimate=pl.CostEstimate(
            flops=12 * tiles * rows * width * length * 4,
            bytes_accessed=8 * q.size,
            transcendentals=tiles * lanes * length // 2,
        ),
        name="attention",
    )(q, g, kv_all, down, up)


def bit_orders(dp, ring):
    seq_bits = [("seq", 1 << b) for b in range(ring.bit_length() - 1)]
    dp_bits = [("dp", 1 << b) for b in range(dp.bit_length() - 1)]
    far = seq_bits[2:]
    return (seq_bits[:2] + dp_bits + far, seq_bits[:1] + dp_bits + seq_bits[1:2] + far)

def side_of(bit):
    axis, weight = bit
    return lax.rem(lax.axis_index(axis) // weight, 2)

def partner_of(bit):
    axis, weight = bit
    me = lax.axis_index(axis)
    return {axis: me + weight - 2 * weight * side_of(bit)}

def add_rows(dst, a, b, dst_at, a_at, rows):
    step = next(n for n in (128, 96, 64, 48, 32, 16) if rows % n == 0)

    def body(i, carry):
        r = pl.multiple_of(i * step, step)
        dst[pl.ds(dst_at + r, step), :] = a[pl.ds(a_at + r, step), :] + b[pl.ds(r, step), :]
        return carry

    lax.fori_loop(0, rows // step, body, 0)


def sum_kernel(orders, spans, x_ref, out_ref, *scratch):
    parts = [(order, i, span) for span in spans for i, order in enumerate(orders)]
    count = len(parts)
    stages = len(orders[0])
    wide = x_ref.shape[1] // len(orders)
    acc, recv = scratch[:count], scratch[count : 2 * count]
    send_sem, recv_sem = scratch[2 * count :]
    barrier = pltpu.get_barrier_semaphore()
    for bit in orders[0]:
        pl.semaphore_signal(barrier, inc=1, device_id=partner_of(bit), device_id_type=MESH)
    pl.semaphore_wait(barrier, stages)

    def copy(p, s, src, dst, bit):
        return pltpu.make_async_remote_copy(
            src_ref=src,
            dst_ref=dst,
            send_sem=send_sem.at[p, s],
            recv_sem=recv_sem.at[p, s],
            device_id=partner_of(bit),
            device_id_type=MESH,
        )

    start = [0] * count
    place = [0] * count
    live = {}

    def size(p, s):
        return parts[p][2][1] // 2 ** min(s + 1, stages - 1)

    def base(p, s):
        return sum(size(p, t) for t in range(s))

    def view(ref, p):
        _, i, (first, rows) = parts[p]
        return ref.at[pl.ds(first, rows), pl.ds(i * wide, wide)]

    def launch(p, s):
        bit = parts[p][0][s]
        half = size(p, s)
        if s < stages - 1:
            other = pl.multiple_of(start[p] + (1 - side_of(bit)) * half, half)
            src = (view(x_ref, p) if s == 0 else acc[p]).at[pl.ds(other, half), :]
        else:
            src = acc[p].at[pl.ds(pl.multiple_of(start[p], half), half), :]
        live[p] = copy(p, s, src, recv[p].at[pl.ds(base(p, s), half), :], bit)
        live[p].start()

    for p in range(count):
        launch(p, 0)
    for s in range(stages):
        for p in range(count):
            side = side_of(parts[p][0][s])
            live[p].wait()
            half = size(p, s)
            got = recv[p].at[pl.ds(base(p, s), half), :]
            if s == 0:
                place[p] = side * half
                add_rows(acc[p], view(x_ref, p), got, 0, pl.multiple_of(side * half, half), half)
            elif s < stages - 1:
                mine = pl.multiple_of(start[p] + side * half, half)
                add_rows(acc[p], acc[p], got, mine, mine, half)
                place[p] = place[p] + side * half
                start[p] = start[p] + side * half
            else:
                at = pl.multiple_of(start[p], half)
                add_rows(view(out_ref, p), acc[p], got, pl.multiple_of(place[p], half), at, half)
            if s < stages - 1:
                launch(p, s + 1)

    def spread(p, s):
        half = size(p, s)
        src = view(out_ref, p).at[pl.ds(pl.multiple_of(place[p], half), half), :]
        live[p] = copy(p, 2 * stages - 2 - s, src, src, parts[p][0][s])
        live[p].start()

    for p in range(count):
        spread(p, stages - 2)
    for s in range(stages - 2, -1, -1):
        for p in range(count):
            live[p].wait()
            place[p] = place[p] - side_of(parts[p][0][s]) * size(p, s)
            if s:
                spread(p, s - 1)


def total_of(x, dp, ring, collective_id):
    orders = bit_orders(dp, ring)
    rows, cols = x.shape
    stages = len(orders[0])
    unit = 16 << (stages - 1)
    first = -(-rows // unit // 2) * unit
    spans = [(0, first), (first, rows - first)]
    wide = cols // len(orders)
    heights = [span[1] for span in spans for _ in orders]
    whole = pl.BlockSpec(memory_space=pltpu.VMEM)
    return pl.pallas_call(
        functools.partial(sum_kernel, orders, spans),
        out_shape=jax.ShapeDtypeStruct(x.shape, BF),
        in_specs=[whole],
        out_specs=whole,
        scratch_shapes=[pltpu.VMEM((h // 2, wide), BF) for h in heights]
        + [
            pltpu.VMEM((sum(h // 2 ** min(s + 1, stages - 1) for s in range(stages)), wide), BF)
            for h in heights
        ]
        + [pltpu.SemaphoreType.DMA((len(heights), 2 * stages - 1))] * 2,
        compiler_params=pltpu.CompilerParams(
            collective_id=collective_id, has_side_effects=True, vmem_limit_bytes=40 * 2**20
        ),
        name="total",
    )(x)


def normal(h):
    center = h - jnp.mean(h, axis=-1, keepdims=True)
    spread = jnp.mean(center * center, axis=-1, keepdims=True)
    inverse = lax.rsqrt(spread + 1e-05)
    return center * inverse, inverse


def norm_gradient(q, gain, n, inverse):
    scaled = q * gain
    inner = jnp.mean(scaled * n, axis=-1, keepdims=True)
    return inverse * (scaled - jnp.mean(scaled, axis=-1, keepdims=True) - n * inner)


def turned_back(rows, cosine, sine):
    half = cosine.shape[0]
    first, second = rows[:half], rows[half : 2 * half]
    return jnp.concatenate(
        [first * cosine + second * sine, second * cosine - first * sine, rows[2 * half :]], axis=0
    )


def finish_kernel(
    att_ref,
    dq_ref,
    slot_ref,
    cos_ref,
    sin_ref,
    h_ref,
    c_ref,
    ff_ref,
    gm_ref,
    norms_ref,
    weight_ref,
    out_weight_ref,
    up_bias_ref,
    layer_ref,
    input_ref,
    rest_ref,
    raw_ref,
    acc_ref,
    lines_ref,
):
    step = pl.program_id(0)
    d = h_ref.shape[1]
    rows = h_ref.shape[0]
    wide = weight_ref.shape[1]

    @pl.when(step == 0)
    def _():
        acc_ref[...] = jnp.zeros_like(acc_ref)
        lines_ref[...] = jnp.zeros_like(lines_ref)
        for i in range(up_bias_ref.shape[1] // d):
            lines_ref[8 + i : 9 + i, :] = up_bias_ref[:, i * d : (i + 1) * d]

    hidden = h_ref[...].astype(F32)
    low_c = c_ref[...]
    cot = low_c.astype(F32)
    n, inverse = normal(hidden)
    gain1, bias1 = norms_ref[0:1, :], norms_ref[1:2, :]
    gain2, bias_out = norms_ref[2:3, :], norms_ref[3:4, :]
    normed = (n * gain1 + bias1).astype(BF)
    att = att_ref[0]
    layer_ref[...] = hidden + dot(att, out_weight_ref[...], 0, 0) + ff_ref[...] + bias_out
    acc_ref[wide : wide + d, :] += dot(att, low_c, 1, 0)
    cosine, sine = cos_ref[0], sin_ref[0]
    for h in range(d // HEAD_DIM):
        at = slice(h * HEAD_DIM, (h + 1) * HEAD_DIM)
        raw_ref[at, :] = turned_back(dq_ref[0, at, :].astype(F32), cosine, sine).astype(BF)
    kv = slot_ref[0, 0].astype(F32)
    for m in range(1, slot_ref.shape[1]):
        kv = kv + slot_ref[0, m].astype(F32)
    lane = lax.broadcasted_iota(jnp.int32, (1, 2 * HEAD_DIM), 1)
    kv = (kv * jnp.where(lane < HEAD_DIM, 1.0 / LOG2E, 1.0)).astype(BF).astype(F32).T
    raw_ref[d : d + HEAD_DIM, :] = turned_back(kv[:HEAD_DIM], cosine, sine).astype(BF)
    raw_ref[d + HEAD_DIM :, :] = kv[HEAD_DIM:].astype(BF)
    raw = raw_ref[...]
    acc_ref[0:wide, :] += dot(raw, normed, 1, 0)
    sums = dot(jnp.ones((8, rows), BF), raw, 1, 1)
    lines_ref[4:5, :] += sums[0:1, :d]
    lines_ref[5:6, 0 : wide - d] += sums[0:1, d:]
    ga = dot(raw, weight_ref[...], 0, 1)
    gm = gm_ref[...]
    lines_ref[0:1, :] += jnp.sum(ga * n, axis=0, keepdims=True)
    lines_ref[1:2, :] += jnp.sum(ga, axis=0, keepdims=True)
    lines_ref[2:3, :] += jnp.sum(gm * n, axis=0, keepdims=True)
    lines_ref[3:4, :] += jnp.sum(gm, axis=0, keepdims=True)
    lines_ref[6:7, :] += jnp.sum(cot, axis=0, keepdims=True)
    input_ref[...] = (
        cot + norm_gradient(ga, gain1, n, inverse) + norm_gradient(gm, gain2, n, inverse)
    )

    @pl.when(step == pl.num_programs(0) - 1)
    def _():
        rest_ref[0:d, :] = acc_ref[0:d, :].T.astype(BF)
        rest_ref[d : 2 * d, :] = acc_ref[wide : wide + d, :].astype(BF)
        rest_ref[2 * d : d + wide, :] = acc_ref[d:wide, :].astype(BF)
        rest_ref[d + wide : d + wide + 16, :] = lines_ref[...].astype(BF)
        rest_ref[d + wide + 16 :, :] = jnp.zeros((rest_ref.shape[0] - d - wide - 16, d), BF)


def finish(att, dq, slots, cosine, sine, hidden, cot, ff, gm, norms, weight, out_weight, up_bias, padded):
    seqs, d, rows = att.shape
    wide = weight.shape[1]
    by_seq = pl.BlockSpec((1, d, rows), lambda i: (i, 0, 0))
    angle = pl.BlockSpec((1,) + cosine.shape[1:], lambda i: (i, 0, 0))
    by_row = pl.BlockSpec((rows, d), lambda i: (i, 0))

    def all_of(a):
        return pl.BlockSpec(a.shape, lambda i: (0,) * a.ndim)

    return pl.pallas_call(
        finish_kernel,
        grid=(seqs,),
        out_shape=[
            jax.ShapeDtypeStruct(hidden.shape, F32),
            jax.ShapeDtypeStruct(hidden.shape, F32),
            jax.ShapeDtypeStruct((padded, d), BF),
        ],
        in_specs=[
            by_seq,
            by_seq,
            pl.BlockSpec((1,) + slots.shape[1:], lambda i: (i, 0, 0, 0)),
            angle,
            angle,
            by_row,
            by_row,
            by_row,
            by_row,
            all_of(norms),
            all_of(weight),
            all_of(out_weight),
            all_of(up_bias),
        ],
        out_specs=[by_row, by_row, pl.BlockSpec((padded, d), lambda i: (0, 0))],
        scratch_shapes=[
            pltpu.VMEM((wide, rows), BF),
            pltpu.VMEM((wide + d, d), F32),
            pltpu.VMEM((16, d), F32),
        ],
        compiler_params=pltpu.CompilerParams(vmem_limit_bytes=48 * 2**20),
        cost_estimate=pl.CostEstimate(
            flops=12 * seqs * rows * d * d, bytes_accessed=26 * seqs * rows * d, transcendentals=0
        ),
        name="finish",
    )(att, dq, slots, cosine, sine, hidden, cot, ff, gm, norms, weight, out_weight, up_bias)


def local(
    hidden_in,
    positions,
    ln1_gain,
    ln1_bias,
    ln2_gain,
    ln2_bias,
    query_projection,
    query_bias,
    shared_key_weight,
    shared_key_bias,
    shared_value_weight,
    shared_value_bias,
    output_weight,
    output_bias,
    up_weight,
    up_bias,
    down_weight,
    down_bias,
    cotangent,
):
    seq_count, local_len = hidden_in.shape[0], hidden_in.shape[1]
    ring = lax.axis_size("seq")
    groups = ring // seq_count
    per_group = HEADS // groups
    width = per_group * HEAD_DIM
    hidden = hidden_in.astype(F32)
    cosine, sine = angles_of(positions)
    normed_a = layer_norm(hidden, ln1_gain, ln1_bias).astype(BF)
    normed_m = layer_norm(hidden, ln2_gain, ln2_bias).astype(BF)

    tokens = seq_count * local_len
    kv_weight = jnp.concatenate([shared_key_weight, shared_value_weight], axis=1)
    kv_bias = jnp.concatenate([shared_key_bias, shared_value_bias])
    kv_pre = jnp.einsum("stc,cw->swt", normed_a, kv_weight, preferred_element_type=F32)
    kv_pre = kv_pre + kv_bias[:, None]
    kv_low = jnp.concatenate(
        [rotary_rows(kv_pre[:, :HEAD_DIM], cosine, sine), kv_pre[:, HEAD_DIM:]], axis=1
    ).astype(BF)
    kv_all = lax.all_gather(kv_low.reshape(-1, local_len), "seq")
    query_pre = jnp.einsum("stc,cw->swt", normed_a, query_projection, preferred_element_type=F32)
    query_pre = (query_pre + query_bias[:, None]).reshape(seq_count, HEADS, HEAD_DIM, local_len)
    query_low = (rotary_rows(query_pre, cosine[:, None], sine[:, None]) * (LOG2E / 8.0)).astype(BF)
    query_tiles = query_low.reshape(-1, width, local_len)
    grad_attended = jnp.einsum(
        "stc,wc->swt", cotangent, output_weight, preferred_element_type=F32
    ).astype(BF)
    grad_tiles = grad_attended.reshape(-1, width, local_len)

    feedforward, grad_normed_m, grad_w_up, grad_w_down, grad_b_up = feed_forward(
        normed_m.reshape(tokens, D),
        cotangent.reshape(tokens, D),
        up_weight,
        up_bias[None],
        down_weight,
    )
    query_tiles, grad_tiles, kv_all, grad_w_up, grad_w_down = lax.optimization_barrier(
        (query_tiles, grad_tiles, kv_all, grad_w_up, grad_w_down)
    )
    dp = lax.axis_size("dp")
    orders = bit_orders(dp, ring)
    out, dq, dkv, parts = attention(
        query_tiles, grad_tiles, kv_all, grad_w_down, grad_w_up, seq_count, dp
    )
    grad_w_down, grad_w_up = unpack(
        parts, down_weight.shape, up_weight.shape, orders, dp, ring
    )
    qkv = D + 2 * HEAD_DIM
    ff = up_weight.shape[1]
    unit = 16 * dp * ring // 2
    padded = -(-(D + qkv + 16) // unit) * unit
    norms = jnp.concatenate(
        [ln1_gain[None], ln1_bias[None], ln2_gain[None], (output_bias + down_bias)[None]]
        + [jnp.zeros((4, D), F32)],
        axis=0,
    )
    layer_out, input_grad, rest = finish(
        out.reshape(seq_count, D, local_len),
        dq.reshape(seq_count, D, local_len),
        dkv,
        cosine,
        sine,
        hidden_in.reshape(tokens, D),
        cotangent.reshape(tokens, D),
        feedforward,
        grad_normed_m,
        norms,
        jnp.concatenate([query_projection, kv_weight], axis=1),
        output_weight,
        grad_b_up,
        padded,
    )
    rest = total_of(rest, dp, ring, 3)
    kv_rows = rest[2 * D : D + qkv].astype(F32)
    lines = rest[D + qkv : D + qkv + 16].astype(F32)
    return (
        layer_out.reshape(hidden.shape),
        input_grad.reshape(hidden.shape),
        lines[0],
        lines[1],
        lines[2],
        lines[3],
        rest[:D].astype(F32),
        lines[4],
        kv_rows[:HEAD_DIM].T,
        lines[5, :HEAD_DIM],
        kv_rows[HEAD_DIM:].T,
        lines[5, HEAD_DIM : 2 * HEAD_DIM],
        rest[D : 2 * D].astype(F32),
        lines[6],
        grad_w_up,
        lines[8 : 8 + ff // D].reshape(ff),
        grad_w_down,
        lines[6],
    )


def solution(mesh):
    rows = P("dp", "seq", None)
    placed = (rows, P("dp", "seq")) + (P(),) * 16 + (rows,)
    return jax.shard_map(
        local,
        mesh=mesh,
        in_specs=placed,
        out_specs=(rows, rows) + (P(),) * 16,
        check_vma=False,
    )
```

```python
import functools
import math

import jax
import jax.numpy as jnp
from jax import lax
from jax.experimental import pallas as pl
from jax.experimental.pallas import tpu as pltpu
from jax.sharding import PartitionSpec as P

D = 768
HEADS = 12
HEAD_DIM = 64
ROT_DIMS = 16
BF = jnp.bfloat16
F32 = jnp.float32
LOG2E = math.log2(math.e)


def layer_norm(values, gain, bias):
    center = values - jnp.mean(values, axis=-1, keepdims=True)
    spread = jnp.mean(center * center, axis=-1, keepdims=True)
    return center * lax.rsqrt(spread + 1e-05) * gain + bias


def rotary_rows(values, cosine, sine):
    half = cosine.shape[-2]
    first, second = values[..., :half, :], values[..., half : 2 * half, :]
    return jnp.concatenate(
        [first * cosine - second * sine, second * cosine + first * sine, values[..., 2 * half :, :]],
        axis=-2,
    )


def angles_of(positions):
    half = ROT_DIMS // 2
    frequency = jnp.exp(
        jnp.arange(half).astype(F32) * (-2.0 * math.log(10000.0) / ROT_DIMS)
    )
    angle = positions.astype(F32)[:, None, :] * frequency[None, :, None]
    return jnp.cos(angle), jnp.sin(angle)


MESH = pl.DeviceIdType.MESH


def dot(a, b, ca, cb):
    return lax.dot_general(a, b, (((ca,), (cb,)), ((), ())), preferred_element_type=F32)


def flip(index, weight):
    return index + weight - 2 * weight * lax.rem(index // weight, 2)


def gelu_parts(u):
    e = jnp.exp(u * u * -0.5)
    t = 1.0 / (1.0 + (0.3275911 / math.sqrt(2.0)) * jnp.abs(u))
    poly = t * (
        0.5 * 0.254829592
        + t
        * (
            0.5 * -0.284496736
            + t * (0.5 * 1.421413741 + t * (0.5 * -1.453152027 + t * (0.5 * 1.061405429)))
        )
    )
    tail = poly * e
    return jnp.where(u >= 0, 1.0 - tail, tail), e * (1.0 / math.sqrt(2.0 * math.pi))


def feed_kernel(
    x_ref,
    c_ref,
    up_ref,
    down_ref,
    bias_ref,
    ff_ref,
    gx_ref,
    gup_ref,
    gdown_ref,
    gbias_ref,
    act_ref,
    grad_ref,
):
    tokens = x_ref.shape[0]
    bias = bias_ref[...]
    sub = min(256, tokens)
    for r in range(0, tokens, sub):
        u = dot(x_ref[r : r + sub, :], up_ref[...], 1, 0) + bias
        share, density = gelu_parts(u)
        act_ref[r : r + sub, :] = (u * share).astype(BF)
        da = dot(c_ref[r : r + sub, :], down_ref[...], 1, 1)
        grad_ref[r : r + sub, :] = (da * (share + u * density)).astype(BF)

    @pl.when(pl.program_id(0) == 0)
    def _():
        ff_ref[...] = jnp.zeros_like(ff_ref)
        gx_ref[...] = jnp.zeros_like(gx_ref)

    act, grad = act_ref[...], grad_ref[...]
    ff_ref[...] += dot(act, down_ref[...], 1, 0)
    gx_ref[...] += dot(grad, up_ref[...], 1, 1)
    gdown_ref[...] = dot(act, c_ref[...], 0, 0).astype(BF)
    gup_ref[...] = dot(x_ref[...], grad, 0, 0).astype(BF)
    gbias_ref[...] = jnp.sum(grad.astype(F32), axis=0, keepdims=True)


def feed_forward(x, cot, up_weight, up_bias, down_weight):
    tokens, d = x.shape
    ff = up_weight.shape[1]
    wide = d
    steps = ff // wide
    whole = pl.BlockSpec((tokens, d), lambda i: (0, 0))
    by_column = pl.BlockSpec((d, wide), lambda i: (0, i))
    by_row = pl.BlockSpec((wide, d), lambda i: (i, 0))
    line = pl.BlockSpec((1, wide), lambda i: (0, i))
    return pl.pallas_call(
        feed_kernel,
        grid=(steps,),
        out_shape=[
            jax.ShapeDtypeStruct((tokens, d), F32),
            jax.ShapeDtypeStruct((tokens, d), F32),
            jax.ShapeDtypeStruct((ff, d), BF),
            jax.ShapeDtypeStruct((ff, d), BF),
            jax.ShapeDtypeStruct((1, ff), F32),
        ],
        in_specs=[whole, whole, by_column, by_row, line],
        out_specs=[whole, whole, pl.BlockSpec((d, wide), lambda i: (i, 0)), by_row, line],
        scratch_shapes=[pltpu.VMEM((tokens, wide), BF), pltpu.VMEM((tokens, wide), BF)],
        compiler_params=pltpu.CompilerParams(vmem_limit_bytes=56 * 2**20),
        cost_estimate=pl.CostEstimate(
            flops=12 * tokens * d * ff,
            bytes_accessed=16 * d * ff,
            transcendentals=tokens * ff,
        ),
        name="feed_forward",
    )(x, cot, up_weight, down_weight, up_bias)


KEYS = 256


def shipped(upper_index, ring, tiles):
    more = upper_index + 2
    return (tiles * (2 * upper_index + 1 - ring) + more) // (2 * more)


class Exchange:
    def __init__(self, index, order, array, out, acc, recv, first, wide, sems):
        self.index, self.order, self.sems = index, order, sems
        self.array, self.out, self.acc, self.recv = array, out, acc, recv
        self.columns = pl.ds(first, wide)
        self.rows = array.shape[0]
        self.halvings = halvings_of(self.rows, len(order))
        self.waits = len(order)

    def size(self, s):
        return self.rows >> min(s, self.halvings)

    def base(self, s):
        return sum(self.size(t + 1) for t in range(s))

    def start(self, s, first=1):
        at = 0
        for t in range(first, min(s, self.halvings)):
            at = at + side_of(self.order[t]) * self.size(t + 1)
        return at

    def copy(self, k):
        bit = self.order[k]
        size = self.size(k + 1)
        other = self.start(k) + ((1 - side_of(bit)) * size if k < self.halvings else 0)
        rows = pl.ds(pl.multiple_of(other, size), size)
        src = (self.array if k == 0 else self.acc).at[rows, self.columns]
        dst = self.recv.at[pl.ds(self.base(k), size), self.columns]
        return pltpu.make_async_remote_copy(
            src_ref=src,
            dst_ref=dst,
            send_sem=self.sems[0].at[self.index, k],
            recv_sem=self.sems[1].at[self.index, k],
            device_id=partner_of(bit),
            device_id_type=MESH,
        )

    def fill(self):
        half = self.size(1)
        rows = pl.ds(pl.multiple_of(side_of(self.order[0]) * half, half), half)
        return pltpu.make_async_copy(
            self.array.at[rows, self.columns],
            self.acc.at[:, self.columns],
            self.sems[2].at[self.index],
        )

    def empty(self):
        size = self.size(self.halvings)
        rows = pl.ds(pl.multiple_of(self.start(self.halvings), size), size)
        return pltpu.make_async_copy(
            self.acc.at[rows, self.columns],
            self.out.at[:, self.columns],
            self.sems[3].at[self.index],
        )

    def begin(self):
        self.fill().start()
        self.copy(0).start()

    def take(self, k):
        self.copy(k).wait()
        if k == 0:
            self.fill().wait()
        size = self.size(k + 1)
        start = self.start(k + 1)
        step = next(n for n in (128, 96, 64, 48, 32, 16) if size % n == 0)
        base = self.base(k)

        def add(i, carry):
            r = pl.multiple_of(i * step, step)
            mine = pl.ds(pl.multiple_of(start + r, step), step)
            self.acc[mine, self.columns] = (
                self.acc[mine, self.columns] + self.recv[pl.ds(base + r, step), self.columns]
            )
            return carry

        lax.fori_loop(0, size // step, add, 0)
        if k == len(self.order) - 1:
            self.empty().start()
            self.empty().wait()
        if k + 1 < self.waits:
            self.copy(k + 1).start()


def owners(rows, order, dp, ring):
    halved = order[: halvings_of(rows, len(order))]
    found = []
    for segment in range(1 << len(halved)):
        place = {"dp": 0, "seq": 0}
        for t, (axis, weight) in enumerate(halved):
            place[axis] += weight * (segment >> (len(halved) - 1 - t) & 1)
        found.append(place["dp"] * ring + place["seq"])
    return found


def unpack_kernel(froms, all_ref, down_out, up_out, low, wide, come_sem, sent_sem):
    count = len(froms[0])
    tall, across = all_ref.shape[2:]
    come = [
        [
            pltpu.make_async_copy(all_ref.at[d, a], low.at[a, i], come_sem.at[a, i])
            for i, d in enumerate(froms[a])
        ]
        for a in range(2)
    ]
    for copy in come[0] + come[1]:
        copy.start()
    gone = []
    for a in range(2):
        for i in range(count):
            come[a][i].wait()
            wide[a, i] = low[a, i].astype(F32)
            at = i * tall
            if a == 0:
                to = down_out.at[pl.ds(at, tall), :]
            else:
                block = at // across
                to = up_out.at[pl.ds(at - block * across, tall), pl.ds(block * across, across)]
            gone.append(pltpu.make_async_copy(wide.at[a, i], to, sent_sem.at[a, i]))
            gone[-1].start()
    for copy in gone:
        copy.wait()


def unpack(parts, down_shape, up_shape, orders, dp, ring):
    everyone = lax.all_gather(parts, ("dp", "seq"))
    froms = [owners(down_shape[0], order, dp, ring) for order in orders]
    anywhere = pl.BlockSpec(memory_space=pl.ANY)
    dma = pltpu.SemaphoreType.DMA
    size = down_shape[0] * down_shape[1]
    count = len(froms[0])
    return pl.pallas_call(
        functools.partial(unpack_kernel, froms),
        out_shape=[jax.ShapeDtypeStruct(down_shape, F32), jax.ShapeDtypeStruct(up_shape, F32)],
        in_specs=[anywhere],
        out_specs=[anywhere] * 2,
        scratch_shapes=[
            pltpu.VMEM((2, count) + parts.shape[1:], BF),
            pltpu.VMEM((2, count) + parts.shape[1:], F32),
            dma((2, count)),
            dma((2, count)),
        ],
        compiler_params=pltpu.CompilerParams(vmem_limit_bytes=48 * 2**20),
        cost_estimate=pl.CostEstimate(flops=4 * size, bytes_accessed=12 * size, transcendentals=0),
        name="unpack",
    )(everyone)


def halvings_of(rows, stages):
    count = 0
    while count < stages and rows % (32 << count) == 0:
        count += 1
    return count


def exchange_rows(rows, stages):
    count = halvings_of(rows, stages)
    return sum(rows >> min(s + 1, count) for s in range(stages))


def attention_kernel(
    seqs,
    groups,
    orders,
    q_ref,
    g_ref,
    all_ref,
    down_ref,
    up_ref,
    att_ref,
    dq_ref,
    slot_ref,
    sum_ref,
    kvt_ref,
    flat_ref,
    rows_ref,
    dkv_ref,
    s_ref,
    p_ref,
    qs_ref,
    gs_ref,
    qin_ref,
    gin_ref,
    atts_ref,
    dqs_ref,
    stage_ref,
    half_ref,
    load_sem,
    own_sem,
    in_send,
    in_recv,
    out_send,
    out_recv,
    core_send,
    core_recv,
    slot_send,
    slot_recv,
    down_acc_ref,
    up_acc_ref,
    down_recv_ref,
    up_recv_ref,
    graw_ref,
    sum_send,
    sum_recv,
    fill_sem,
    empty_sem,
):
    tiles, width, rows = q_ref.shape
    ring = all_ref.shape[0]
    chips = ring // 2
    heads = width // HEAD_DIM
    lanes = heads * rows
    length = ring * rows
    me = lax.axis_index("seq")
    chip, core = me // 2, lax.rem(me, 2)
    upper = me // chips
    partner = ring - 1 - me
    count = shipped(me + (1 - upper) * (partner - me), ring, tiles)

    def to(index):
        return {"seq": index}

    barrier = pltpu.get_barrier_semaphore()

    def greet(index):
        pl.semaphore_signal(barrier, inc=1, device_id=to(index), device_id_type=MESH)

    greet(partner)
    greet(flip(me, 1))
    for m in range(1, chips):
        greet(lax.rem(me + 2 * m, ring))
    across = [bit for bit in orders[0] if bit[0] == "dp"]
    for bit in across:
        pl.semaphore_signal(
            barrier, inc=1, device_id=partner_of(bit), device_id_type=MESH
        )
    pl.semaphore_wait(barrier, chips + 1 + len(across))

    def load(s, slot):
        return pltpu.make_async_copy(
            all_ref.at[:, pl.ds(pl.multiple_of(s * 2 * HEAD_DIM, 2 * HEAD_DIM), 2 * HEAD_DIM), :],
            kvt_ref.at[slot],
            load_sem.at[slot],
        )

    load(0, 0).start()

    def place(k):
        return lax.rem(k, seqs) * groups + k // seqs

    def remote(src, dst, sems, which, k, index):
        return pltpu.make_async_remote_copy(
            src_ref=src,
            dst_ref=dst,
            send_sem=sems[0].at[which, k],
            recv_sem=sems[1].at[which, k],
            device_id=to(index),
            device_id_type=MESH,
        )

    def q_in(k):
        return remote(q_ref.at[place(k)], qin_ref.at[k], (in_send, in_recv), 0, k, partner)

    def g_in(k):
        return remote(g_ref.at[place(k)], gin_ref.at[k], (in_send, in_recv), 1, k, partner)

    def att_out(k):
        return remote(atts_ref.at[k], att_ref.at[place(k)], (out_send, out_recv), 0, k, partner)

    def dq_out(k):
        return remote(dqs_ref.at[k], dq_ref.at[place(k)], (out_send, out_recv), 1, k, partner)

    def given_of(s):
        return (count - s + seqs - 1) // seqs

    def start_in(s):
        def one(i, carry):
            q_in(i * seqs + s).start()
            g_in(i * seqs + s).start()
            return carry

        lax.fori_loop(0, upper * given_of(s), one, 0)

    start_in(0)

    sems = (sum_send, sum_recv, fill_sem, empty_sem)
    half_down, half_up = down_ref.shape[1] // 2, up_ref.shape[1] // 2
    teams = []
    for i in range(2):
        teams.append(
            [
                Exchange(
                    2 * i, orders[0], down_ref, sum_ref.at[0], down_acc_ref, down_recv_ref,
                    i * half_down, half_down, sems,
                ),
                Exchange(
                    2 * i + 1, orders[1], up_ref, sum_ref.at[1], up_acc_ref, up_recv_ref,
                    i * half_up, half_up, sems,
                ),
            ]
        )
    most_waits = [max(e.waits for e in team) for team in teams]
    planned = ((10, 40, 58, 72, 86), (18, 58, 76, 90, 101))
    acts = []
    for i in range(2):
        for k in range(most_waits[i]):
            acts.append((planned[i][min(k, 4)] + max(0, k - 4), i, k))
    acts.sort()
    dues = [due for due, _, _ in acts]
    acts = [(i, k) for _, i, k in acts]
    for team in teams:
        for e in team:
            e.begin()

    def act(number, carry):
        for n, (i, k) in enumerate(acts):
            def run(i=i, k=k):
                for e in teams[i]:
                    if k < e.waits:
                        e.take(k)

            pl.when(number == n)(run)
        return carry

    def cost_of(position):
        return position * rows // KEYS + 2

    total_cost = (tiles - upper * count) * cost_of(me) + (1 - upper) * count * cost_of(partner)

    def advance(acted, progress):
        due = sum(jnp.where(progress * 100 >= at * total_cost, 1, 0) for at in dues)
        lax.fori_loop(acted, due, act, 0)
        return jnp.maximum(acted, due)

    def core_out(s):
        return pltpu.make_async_remote_copy(
            src_ref=stage_ref.at[lax.rem(s, 2), :, 1 - core],
            dst_ref=half_ref.at[s],
            send_sem=core_send.at[s],
            recv_sem=core_recv.at[s],
            device_id=to(flip(me, 1)),
            device_id_type=MESH,
        )

    def slot_out(s, m):
        target = lax.rem(chip + m, chips)
        return pltpu.make_async_remote_copy(
            src_ref=half_ref.at[s, target],
            dst_ref=slot_ref.at[s, m],
            send_sem=slot_send.at[s, m],
            recv_sem=slot_recv.at[s, m],
            device_id=to(2 * target + core),
            device_id_type=MESH,
        )

    def slot_own(s):
        return pltpu.make_async_copy(half_ref.at[s, chip], slot_ref.at[s, 0], own_sem.at[s])

    def pass_on(s):
        core_out(s).wait()

        def add(m, carry):
            half_ref[s, m] = (
                half_ref[s, m].astype(F32) + stage_ref[lax.rem(s, 2), m, core].astype(F32)
            ).astype(BF)
            return carry

        lax.fori_loop(0, chips, add, 0)
        slot_own(s).start()
        for m in range(1, chips):
            slot_out(s, m).start()

    qs_ref[...] = jnp.zeros_like(qs_ref)
    gs_ref[...] = jnp.zeros_like(gs_ref)

    def at(b, n=1):
        return pl.ds(pl.multiple_of(b * KEYS, KEYS), n * KEYS)

    def blocks(count_blocks, body, state):
        state = lax.fori_loop(0, count_blocks // 4, lambda i, c: body(4 * i, 4, c), state)
        pairs = count_blocks // 2
        state = lax.fori_loop(
            count_blocks // 4 * 2, pairs, lambda i, c: body(2 * i, 2, c), state
        )
        return lax.fori_loop(2 * pairs, count_blocks, lambda i, c: body(i, 1, c), state)

    def spread(tile, out):
        for h in range(heads):
            tile[h * HEAD_DIM : (h + 1) * HEAD_DIM, :] = out[:, h * rows : (h + 1) * rows].astype(
                BF
            )

    def gather(tile, out):
        for h in range(heads):
            out[0:HEAD_DIM, h * rows : (h + 1) * rows] = tile[
                h * HEAD_DIM : (h + 1) * HEAD_DIM, :
            ]

    def tile(mine, t, k, position, acted, progress):
        start = position * rows
        edge = start // KEYS
        shift = lax.rem(start, KEYS)
        other = jnp.logical_not(mine)

        @pl.when(mine)
        def _():
            gather(q_ref.at[t], qs_ref)
            gather(g_ref.at[t], graw_ref)

        @pl.when(other)
        def _():
            q_in(k).wait_recv()
            g_in(k).wait_recv()
            gather(qin_ref.at[k], qs_ref)
            gather(gin_ref.at[k], graw_ref)

        s = dot(rows_ref[at(edge), :], qs_ref[...], 1, 0)
        column = lax.rem(lax.broadcasted_iota(jnp.int32, (1, lanes), 1), rows) + shift
        keep = lax.broadcasted_iota(jnp.int32, (KEYS, lanes), 0) <= column
        s = jnp.where(keep, s, -1e30)
        s_ref[at(edge), :] = s

        def top_of(s, n):
            return jnp.max(s.reshape(n * KEYS // 8, 8, lanes), axis=0)

        def scores(b, n, top):
            s = dot(rows_ref[at(b, n), :], qs_ref[...], 1, 0)
            s_ref[at(b, n), :] = s
            return jnp.maximum(top, top_of(s, n))

        top = jnp.max(blocks(edge, scores, top_of(s, 1)), axis=0, keepdims=True)

        def forward(b, n, state):
            total, out = state
            p = jnp.exp2(s_ref[at(b, n), :] - top)
            low = p.astype(BF)
            p_ref[at(b, n), :] = low
            return (
                total + jnp.sum(p.reshape(n * KEYS // 8, 8, lanes), axis=0),
                out + dot(flat_ref[HEAD_DIM : 2 * HEAD_DIM, at(b, n)], low, 1, 0),
            )

        total, out = blocks(
            edge + 1, forward, (jnp.zeros((8, lanes), F32), jnp.zeros((HEAD_DIM, lanes), F32))
        )
        inverse = 1.0 / jnp.sum(total, axis=0, keepdims=True)
        out = out * inverse
        pl.when(mine)(lambda: spread(att_ref.at[t], out))

        @pl.when(other)
        def _():
            spread(atts_ref.at[k], out)
            att_out(k).start()

        acted = advance(acted, progress + (edge + 2) // 2)
        g = graw_ref[...]
        scaled = (g.astype(F32) * inverse).astype(BF)
        gs_ref[HEAD_DIM : 2 * HEAD_DIM, :] = scaled
        delta = jnp.sum(scaled.astype(F32) * out, axis=0, keepdims=True)

        def backward(b, n, dq):
            p = p_ref[at(b, n), :]
            dp = dot(rows_ref[at(b, n), :], gs_ref[...], 1, 0)
            ds = (p.astype(F32) * (dp - delta)).astype(BF)
            dkv_ref[at(b, n), :] += dot(p, gs_ref[...], 1, 1) + dot(ds, qs_ref[...], 1, 1)
            return dq + dot(flat_ref[0:HEAD_DIM, at(b, n)], ds, 1, 0)

        dq = blocks(edge + 1, backward, jnp.zeros((HEAD_DIM, lanes), F32))
        dq = dq * (HEAD_DIM**-0.5)
        pl.when(mine)(lambda: spread(dq_ref.at[t], dq))

        @pl.when(other)
        def _():
            spread(dqs_ref.at[k], dq)
            dq_out(k).start()

        progress = progress + edge + 2
        return advance(acted, progress), progress

    per_block = KEYS // rows

    def sequence(s, state):
        slot = lax.rem(s, 2)
        load(s, slot).wait()
        pl.when(s + 1 < seqs)(lambda: load(s + 1, 1 - slot).start())
        dkv_ref[...] = jnp.zeros_like(dkv_ref)

        def turn(b, c):
            wide = jnp.concatenate(
                [kvt_ref[slot, b * per_block + i] for i in range(per_block)], axis=1
            )
            flat_ref[:, at(b)] = wide
            rows_ref[at(b), :] = wide.T
            return c

        lax.fori_loop(0, length // KEYS, turn, 0)
        pl.when(s + 1 < seqs)(lambda: start_in(s + 1))
        given = given_of(s)
        own = groups - upper * given
        taken = (1 - upper) * given
        later = jnp.minimum(s, 1)

        def work(u, state):
            acted, progress = state
            v = u - taken * later
            mine = (v >= 0) & (v < own)
            t = s * groups + upper * given + jnp.clip(v, 0, own - 1)
            k = jnp.clip(u - own * (1 - later), 0, jnp.maximum(taken - 1, 0)) * seqs + s
            position = jnp.where(mine, me, partner)
            state = tile(mine, t, k, position, acted, progress)
            pl.when((u == 0) & (s > 0))(lambda: pass_on(s - 1))
            return state

        state = lax.fori_loop(0, own + taken, work, state)
        stage_ref[slot] = dkv_ref[...].reshape(chips, 2, rows, 2 * HEAD_DIM).astype(BF)
        core_out(s).start()
        return state

    acted, _ = lax.fori_loop(0, seqs, sequence, (jnp.int32(0), jnp.int32(0)))
    pass_on(seqs - 1)
    lax.fori_loop(acted, len(acts), act, 0)

    def end_given(k, c):
        q_in(k).wait_send()
        g_in(k).wait_send()
        att_out(k).wait_recv()
        dq_out(k).wait_recv()
        return c

    def end_taken(k, c):
        att_out(k).wait_send()
        dq_out(k).wait_send()
        return c

    lax.fori_loop(0, count * upper, end_given, 0)
    lax.fori_loop(0, count * (1 - upper), end_taken, 0)

    def end(s, c):
        slot_own(s).wait()
        for m in range(1, chips):
            slot_out(s, m).wait()
        return c

    lax.fori_loop(0, seqs, end, 0)


def attention(q, g, kv_all, down, up, seqs, dp):
    tiles, width, rows = q.shape
    ring = kv_all.shape[0]
    chips = ring // 2
    length = ring * rows
    lanes = width // HEAD_DIM * rows
    most = max(shipped(i, ring, tiles) for i in range(chips, ring))
    vmem = pl.BlockSpec(memory_space=pltpu.VMEM)
    anywhere = pl.BlockSpec(memory_space=pl.ANY)
    pair = 2 * HEAD_DIM
    dma = pltpu.SemaphoreType.DMA
    orders = bit_orders(dp, ring)
    stages = len(orders[0])
    return pl.pallas_call(
        functools.partial(attention_kernel, seqs, tiles // seqs, orders),
        out_shape=[
            jax.ShapeDtypeStruct(q.shape, BF),
            jax.ShapeDtypeStruct(q.shape, BF),
            jax.ShapeDtypeStruct((seqs, chips, rows, pair), BF),
            jax.ShapeDtypeStruct(
                (2, down.shape[0] >> halvings_of(down.shape[0], stages), down.shape[1]), BF
            ),
        ],
        in_specs=[vmem, vmem, anywhere, anywhere, anywhere],
        out_specs=[vmem, vmem, anywhere, anywhere],
        scratch_shapes=[
            pltpu.VMEM((2, ring, pair, rows), BF),
            pltpu.VMEM((pair, length), BF),
            pltpu.VMEM((length, pair), BF),
            pltpu.VMEM((length, pair), F32),
            pltpu.VMEM((length, lanes), F32),
            pltpu.VMEM((length, lanes), BF),
            pltpu.VMEM((pair, lanes), BF),
            pltpu.VMEM((pair, lanes), BF),
            pltpu.VMEM((most, width, rows), BF),
            pltpu.VMEM((most, width, rows), BF),
            pltpu.VMEM((most, width, rows), BF),
            pltpu.VMEM((most, width, rows), BF),
            pltpu.VMEM((2, chips, 2, rows, pair), BF),
            pltpu.VMEM((seqs, chips, rows, pair), BF),
            dma((2,)),
            dma((seqs,)),
            dma((2, most)),
            dma((2, most)),
            dma((2, most)),
            dma((2, most)),
            dma((seqs,)),
            dma((seqs,)),
            dma((seqs, chips)),
            dma((seqs, chips)),
            pltpu.VMEM((down.shape[0] // 2, down.shape[1]), BF),
            pltpu.VMEM((up.shape[0] // 2, up.shape[1]), BF),
            pltpu.VMEM((exchange_rows(down.shape[0], stages), down.shape[1]), BF),
            pltpu.VMEM((exchange_rows(up.shape[0], stages), up.shape[1]), BF),
            pltpu.VMEM((HEAD_DIM, lanes), BF),
            dma((4, stages)),
            dma((4, stages)),
            dma((4,)),
            dma((4,)),
        ],
        compiler_params=pltpu.CompilerParams(
            collective_id=2, has_side_effects=True, vmem_limit_bytes=60 * 2**20
        ),
        cost_estimate=pl.CostEstimate(
            flops=12 * tiles * rows * width * length * 4,
            bytes_accessed=8 * q.size,
            transcendentals=tiles * lanes * length // 2,
        ),
        name="attention",
    )(q, g, kv_all, down, up)


def bit_orders(dp, ring):
    seq_bits = [("seq", 1 << b) for b in range(ring.bit_length() - 1)]
    dp_bits = [("dp", 1 << b) for b in range(dp.bit_length() - 1)]
    far = seq_bits[2:]
    return (seq_bits[:2] + dp_bits + far, seq_bits[:1] + dp_bits + seq_bits[1:2] + far)

def side_of(bit):
    axis, weight = bit
    return lax.rem(lax.axis_index(axis) // weight, 2)

def partner_of(bit):
    axis, weight = bit
    me = lax.axis_index(axis)
    return {axis: me + weight - 2 * weight * side_of(bit)}

def add_rows(dst, a, b, dst_at, a_at, rows):
    step = next(n for n in (128, 96, 64, 48, 32, 16) if rows % n == 0)

    def body(i, carry):
        r = pl.multiple_of(i * step, step)
        dst[pl.ds(dst_at + r, step), :] = a[pl.ds(a_at + r, step), :] + b[pl.ds(r, step), :]
        return carry

    lax.fori_loop(0, rows // step, body, 0)


def sum_kernel(orders, spans, x_ref, out_ref, *scratch):
    parts = [(order, i, span) for span in spans for i, order in enumerate(orders)]
    count = len(parts)
    stages = len(orders[0])
    wide = x_ref.shape[1] // len(orders)
    acc, recv = scratch[:count], scratch[count : 2 * count]
    send_sem, recv_sem = scratch[2 * count :]
    barrier = pltpu.get_barrier_semaphore()
    for bit in orders[0]:
        pl.semaphore_signal(barrier, inc=1, device_id=partner_of(bit), device_id_type=MESH)
    pl.semaphore_wait(barrier, stages)

    def copy(p, s, src, dst, bit):
        return pltpu.make_async_remote_copy(
            src_ref=src,
            dst_ref=dst,
            send_sem=send_sem.at[p, s],
            recv_sem=recv_sem.at[p, s],
            device_id=partner_of(bit),
            device_id_type=MESH,
        )

    start = [0] * count
    place = [0] * count
    live = {}

    def size(p, s):
        return parts[p][2][1] // 2 ** min(s + 1, stages - 1)

    def base(p, s):
        return sum(size(p, t) for t in range(s))

    def view(ref, p):
        _, i, (first, rows) = parts[p]
        return ref.at[pl.ds(first, rows), pl.ds(i * wide, wide)]

    def launch(p, s):
        bit = parts[p][0][s]
        half = size(p, s)
        if s < stages - 1:
            other = pl.multiple_of(start[p] + (1 - side_of(bit)) * half, half)
            src = (view(x_ref, p) if s == 0 else acc[p]).at[pl.ds(other, half), :]
        else:
            src = acc[p].at[pl.ds(pl.multiple_of(start[p], half), half), :]
        live[p] = copy(p, s, src, recv[p].at[pl.ds(base(p, s), half), :], bit)
        live[p].start()

    for p in range(count):
        launch(p, 0)
    for s in range(stages):
        for p in range(count):
            side = side_of(parts[p][0][s])
            live[p].wait()
            half = size(p, s)
            got = recv[p].at[pl.ds(base(p, s), half), :]
            if s == 0:
                place[p] = side * half
                add_rows(acc[p], view(x_ref, p), got, 0, pl.multiple_of(side * half, half), half)
            elif s < stages - 1:
                mine = pl.multiple_of(start[p] + side * half, half)
                add_rows(acc[p], acc[p], got, mine, mine, half)
                place[p] = place[p] + side * half
                start[p] = start[p] + side * half
            else:
                at = pl.multiple_of(start[p], half)
                add_rows(view(out_ref, p), acc[p], got, pl.multiple_of(place[p], half), at, half)
            if s < stages - 1:
                launch(p, s + 1)

    def spread(p, s):
        half = size(p, s)
        src = view(out_ref, p).at[pl.ds(pl.multiple_of(place[p], half), half), :]
        live[p] = copy(p, 2 * stages - 2 - s, src, src, parts[p][0][s])
        live[p].start()

    for p in range(count):
        spread(p, stages - 2)
    for s in range(stages - 2, -1, -1):
        for p in range(count):
            live[p].wait()
            place[p] = place[p] - side_of(parts[p][0][s]) * size(p, s)
            if s:
                spread(p, s - 1)


def total_of(x, dp, ring, collective_id):
    orders = bit_orders(dp, ring)
    rows, cols = x.shape
    stages = len(orders[0])
    unit = 16 << (stages - 1)
    first = -(-rows // unit // 2) * unit
    spans = [(0, first), (first, rows - first)]
    wide = cols // len(orders)
    heights = [span[1] for span in spans for _ in orders]
    whole = pl.BlockSpec(memory_space=pltpu.VMEM)
    return pl.pallas_call(
        functools.partial(sum_kernel, orders, spans),
        out_shape=jax.ShapeDtypeStruct(x.shape, BF),
        in_specs=[whole],
        out_specs=whole,
        scratch_shapes=[pltpu.VMEM((h // 2, wide), BF) for h in heights]
        + [
            pltpu.VMEM((sum(h // 2 ** min(s + 1, stages - 1) for s in range(stages)), wide), BF)
            for h in heights
        ]
        + [pltpu.SemaphoreType.DMA((len(heights), 2 * stages - 1))] * 2,
        compiler_params=pltpu.CompilerParams(
            collective_id=collective_id, has_side_effects=True, vmem_limit_bytes=40 * 2**20
        ),
        name="total",
    )(x)


def normal(h):
    center = h - jnp.mean(h, axis=-1, keepdims=True)
    spread = jnp.mean(center * center, axis=-1, keepdims=True)
    inverse = lax.rsqrt(spread + 1e-05)
    return center * inverse, inverse


def norm_gradient(q, gain, n, inverse):
    scaled = q * gain
    inner = jnp.mean(scaled * n, axis=-1, keepdims=True)
    return inverse * (scaled - jnp.mean(scaled, axis=-1, keepdims=True) - n * inner)


def turned_back(rows, cosine, sine):
    half = cosine.shape[0]
    first, second = rows[:half], rows[half : 2 * half]
    return jnp.concatenate(
        [first * cosine + second * sine, second * cosine - first * sine, rows[2 * half :]], axis=0
    )


def finish_kernel(
    att_ref,
    dq_ref,
    slot_ref,
    cos_ref,
    sin_ref,
    h_ref,
    c_ref,
    ff_ref,
    gm_ref,
    norms_ref,
    weight_ref,
    out_weight_ref,
    up_bias_ref,
    layer_ref,
    input_ref,
    rest_ref,
    raw_ref,
    acc_ref,
    lines_ref,
):
    step = pl.program_id(0)
    d = h_ref.shape[1]
    rows = h_ref.shape[0]
    wide = weight_ref.shape[1]

    @pl.when(step == 0)
    def _():
        acc_ref[...] = jnp.zeros_like(acc_ref)
        lines_ref[...] = jnp.zeros_like(lines_ref)
        for i in range(up_bias_ref.shape[1] // d):
            lines_ref[8 + i : 9 + i, :] = up_bias_ref[:, i * d : (i + 1) * d]

    hidden = h_ref[...].astype(F32)
    low_c = c_ref[...]
    cot = low_c.astype(F32)
    n, inverse = normal(hidden)
    gain1, bias1 = norms_ref[0:1, :], norms_ref[1:2, :]
    gain2, bias_out = norms_ref[2:3, :], norms_ref[3:4, :]
    normed = (n * gain1 + bias1).astype(BF)
    att = att_ref[0]
    layer_ref[...] = hidden + dot(att, out_weight_ref[...], 0, 0) + ff_ref[...] + bias_out
    acc_ref[wide : wide + d, :] += dot(att, low_c, 1, 0)
    cosine, sine = cos_ref[0], sin_ref[0]
    for h in range(d // HEAD_DIM):
        at = slice(h * HEAD_DIM, (h + 1) * HEAD_DIM)
        raw_ref[at, :] = turned_back(dq_ref[0, at, :].astype(F32), cosine, sine).astype(BF)
    kv = slot_ref[0, 0].astype(F32)
    for m in range(1, slot_ref.shape[1]):
        kv = kv + slot_ref[0, m].astype(F32)
    lane = lax.broadcasted_iota(jnp.int32, (1, 2 * HEAD_DIM), 1)
    kv = (kv * jnp.where(lane < HEAD_DIM, 1.0 / LOG2E, 1.0)).astype(BF).astype(F32).T
    raw_ref[d : d + HEAD_DIM, :] = turned_back(kv[:HEAD_DIM], cosine, sine).astype(BF)
    raw_ref[d + HEAD_DIM :, :] = kv[HEAD_DIM:].astype(BF)
    raw = raw_ref[...]
    acc_ref[0:wide, :] += dot(raw, normed, 1, 0)
    sums = dot(jnp.ones((8, rows), BF), raw, 1, 1)
    lines_ref[4:5, :] += sums[0:1, :d]
    lines_ref[5:6, 0 : wide - d] += sums[0:1, d:]
    ga = dot(raw, weight_ref[...], 0, 1)
    gm = gm_ref[...]
    lines_ref[0:1, :] += jnp.sum(ga * n, axis=0, keepdims=True)
    lines_ref[1:2, :] += jnp.sum(ga, axis=0, keepdims=True)
    lines_ref[2:3, :] += jnp.sum(gm * n, axis=0, keepdims=True)
    lines_ref[3:4, :] += jnp.sum(gm, axis=0, keepdims=True)
    lines_ref[6:7, :] += jnp.sum(cot, axis=0, keepdims=True)
    input_ref[...] = (
        cot + norm_gradient(ga, gain1, n, inverse) + norm_gradient(gm, gain2, n, inverse)
    )

    @pl.when(step == pl.num_programs(0) - 1)
    def _():
        rest_ref[0:d, :] = acc_ref[0:d, :].T.astype(BF)
        rest_ref[d : 2 * d, :] = acc_ref[wide : wide + d, :].astype(BF)
        rest_ref[2 * d : d + wide, :] = acc_ref[d:wide, :].astype(BF)
        rest_ref[d + wide : d + wide + 16, :] = lines_ref[...].astype(BF)
        rest_ref[d + wide + 16 :, :] = jnp.zeros((rest_ref.shape[0] - d - wide - 16, d), BF)


def finish(att, dq, slots, cosine, sine, hidden, cot, ff, gm, norms, weight, out_weight, up_bias, padded):
    seqs, d, rows = att.shape
    wide = weight.shape[1]
    by_seq = pl.BlockSpec((1, d, rows), lambda i: (i, 0, 0))
    angle = pl.BlockSpec((1,) + cosine.shape[1:], lambda i: (i, 0, 0))
    by_row = pl.BlockSpec((rows, d), lambda i: (i, 0))

    def all_of(a):
        return pl.BlockSpec(a.shape, lambda i: (0,) * a.ndim)

    return pl.pallas_call(
        finish_kernel,
        grid=(seqs,),
        out_shape=[
            jax.ShapeDtypeStruct(hidden.shape, F32),
            jax.ShapeDtypeStruct(hidden.shape, F32),
            jax.ShapeDtypeStruct((padded, d), BF),
        ],
        in_specs=[
            by_seq,
            by_seq,
            pl.BlockSpec((1,) + slots.shape[1:], lambda i: (i, 0, 0, 0)),
            angle,
            angle,
            by_row,
            by_row,
            by_row,
            by_row,
            all_of(norms),
            all_of(weight),
            all_of(out_weight),
            all_of(up_bias),
        ],
        out_specs=[by_row, by_row, pl.BlockSpec((padded, d), lambda i: (0, 0))],
        scratch_shapes=[
            pltpu.VMEM((wide, rows), BF),
            pltpu.VMEM((wide + d, d), F32),
            pltpu.VMEM((16, d), F32),
        ],
        compiler_params=pltpu.CompilerParams(vmem_limit_bytes=48 * 2**20),
        cost_estimate=pl.CostEstimate(
            flops=12 * seqs * rows * d * d, bytes_accessed=26 * seqs * rows * d, transcendentals=0
        ),
        name="finish",
    )(att, dq, slots, cosine, sine, hidden, cot, ff, gm, norms, weight, out_weight, up_bias)


def local(
    hidden_in,
    positions,
    ln1_gain,
    ln1_bias,
    ln2_gain,
    ln2_bias,
    query_projection,
    query_bias,
    shared_key_weight,
    shared_key_bias,
    shared_value_weight,
    shared_value_bias,
    output_weight,
    output_bias,
    up_weight,
    up_bias,
    down_weight,
    down_bias,
    cotangent,
):
    seq_count, local_len = hidden_in.shape[0], hidden_in.shape[1]
    ring = lax.axis_size("seq")
    groups = ring // seq_count
    per_group = HEADS // groups
    width = per_group * HEAD_DIM
    hidden = hidden_in.astype(F32)
    cosine, sine = angles_of(positions)
    normed_a = layer_norm(hidden, ln1_gain, ln1_bias).astype(BF)
    normed_m = layer_norm(hidden, ln2_gain, ln2_bias).astype(BF)

    tokens = seq_count * local_len
    kv_weight = jnp.concatenate([shared_key_weight, shared_value_weight], axis=1)
    kv_bias = jnp.concatenate([shared_key_bias, shared_value_bias])
    kv_pre = jnp.einsum("stc,cw->swt", normed_a, kv_weight, preferred_element_type=F32)
    kv_pre = kv_pre + kv_bias[:, None]
    kv_low = jnp.concatenate(
        [rotary_rows(kv_pre[:, :HEAD_DIM], cosine, sine), kv_pre[:, HEAD_DIM:]], axis=1
    ).astype(BF)
    kv_all = lax.all_gather(kv_low.reshape(-1, local_len), "seq")
    query_pre = jnp.einsum("stc,cw->swt", normed_a, query_projection, preferred_element_type=F32)
    query_pre = (query_pre + query_bias[:, None]).reshape(seq_count, HEADS, HEAD_DIM, local_len)
    query_low = (rotary_rows(query_pre, cosine[:, None], sine[:, None]) * (LOG2E / 8.0)).astype(BF)
    query_tiles = query_low.reshape(-1, width, local_len)
    grad_attended = jnp.einsum(
        "stc,wc->swt", cotangent, output_weight, preferred_element_type=F32
    ).astype(BF)
    grad_tiles = grad_attended.reshape(-1, width, local_len)

    feedforward, grad_normed_m, grad_w_up, grad_w_down, grad_b_up = feed_forward(
        normed_m.reshape(tokens, D),
        cotangent.reshape(tokens, D),
        up_weight,
        up_bias[None],
        down_weight,
    )
    query_tiles, grad_tiles, kv_all, grad_w_up, grad_w_down = lax.optimization_barrier(
        (query_tiles, grad_tiles, kv_all, grad_w_up, grad_w_down)
    )
    dp = lax.axis_size("dp")
    orders = bit_orders(dp, ring)
    out, dq, dkv, parts = attention(
        query_tiles, grad_tiles, kv_all, grad_w_down, grad_w_up, seq_count, dp
    )
    grad_w_down, grad_w_up = unpack(
        parts, down_weight.shape, up_weight.shape, orders, dp, ring
    )
    qkv = D + 2 * HEAD_DIM
    ff = up_weight.shape[1]
    unit = 16 * dp * ring // 2
    padded = -(-(D + qkv + 16) // unit) * unit
    norms = jnp.concatenate(
        [ln1_gain[None], ln1_bias[None], ln2_gain[None], (output_bias + down_bias)[None]]
        + [jnp.zeros((4, D), F32)],
        axis=0,
    )
    layer_out, input_grad, rest = finish(
        out.reshape(seq_count, D, local_len),
        dq.reshape(seq_count, D, local_len),
        dkv,
        cosine,
        sine,
        hidden_in.reshape(tokens, D),
        cotangent.reshape(tokens, D),
        feedforward,
        grad_normed_m,
        norms,
        jnp.concatenate([query_projection, kv_weight], axis=1),
        output_weight,
        grad_b_up,
        padded,
    )
    rest = total_of(rest, dp, ring, 3)
    kv_rows = rest[2 * D : D + qkv].astype(F32)
    lines = rest[D + qkv : D + qkv + 16].astype(F32)
    return (
        layer_out.reshape(hidden.shape),
        input_grad.reshape(hidden.shape),
        lines[0],
        lines[1],
        lines[2],
        lines[3],
        rest[:D].astype(F32),
        lines[4],
        kv_rows[:HEAD_DIM].T,
        lines[5, :HEAD_DIM],
        kv_rows[HEAD_DIM:].T,
        lines[5, HEAD_DIM : 2 * HEAD_DIM],
        rest[D : 2 * D].astype(F32),
        lines[6],
        grad_w_up,
        lines[8 : 8 + ff // D].reshape(ff),
        grad_w_down,
        lines[6],
    )


def solution(mesh):
    rows = P("dp", "seq", None)
    placed = (rows, P("dp", "seq")) + (P(),) * 16 + (rows,)
    return jax.shard_map(
        local,
        mesh=mesh,
        in_specs=placed,
        out_specs=(rows, rows) + (P(),) * 16,
        check_vma=False,
    )
```
